32 devices in a mesh: pipe: 4 (over z), group: 4 (over y, core), dp: 2 (over x).
Axes of the slice: x: 2, y: 2, z: 4, core: 2. Of those that a mesh axis runs over, the one named last changes fastest.
Arguments:
- tokens: bfloat16 [16384, 768], P(('group', 'dp')), may hold values from -6 to 6
- doc_ids: int32 [16384], P(('group', 'dp')), may hold values from 0 to 7, as said below
- cotangent: bfloat16 [16384, 768], P(('group', 'dp')), may hold values from -6 to 6
- w_qkv: bfloat16 [4, 768, 2304], P('pipe'), may hold values from -0.21875 to 0.21875
- w_out: bfloat16 [4, 768, 768], P('pipe'), may hold values from -2.5 to 2.5
- w_up: bfloat16 [4, 768, 3072], P('pipe'), may hold values from -0.21875 to 0.21875
- w_down: bfloat16 [4, 3072, 768], P('pipe'), may hold values from -0.109375 to 0.109375
- first_gain: float32 [4, 768], P('pipe'), may hold values from 0.5 to 1.5
- first_bias: float32 [4, 768], P('pipe'), may hold values from -2 to 2
- second_gain: float32 [4, 768], P('pipe'), may hold values from 0.5 to 1.5
- second_bias: float32 [4, 768], P('pipe'), may hold values from -2 to 2
Outputs:
- block_out: bfloat16 [4, 16384, 768], P('pipe', ('group', 'dp'))
- input_grad: bfloat16 [4, 16384, 768], P('pipe', ('group', 'dp'))
- grad_w_qkv: float32 [4, 768, 2304], P('pipe', None, 'group')
- grad_w_out: float32 [4, 768, 768], P('pipe', None, 'group')
- grad_w_up: float32 [4, 768, 3072], P('pipe', None, 'group')
- grad_w_down: float32 [4, 3072, 768], P('pipe', 'group')
- grad_first_gain: float32 [4, 768], P('pipe', 'group')
- grad_first_bias: float32 [4, 768], P('pipe', 'group')
- grad_second_gain: float32 [4, 768], P('pipe', 'group')
- grad_second_bias: float32 [4, 768], P('pipe', 'group')
The draws below stay inside these ranges and needn't reach their ends.
Inputs may be any that keep to these rules, and one draw needn't show every extreme that they name: `doc_ids`: within the m-th aligned block of 1024 rows of a replica (m from 0) the ids do not fall, begin at 4 * m and lie in 4 * m to 4 * m + 3; all documents of a block have one length, 1024, 512 or 256 rows; some replica has one document in its first block and four in its last.
All inputs are finite; a program needn't handle non-finite values.
Results may differ from the reference program's by a relative error of at most 0.017.
Values may be sent and summed in bfloat16 or wider, within the bound.
No kernel may reach another device: no remote copies, remote signals or barrier semaphores. Data moves between devices by JAX's collectives and lax.ppermute only.
A program may use at most 384 MiB of HBM per device.

```python
import math
import jax
import jax.numpy as jnp
from jax import lax

D = 768
HEADS = 12
FF = 3072
MB_ROWS = 1024
MICRO = 2
TOKENS = 16384
LAYERS = 4


def draw_doc_ids(key, part):
    key = jax.random.fold_in(key, 17)
    blocks = TOKENS // MB_ROWS
    kind_key, pick_key = jax.random.split(key)
    doc_kind = jax.random.randint(kind_key, (blocks,), 0, 3)
    chosen = jax.random.randint(pick_key, (), 0, blocks // MICRO)
    doc_kind = doc_kind.at[chosen * MICRO].set(0)
    doc_kind = doc_kind.at[chosen * MICRO + MICRO - 1].set(2)
    pieces_per = jnp.where(doc_kind == 0, 1, jnp.where(doc_kind == 1, 2, 4)).astype(jnp.int32)
    row_index = jnp.arange(MB_ROWS, dtype=jnp.int32)
    within = row_index[None, :] * pieces_per[:, None] // MB_ROWS
    block_slot = jnp.arange(blocks, dtype=jnp.int32) % MICRO
    doc_numbers = block_slot[:, None] * 4 + within
    return doc_numbers.reshape(TOKENS).astype(jnp.int32)


def block_levels(rng, extent, cuts, low, top_value):
    factor_of, own = 1.0, jax.random.fold_in(rng, 6)
    for dim, shards_of in cuts:
        steps = jnp.exp(jax.random.uniform(jax.random.fold_in(own, dim), (shards_of,), jnp.float32, low / len(cuts), top_value / len(cuts)))
        factor_of = factor_of * jnp.repeat(steps, extent[dim] // shards_of).reshape([-1 if axis == dim else 1 for axis in range(len(extent))])
    return factor_of


def scatter_about(own_key, shape, scale, reach, cuts=(), held_as=jnp.bfloat16):
    array = scale * jax.random.normal(own_key, shape, jnp.float32)
    if cuts:
        array = array * block_levels(own_key, shape, cuts, -0.22, 0.18)
    return jnp.clip(array, -reach, reach).astype(held_as)


def setup_inputs(seed: int = 0) -> dict:
    arg_keys = jax.random.split(jax.random.key(seed), 12)
    return {
        "tokens": scatter_about(arg_keys[0], (TOKENS, D), 1.0, 6.0, ((0, 8),)),
        "doc_ids": draw_doc_ids(jax.random.fold_in(arg_keys[11], 71), 0),
        "cotangent": scatter_about(arg_keys[2], (TOKENS, D), 1.0, 6.0, ((0, 8),)),
        "w_qkv": scatter_about(arg_keys[3], (LAYERS, D, 3 * D), D ** -0.5, 0.21875, ((0, 4),)),
        "w_out": scatter_about(arg_keys[4], (LAYERS, D, D), (max(D // 128, 1)) ** -0.5, 2.5, ((0, 4),)),
        "w_up": scatter_about(arg_keys[5], (LAYERS, D, FF), D ** -0.5, 0.21875, ((0, 4),)),
        "w_down": scatter_about(arg_keys[6], (LAYERS, FF, D), FF ** -0.5, 0.109375, ((0, 4),)),
        "first_gain": jnp.clip(1.0 + 0.1 * jax.random.normal(arg_keys[7], (LAYERS, D), jnp.float32), 0.5, 1.5),
        "first_bias": scatter_about(arg_keys[8], (LAYERS, D), 0.3, 2.0, ((0, 4),), jnp.float32),
        "second_gain": jnp.clip(1.0 + 0.1 * jax.random.normal(arg_keys[9], (LAYERS, D), jnp.float32), 0.5, 1.5),
        "second_bias": scatter_about(arg_keys[10], (LAYERS, D), 0.3, 2.0, ((0, 4),), jnp.float32),
    }


@jax.custom_vjp
def low(v):
    return lax.optimization_barrier(v.astype(jnp.bfloat16)).astype(jnp.float32)

@jax.custom_vjp
def low_back(v):
    return v

def low_keep(v):
    return (low(v), None)

def low_pass(kept, grad):
    return (grad,)

def back_keep(v):
    return (v, None)

def back_low(kept, grad):
    return (low(grad),)
low.defvjp(low_keep, low_pass)
low_back.defvjp(back_keep, back_low)
highest = lax.Precision.HIGHEST
norm_eps = 1e-05

def layer_norm(inputs, norm_gain, norm_bias):
    centre = lax.optimization_barrier(jnp.mean(inputs, axis=-1, keepdims=True))
    centred = inputs - centre
    spread = lax.optimization_barrier(jnp.mean(centred * centred, axis=-1, keepdims=True))
    return centred * lax.rsqrt(spread + norm_eps) * norm_gain + norm_bias

def doc_geometry(doc_row):
    row_count = doc_row.shape[0]
    same_doc = doc_row[:, None] == doc_row[None, :]
    row_order = jnp.arange(row_count, dtype=jnp.int32)
    earlier = row_order[None, :] <= row_order[:, None]
    causal = jnp.where(same_doc & earlier, 1.0, 0.0).astype(jnp.float32)
    position = lax.optimization_barrier(jnp.sum(causal, axis=1)) - 1.0
    doc_length = lax.optimization_barrier(jnp.sum(jnp.where(same_doc, 1.0, 0.0).astype(jnp.float32), axis=1))
    phase_angle = 0.5 * math.pi * position / doc_length
    return (causal, jnp.cos(phase_angle)[:, None, None], jnp.sin(phase_angle)[:, None, None])

def feature_map(raw_part, cos_part, sin_part):
    positive = jax.nn.softplus(raw_part.reshape(raw_part.shape[0], HEADS, -1))
    return jnp.concatenate([positive * cos_part, positive * sin_part], axis=2)

def head_attention(causal, query_feat, key_feat, value_head):
    scores = jnp.dot(query_feat, key_feat.T, precision=highest)
    masked = low_back(scores * causal)
    denominator = lax.optimization_barrier(jnp.sum(masked, axis=1, keepdims=True))
    shares = low(masked / denominator)
    return jnp.dot(shares, value_head, precision=highest)

def layer_apply(state, geometry, weights):
    causal, cos_part, sin_part = geometry
    w_qkv, w_out, w_up, w_down, gain_one, bias_one, gain_two, bias_two = weights
    width = state.shape[1]
    row_count = state.shape[0]
    mixed = low_back(jnp.dot(state, w_qkv, precision=highest))
    query_feat = low(feature_map(mixed[:, :width], cos_part, sin_part))
    key_feat = low(feature_map(mixed[:, width:2 * width], cos_part, sin_part))
    value_heads = low(mixed[:, 2 * width:].reshape(row_count, HEADS, -1))
    attend = jax.checkpoint(head_attention)
    heads_out = lax.map(lambda items: attend(causal, items[0], items[1], items[2]), (jnp.swapaxes(query_feat, 0, 1), jnp.swapaxes(key_feat, 0, 1), jnp.swapaxes(value_heads, 0, 1)))
    attended = low_back(low(jnp.swapaxes(heads_out, 0, 1).reshape(row_count, width)))
    residual = state + low_back(jnp.dot(attended, w_out, precision=highest))
    hidden = layer_norm(residual, gain_one, bias_one)
    upper = low_back(jnp.dot(low(hidden), w_up, precision=highest))
    active = low(jax.nn.gelu(upper, approximate=False))
    residual_two = hidden + low_back(jnp.dot(active, w_down, precision=highest))
    return layer_norm(residual_two, gain_two, bias_two)

def block_grads(token_block, doc_block, cot_block, params):
    geometry = doc_geometry(doc_block)

    def forward(start, extras, weight_set):
        state = low_back(start)
        sent_all = []
        sent_value = start
        for depth in range(LAYERS):
            if depth > 0:
                state = low_back(sent_value + extras[depth - 1])
            output = layer_apply(state, geometry, tuple((weight_item[depth] for weight_item in weight_set)))
            sent_value = low(output)
            sent_all.append(sent_value)
        return (sent_value, jnp.stack(sent_all))
    extras = jnp.zeros((LAYERS - 1, MB_ROWS, D), jnp.float32)
    last_out, pullback, sent_stack = jax.vjp(forward, token_block, extras, params, has_aux=True)
    grad_start, grad_extras, grad_params = pullback(cot_block)
    ins_stack = jnp.concatenate([grad_start[None], grad_extras], axis=0)
    return (sent_stack, ins_stack, grad_params)

def reference(tokens, doc_ids, cotangent, w_qkv, w_out, w_up, w_down, first_gain, first_bias, second_gain, second_bias):
    params = tuple((weight_item.astype(jnp.float32) for weight_item in (w_qkv, w_out, w_up, w_down, first_gain, first_bias, second_gain, second_bias)))
    blocks = TOKENS // MB_ROWS
    token_blocks = tokens.astype(jnp.float32).reshape(blocks, MB_ROWS, D)
    doc_blocks = doc_ids.reshape(blocks, MB_ROWS)
    cot_blocks = cotangent.astype(jnp.float32).reshape(blocks, MB_ROWS, D)

    def step(totals, items):
        sent_stack, ins_stack, grad_params = block_grads(items[0], items[1], items[2], params)
        totals = tuple((left + right for left, right in zip(totals, grad_params)))
        return (totals, (sent_stack, ins_stack))
    zeros_init = tuple((jnp.zeros_like(weight_item) for weight_item in params))
    totals, (outs_all, ins_all) = lax.scan(step, zeros_init, (token_blocks, doc_blocks, cot_blocks))
    block_out = jnp.swapaxes(outs_all, 0, 1).reshape(LAYERS, TOKENS, D).astype(jnp.bfloat16)
    input_grad = jnp.swapaxes(ins_all, 0, 1).reshape(LAYERS, TOKENS, D).astype(jnp.bfloat16)
    return (block_out, input_grad, totals[0], totals[1], totals[2], totals[3], totals[4], totals[5], totals[6], totals[7])
```

```python
import functools, math
import jax, jax.numpy as jnp
from jax import lax
from jax.experimental import pallas as pl
from jax.experimental.pallas import tpu as pltpu
from jax.sharding import PartitionSpec as P

bf = jnp.bfloat16
f32 = jnp.float32
EPS = 1e-05
D = 768
PAIRS = 6
NT = (((1,), (1,)), ((), ()))
TN = (((0,), (0,)), ((), ()))


def nn_dot(a, b):
    return jnp.dot(a, b, preferred_element_type=f32)


def nt_dot(a, b):
    return lax.dot_general(a, b, NT, preferred_element_type=f32)


def tn_dot(a, b):
    return lax.dot_general(a, b, TN, preferred_element_type=f32)


def head_lanes(rows, lanes):
    lane = lax.broadcasted_iota(jnp.int32, (rows, lanes), 1)
    return (lane & 64) == 0


def block_diag(size):
    r = lax.broadcasted_iota(jnp.int32, (size, size), 0)
    c = lax.broadcasted_iota(jnp.int32, (size, size), 1)
    return ((r ^ c) & 64) == 0


def soft_pair(raw):
    e = jnp.exp(-jnp.abs(raw))
    one = 1.0 + e
    tail = jnp.where(e < 1e-3, e * (1.0 - e * (0.5 - e * (1.0 / 3.0))), jnp.log(one))
    soft = jnp.maximum(raw, 0.0) + tail
    sig = jnp.where(raw >= 0.0, 1.0, e) / one
    return soft, sig


def norm_rows(v):
    centre = jnp.mean(v, axis=-1, keepdims=True)
    centred = v - centre
    spread = jnp.mean(centred * centred, axis=-1, keepdims=True)
    rstd = lax.rsqrt(spread + EPS)
    return centred * rstd, rstd


class Sender:
    def __init__(self, sems):
        self.sems, self.copies = sems, []

    def put(self, src, dst):
        copy = pltpu.make_async_copy(src, dst, self.sems.at[len(self.copies)])
        copy.start()
        self.copies.append(copy)

    def finish(self):
        for copy in self.copies:
            copy.wait()


def forward_kernel(delta, n, rows,
                   t_ref, meta_ref, tok_ref, arr_ref, cos_ref, sin_ref,
                   wq_ref, wo_ref, wu_ref, wd_ref, gb_ref, s_in, all_in,
                   y_ref, x_o, att_o, hb_o, act_o, qn_o, kf_o, v_o, sg_o, n1_o, gp_o, n2_o, rs_o, sb_o, s_out, all_out,
                   x_ref, att_ref, hb_ref, act_ref, qn_ref, kf_ref, v_ref, sg_ref, n1_ref, gp_ref, n2_ref, rs_ref, sb_ref, sems):
    stage = meta_ref[0]
    chunk = t_ref[0] - delta * stage
    valid = (chunk >= 0) & (chunk < n)

    @pl.when(valid)
    def _():
        send = Sender(sems)
        base = pl.multiple_of(chunk * rows, rows)
        first = meta_ref[1 + chunk] != 0

        @pl.when(stage == 0)
        def _():
            x_ref[...] = tok_ref[pl.ds(base, rows), :]

        @pl.when(stage != 0)
        def _():
            x_ref[...] = arr_ref[...]

        @pl.when(first)
        def _():
            s_out[...] = jnp.zeros_like(s_out)

        @pl.when(jnp.logical_not(first))
        def _():
            s_out[...] = s_in[...]

        send.put(x_ref, x_o)
        x = x_ref[...]
        cos = cos_ref[pl.ds(base, rows), :]
        sin = sin_ref[pl.ds(base, rows), :]
        q_raw = nn_dot(x, wq_ref[:, 0:D])
        k_raw = nn_dot(x, wq_ref[:, D:2 * D])
        v_ref[...] = nn_dot(x, wq_ref[:, 2 * D:]).astype(bf)
        send.put(v_ref, v_o)
        m_a = head_lanes(rows, 256)
        ri = lax.broadcasted_iota(jnp.int32, (rows, rows), 0)
        ci = lax.broadcasted_iota(jnp.int32, (rows, rows), 1)
        tril = ci <= ri
        diag = block_diag(256)
        ones = jnp.ones((rows, 128), bf)
        zero = jnp.zeros((), bf)
        for p in range(PAIRS):
            lanes = slice(128 * p, 128 * p + 128)
            wide = slice(256 * p, 256 * p + 256)
            q, sq = soft_pair(q_raw[:, lanes])
            k, sk = soft_pair(k_raw[:, lanes])
            qc, qs = q * cos, q * sin
            qf = jnp.concatenate([qc, qs], axis=1).astype(bf)
            kf = jnp.concatenate([k * cos, k * sin], axis=1).astype(bf)
            kf_ref[:, wide] = kf
            sg_ref[:, D + 128 * p:D + 128 * p + 128] = sk.astype(bf)
            ve = jnp.concatenate([v_ref[:, lanes], ones], axis=1)
            s_a = nt_dot(jnp.where(m_a, qf, zero), kf)
            s_b = nt_dot(jnp.where(m_a, zero, qf), kf)
            p_ab = jnp.concatenate([jnp.where(tril, s_a, 0.0), jnp.where(tril, s_b, 0.0)], axis=1).astype(bf)
            ve2 = jnp.concatenate([jnp.where(m_a, ve, zero), jnp.where(m_a, zero, ve)], axis=0)
            before = s_out[p].astype(bf)
            sb_ref[p] = before
            nd = nn_dot(p_ab, ve2) + nn_dot(qf, before)
            inv = 1.0 / nd[:, 128:]
            att_ref[:, lanes] = (nd[:, :128] * inv).astype(bf)
            qn_ref[:, wide] = jnp.concatenate([qc * inv, qs * inv], axis=1).astype(bf)
            sg_ref[:, lanes] = (sq * inv).astype(bf)
            s_out[p] = s_out[p] + jnp.where(diag, tn_dot(kf, ve), 0.0)
        send.put(kf_ref, kf_o)
        send.put(att_ref, att_o)
        send.put(qn_ref, qn_o)
        send.put(sg_ref, sg_o)
        send.put(sb_ref, sb_o)
        residual = x.astype(f32) + nn_dot(att_ref[...], wo_ref[...])
        n1, r1 = norm_rows(residual)
        n1_ref[...] = n1.astype(bf)
        hidden = n1 * gb_ref[0:1, :] + gb_ref[1:2, :]
        hb = hidden.astype(bf)
        hb_ref[...] = hb
        send.put(n1_ref, n1_o)
        send.put(hb_ref, hb_o)
        total = hidden
        FB = 768
        for j in range(0, 4 * D, FB):
            cols = slice(j, j + FB)
            u = nn_dot(hb, wu_ref[:, cols])
            cdf = 0.5 + 0.5 * lax.erf(u * (1.0 / math.sqrt(2.0)))
            act = (u * cdf).astype(bf)
            act_ref[:, cols] = act
            gp_ref[:, cols] = (cdf + u * (jnp.exp(-0.5 * u * u) * (1.0 / math.sqrt(2.0 * math.pi)))).astype(bf)
            total = total + nn_dot(act, wd_ref[cols, :])
        send.put(act_ref, act_o)
        send.put(gp_ref, gp_o)
        n2, r2 = norm_rows(total)
        n2_ref[...] = n2.astype(bf)
        lane = lax.broadcasted_iota(jnp.int32, (rows, 128), 1)
        rs_ref[...] = jnp.where(lane < 64, r1, r2)
        send.put(n2_ref, n2_o)
        send.put(rs_ref, rs_o)
        y_ref[...] = (n2 * gb_ref[2:3, :] + gb_ref[3:4, :]).astype(bf)
        send.put(y_ref, all_out.at[pl.ds(base, rows), :])
        send.finish()


def forward_call(rows, n, delta, limit=28):
    V = pl.BlockSpec(memory_space=pltpu.VMEM)
    S = pl.BlockSpec(memory_space=pltpu.SMEM)
    A = pl.BlockSpec(memory_space=pl.ANY)
    sd = jax.ShapeDtypeStruct
    saved = [((rows, D), bf)] * 3 + [((rows, 4 * D), bf)] + [((rows, 2 * D), bf)] * 2 + [((rows, D), bf), ((rows, 2 * D), bf), ((rows, D), bf), ((rows, 4 * D), bf), ((rows, D), bf), ((rows, 128), f32), ((PAIRS, 256, 256), bf)]
    outs = [sd((rows, D), bf)] + [sd(*item) for item in saved] + [sd((PAIRS, 256, 256), f32), sd((n * rows, D), bf)]
    return pl.pallas_call(
        functools.partial(forward_kernel, delta, n, rows),
        in_specs=[S, S] + [V] * 10 + [A],
        out_specs=[V] + [A] * 13 + [V, A],
        out_shape=outs,
        scratch_shapes=[pltpu.VMEM(*item) for item in saved] + [pltpu.SemaphoreType.DMA((14,))],
        input_output_aliases={11: 14, 12: 15},
        cost_estimate=pl.CostEstimate(flops=rows * 2 * 9 * 10**6, bytes_accessed=4 * 2**20, transcendentals=0),
        compiler_params=pltpu.CompilerParams(vmem_limit_bytes=limit * 2**20),
        name="layer_forward",
    )


def norm_back(grad, normed, rstd, gain):
    scaled = grad * gain
    mean_one = jnp.mean(scaled, axis=-1, keepdims=True)
    mean_two = jnp.mean(scaled * normed, axis=-1, keepdims=True)
    return rstd * (scaled - mean_one - normed * mean_two)


def backward_kernel(delta, n, rows, stages,
                    t_ref, meta_ref, cot_ref, arr_ref, cos_ref, sin_ref,
                    wq_ref, wo_ref, wu_ref, wd_ref, gb_ref,
                    att_ref, qn_ref, kf_ref, v_ref, sg_ref, n1_ref, gp_ref, n2_ref, rs_ref, sb_ref,
                    t_in, ga_in, all_in,
                    ds_ref, df_o, du_o, dp_o, dm_o, t_out, ga_out, all_out,
                    df_ref, du_ref, dp_ref, dm_ref, da_ref, g_ref, sems):
    stage = meta_ref[0]
    chunk = n - 1 - t_ref[0] + delta * (stages - 1 - stage)
    valid = (chunk >= 0) & (chunk < n)

    @pl.when(valid)
    def _():
        send = Sender(sems)
        base = pl.multiple_of(chunk * rows, rows)
        last = meta_ref[1 + n + chunk] != 0

        @pl.when(stage == stages - 1)
        def _():
            g_ref[...] = cot_ref[pl.ds(base, rows), :]

        @pl.when(stage != stages - 1)
        def _():
            g_ref[...] = arr_ref[...]

        @pl.when(last)
        def _():
            t_out[...] = jnp.zeros_like(t_out)

        @pl.when(jnp.logical_not(last))
        def _():
            t_out[...] = t_in[...]

        @pl.when(chunk == n - 1)
        def _():
            ga_out[...] = jnp.zeros_like(ga_out)

        @pl.when(chunk != n - 1)
        def _():
            ga_out[...] = ga_in[...]

        g = g_ref[...].astype(f32)
        n2 = n2_ref[...].astype(f32)
        r1 = rs_ref[:, 0:1]
        r2 = rs_ref[:, 64:65]
        ga_out[2:3, :] += jnp.sum(g * n2, axis=0, keepdims=True)
        ga_out[3:4, :] += jnp.sum(g, axis=0, keepdims=True)
        d_two = norm_back(g, n2, r2, gb_ref[2:3, :])
        df = d_two.astype(bf)
        df_ref[...] = df
        send.put(df_ref, df_o)
        total = d_two
        FB = 768
        for j in range(0, 4 * D, FB):
            cols = slice(j, j + FB)
            du = (nt_dot(df, wd_ref[cols, :]) * gp_ref[:, cols].astype(f32)).astype(bf)
            du_ref[:, cols] = du
            total = total + nt_dot(du, wu_ref[:, cols])
        send.put(du_ref, du_o)
        n1 = n1_ref[...].astype(f32)
        ga_out[0:1, :] += jnp.sum(total * n1, axis=0, keepdims=True)
        ga_out[1:2, :] += jnp.sum(total, axis=0, keepdims=True)
        d_res = norm_back(total, n1, r1, gb_ref[0:1, :])
        dp = d_res.astype(bf)
        dp_ref[...] = dp
        send.put(dp_ref, dp_o)
        da_ref[...] = nt_dot(dp, wo_ref[...]).astype(bf)
        cos = cos_ref[pl.ds(base, rows), :]
        sin = sin_ref[pl.ds(base, rows), :]
        m_a = head_lanes(rows, 256)
        lane = lax.broadcasted_iota(jnp.int32, (rows, 128), 1)
        ri = lax.broadcasted_iota(jnp.int32, (rows, rows), 0)
        ci = lax.broadcasted_iota(jnp.int32, (rows, rows), 1)
        tril = ci <= ri
        triu = ri <= ci
        diag = block_diag(256)
        ones = jnp.ones((rows, 128), bf)
        zero = jnp.zeros((), bf)
        for p in range(PAIRS):
            lanes = slice(128 * p, 128 * p + 128)
            wide = slice(256 * p, 256 * p + 256)
            d_o = da_ref[:, lanes]
            prod = d_o.astype(f32) * att_ref[:, lanes].astype(f32)
            in_a = jnp.sum(jnp.where(lane < 64, prod, 0.0), axis=1, keepdims=True)
            in_b = jnp.sum(jnp.where(lane < 64, 0.0, prod), axis=1, keepdims=True)
            inner = jnp.where(lane < 64, -in_a, -in_b)
            high = inner.astype(bf).astype(f32)
            ext = jnp.where((lane & 63) == 0, high, jnp.where((lane & 63) == 1, inner - high, 0.0)).astype(bf)
            left = jnp.concatenate([d_o, ext], axis=1)
            left_a, left_b = jnp.where(m_a, left, zero), jnp.where(m_a, zero, left)
            ve = jnp.concatenate([v_ref[:, lanes], ones], axis=1)
            qn = qn_ref[:, wide]
            kf = kf_ref[:, wide]
            qn_a, qn_b = jnp.where(m_a, qn, zero), jnp.where(m_a, zero, qn)
            kf_a, kf_b = jnp.where(m_a, kf, zero), jnp.where(m_a, zero, kf)
            pt = jnp.concatenate([jnp.where(triu, nt_dot(kf, qn_a), 0.0), jnp.where(triu, nt_dot(kf, qn_b), 0.0)], axis=1).astype(bf)
            gg = jnp.concatenate([jnp.where(tril, nt_dot(left_a, ve), 0.0), jnp.where(tril, nt_dot(left_b, ve), 0.0)], axis=1).astype(bf)
            gt = jnp.concatenate([jnp.where(triu, nt_dot(ve, left_a), 0.0), jnp.where(triu, nt_dot(ve, left_b), 0.0)], axis=1).astype(bf)
            after = t_out[p].astype(bf)
            dv = nn_dot(pt, jnp.concatenate([left_a[:, :128], left_b[:, :128]], axis=0)) + nn_dot(kf, after[:, :128])
            dq = nn_dot(gg, jnp.concatenate([kf_a, kf_b], axis=0)) + nt_dot(left, sb_ref[p])
            dk = nn_dot(gt, jnp.concatenate([qn_a, qn_b], axis=0)) + nt_dot(ve, after)
            t_out[p] = t_out[p] + jnp.where(diag, tn_dot(qn, left), 0.0)
            sq = sg_ref[:, lanes].astype(f32)
            sk = sg_ref[:, D + 128 * p:D + 128 * p + 128].astype(f32)
            dm_ref[:, lanes] = ((dq[:, :128] * cos + dq[:, 128:] * sin) * sq).astype(bf)
            dm_ref[:, D + 128 * p:D + 128 * p + 128] = ((dk[:, :128] * cos + dk[:, 128:] * sin) * sk).astype(bf)
            dm_ref[:, 2 * D + 128 * p:2 * D + 128 * p + 128] = dv.astype(bf)
        send.put(dm_ref, dm_o)
        ds_ref[...] = (d_res + nt_dot(dm_ref[...], wq_ref[...])).astype(bf)
        send.put(ds_ref, all_out.at[pl.ds(base, rows), :])
        send.finish()


def backward_call(rows, n, delta, stages, limit=28):
    V = pl.BlockSpec(memory_space=pltpu.VMEM)
    S = pl.BlockSpec(memory_space=pltpu.SMEM)
    A = pl.BlockSpec(memory_space=pl.ANY)
    sd = jax.ShapeDtypeStruct
    made = [((rows, D), bf), ((rows, 4 * D), bf), ((rows, D), bf), ((rows, 3 * D), bf)]
    outs = [sd((rows, D), bf)] + [sd(*item) for item in made] + [sd((PAIRS, 256, 256), f32), sd((8, D), f32), sd((n * rows, D), bf)]
    return pl.pallas_call(
        functools.partial(backward_kernel, delta, n, rows, stages),
        in_specs=[S, S] + [V] * 21 + [A],
        out_specs=[V] + [A] * 4 + [V] * 2 + [A],
        out_shape=outs,
        scratch_shapes=[pltpu.VMEM(*item) for item in made] + [pltpu.VMEM((rows, D), bf), pltpu.VMEM((rows, D), bf), pltpu.SemaphoreType.DMA((5,))],
        input_output_aliases={21: 5, 22: 6, 23: 7},
        cost_estimate=pl.CostEstimate(flops=rows * 2 * 10 * 10**6, bytes_accessed=4 * 2**20, transcendentals=0),
        compiler_params=pltpu.CompilerParams(vmem_limit_bytes=limit * 2**20),
        name="layer_backward",
    )


def weight_kernel(delta, n, rows, stages, slots, units,
                  meta_ref, *refs):
    lefts, rights = refs[:slots], refs[slots:2 * slots]
    keep_ref, send_ref, left_buf, right_buf, left_sem, right_sem = refs[2 * slots:]
    step, steps = pl.program_id(0), pl.num_programs(0)
    stage, me = meta_ref[0], meta_ref[1]

    def fetch(tile, slot):
        cols = pl.ds(pl.multiple_of(tile * 384, 128), 384)
        for owner in range(stages):
            @pl.when(stage == owner)
            def _():
                for k in range(n):
                    pltpu.make_async_copy(lefts[delta * owner + k].at[:, cols], left_buf.at[slot, pl.ds(k * rows, rows), :], left_sem.at[slot]).start()

    @pl.when(step == 0)
    def _():
        for owner in range(stages):
            @pl.when(stage == owner)
            def _():
                for k in range(n):
                    pltpu.make_async_copy(rights[delta * owner + k], right_buf.at[pl.ds(k * rows, rows), :], right_sem).start()
        fetch(0, 0)
        pltpu.make_async_copy(right_buf, right_buf, right_sem).wait()

    @pl.when(step + 1 < steps)
    def _():
        fetch(step + 1, (step + 1) & 1)

    slot = step & 1
    pltpu.make_async_copy(left_buf.at[slot], left_buf.at[slot], left_sem.at[slot]).wait()
    value = tn_dot(left_buf[slot], right_buf[...]).astype(bf)
    for half in range(2):
        unit = step * 2 + half
        group = unit // units
        inside = pl.multiple_of((unit - group * units) * 192, 192)
        rel = group ^ me
        part = value[half * 192:half * 192 + 192, :]

        @pl.when((rel & 1) == 0)
        def _():
            keep_ref[rel >> 1, pl.ds(inside, 192), :] = part

        @pl.when((rel & 1) == 1)
        def _():
            send_ref[rel >> 1, pl.ds(inside, 192), :] = part


def weight_call(rows, n, delta, stages, slots, width, groups, limit=40):
    V = pl.BlockSpec(memory_space=pltpu.VMEM)
    S = pl.BlockSpec(memory_space=pltpu.SMEM)
    A = pl.BlockSpec(memory_space=pl.ANY)
    out = jax.ShapeDtypeStruct((2, width // groups, D), bf)
    return pl.pallas_call(
        functools.partial(weight_kernel, delta, n, rows, stages, slots, width // groups // 192),
        grid=(width // 384,),
        in_specs=[S] + [A] * (2 * slots),
        out_specs=[V, V],
        out_shape=[out, out],
        scratch_shapes=[pltpu.VMEM((2, n * rows, 384), bf), pltpu.VMEM((n * rows, D), bf), pltpu.SemaphoreType.DMA((2,)), pltpu.SemaphoreType.DMA],
        cost_estimate=pl.CostEstimate(flops=2 * n * rows * D * width, bytes_accessed=n * rows * (D + width) * 2, transcendentals=0),
        compiler_params=pltpu.CompilerParams(vmem_limit_bytes=limit * 2**20),
        name="weight_grad",
    )


MB_ROWS = 1024
MICRO = 2
ROWS = 256
DELTA = 2


def geometry(doc_ids):
    quarter = MB_ROWS // 4
    marks = doc_ids.reshape(-1, MB_ROWS)[:, ::quarter]
    pieces = 1 + jnp.sum((marks[:, 1:] != marks[:, :-1]).astype(jnp.int32), axis=1)
    length = MB_ROWS // pieces
    row = jnp.arange(MB_ROWS, dtype=jnp.int32)
    position = row[None, :] % length[:, None]
    angle = (0.5 * math.pi) * position.astype(f32) / length[:, None].astype(f32)
    angle = angle.reshape(-1, 1)
    starts = jnp.arange(0, MB_ROWS, ROWS, dtype=jnp.int32)
    first = (starts[None, :] % length[:, None]) == 0
    last = ((starts[None, :] + ROWS) % length[:, None]) == 0
    wide = (angle.shape[0], 128)
    return (jnp.broadcast_to(jnp.cos(angle), wide), jnp.broadcast_to(jnp.sin(angle), wide),
            first.reshape(-1).astype(jnp.int32), last.reshape(-1).astype(jnp.int32))


def exchange(block, axis, flip):
    route = [(i, i ^ flip) for i in range(lax.axis_size(axis))]
    return lax.ppermute(block, axis, route)


def reduced(keep, send):
    half = lax.optimization_barrier((keep.astype(f32) + exchange(send, "group", 1).astype(f32)).astype(bf))
    own = lax.optimization_barrier((half[0].astype(f32) + exchange(half[1], "group", 2).astype(f32)).astype(bf))
    if lax.axis_size("dp") == 2:
        return own.astype(f32) + exchange(own, "dp", 1).astype(f32)
    return lax.psum(own, "dp").astype(f32)


def local(tokens, doc_ids, cotangent, w_qkv, w_out, w_up, w_down,
          first_gain, first_bias, second_gain, second_bias):
    stages = lax.axis_size("pipe")
    groups = lax.axis_size("group")
    stage = lax.axis_index("pipe").astype(jnp.int32)
    me = lax.axis_index("group").astype(jnp.int32)
    n = tokens.shape[0] // ROWS
    ticks = n + DELTA * (stages - 1)
    cos, sin, first, last = geometry(doc_ids)
    meta = jnp.concatenate([stage[None], first, last])
    weights = (w_qkv[0], w_out[0], w_up[0], w_down[0])
    gb = jnp.concatenate([first_gain, first_bias, second_gain, second_bias], axis=0)
    forward = forward_call(ROWS, n, DELTA)
    backward = backward_call(ROWS, n, DELTA, stages)
    blank = jnp.zeros((ROWS, D), bf)
    arriving = [blank] * DELTA
    state = jnp.zeros((PAIRS, 256, 256), f32)
    block_out = jnp.zeros((n * ROWS, D), bf)
    saved = []
    for t in range(ticks):
        made = forward(jnp.full((1,), t, jnp.int32), meta, tokens, arriving.pop(0), cos, sin, *weights, gb, state, block_out)
        state, block_out = made[-2:]
        saved.append(made[1:-2])
        route = [(a, a + 1) for a in range(stages - 1) if 0 <= t - a * DELTA < n]
        arriving.append(lax.ppermute(made[0], "pipe", route) if route else blank)
    arriving = [blank] * DELTA
    state = jnp.zeros((PAIRS, 256, 256), f32)
    sums = jnp.zeros((8, D), f32)
    input_grad = jnp.zeros((n * ROWS, D), bf)
    diffs = [None] * ticks
    for t in range(ticks):
        slot = ticks - 1 - t
        x, att, hb, act, qn, kf, v, sg, n1, gp, n2, rs, sb = saved[slot]
        made = backward(jnp.full((1,), t, jnp.int32), meta, cotangent, arriving.pop(0), cos, sin, *weights, gb,
                        att, qn, kf, v, sg, n1, gp, n2, rs, sb, state, sums, input_grad)
        state, sums, input_grad = made[-3:]
        diffs[slot] = made[1:-3]
        route = [(a, a - 1) for a in range(1, stages) if 0 <= t - (stages - 1 - a) * DELTA < n]
        arriving.append(lax.ppermute(made[0], "pipe", route) if route else blank)
    where = jnp.stack([stage, me])

    def weight(left, right):
        call = weight_call(ROWS, n, DELTA, stages, ticks, left[0].shape[1], groups)
        return reduced(*call(where, *left, *right))

    pick = lambda items, i: [item[i] for item in items]
    g_down = weight(pick(saved, 3), pick(diffs, 0))
    g_up = weight(pick(diffs, 1), pick(saved, 2))
    g_qkv = weight(pick(diffs, 3), pick(saved, 0))
    g_out = weight(pick(diffs, 2), pick(saved, 1))
    total = lax.psum(sums[:4], ("group", "dp"))
    mine = lax.dynamic_slice_in_dim(total, me * (D // groups), D // groups, axis=1)
    return (block_out[None], input_grad[None], g_qkv.T[None], g_out.T[None], g_up.T[None], g_down[None],
            mine[0:1], mine[1:2], mine[2:3], mine[3:4])


def solution(mesh):
    rows = ("group", "dp")
    whole = P("pipe", None, None)
    vector = P("pipe", None)
    return jax.shard_map(
        local,
        mesh=mesh,
        in_specs=(P(rows, None), P(rows), P(rows, None)) + (whole,) * 4 + (vector,) * 4,
        out_specs=(P("pipe", rows, None), P("pipe", rows, None), P("pipe", None, "group"), P("pipe", None, "group"),
                   P("pipe", None, "group"), P("pipe", "group", None)) + (P("pipe", "group"),) * 4,
        check_vma=False,
    )
```

```python
import functools, math
import jax, jax.numpy as jnp
from jax import lax
from jax.experimental import pallas as pl
from jax.experimental.pallas import tpu as pltpu
from jax.sharding import PartitionSpec as P

bf = jnp.bfloat16
f32 = jnp.float32
EPS = 1e-05
D = 768
PAIRS = 6
TILE = 256
TILES = 4 * D // TILE
NT = (((1,), (1,)), ((), ()))
TN = (((0,), (0,)), ((), ()))


def nn_dot(a, b):
    return jnp.dot(a, b, preferred_element_type=f32)


def nt_dot(a, b):
    return lax.dot_general(a, b, NT, preferred_element_type=f32)


def tn_dot(a, b):
    return lax.dot_general(a, b, TN, preferred_element_type=f32)


def head_lanes(rows, lanes):
    lane = lax.broadcasted_iota(jnp.int32, (rows, lanes), 1)
    return (lane & 64) == 0


def block_diag(size):
    r = lax.broadcasted_iota(jnp.int32, (size, size), 0)
    c = lax.broadcasted_iota(jnp.int32, (size, size), 1)
    return ((r ^ c) & 64) == 0


def soft_pair(raw):
    e = jnp.exp(-jnp.abs(raw))
    one = 1.0 + e
    tail = jnp.where(e < 1e-3, e * (1.0 - e * (0.5 - e * (1.0 / 3.0))), jnp.log(one))
    soft = jnp.maximum(raw, 0.0) + tail
    sig = jnp.where(raw >= 0.0, 1.0, e) / one
    return soft, sig


def norm_rows(v):
    centre = jnp.mean(v, axis=-1, keepdims=True)
    centred = v - centre
    spread = jnp.mean(centred * centred, axis=-1, keepdims=True)
    rstd = lax.rsqrt(spread + EPS)
    return centred * rstd, rstd


class Sender:
    def __init__(self, sems):
        self.sems, self.copies = sems, []

    def put(self, src, dst):
        copy = pltpu.make_async_copy(src, dst, self.sems.at[len(self.copies)])
        copy.start()
        self.copies.append(copy)

    def finish(self):
        for copy in self.copies:
            copy.wait()


def forward_kernel(delta, n, rows,
                   t_ref, meta_ref, tok_ref, arr_ref, cos_ref, sin_ref,
                   wq_ref, wo_ref, wu_ref, wd_ref, gb_ref, s_in,
                   y_ref, s_out, all_o, x_o, att_o, hb_o, act_o, qn_o, kf_o, v_o, sg_o, n1_o, gp_o, n2_o, rs_o, sb_o,
                   x_ref, att_ref, hb_ref, act_ref, qn_ref, kf_ref, v_ref, sg_ref, n1_ref, gp_ref, n2_ref, rs_ref, sb_ref, sems, loads=()):
    stage = meta_ref[0]
    chunk = t_ref[0] - delta * stage
    valid = (chunk >= 0) & (chunk < n)

    def loaded(*which):
        for i in which:
            if loads:
                loads[i].wait()

    @pl.when(jnp.logical_not(valid))
    def _():
        loaded(*range(len(loads)))

    @pl.when(valid)
    def _():
        send = Sender(sems)
        base = pl.multiple_of(chunk * rows, rows)
        here = pl.ds(base, rows)
        first = meta_ref[2 + chunk] != 0
        loaded(0)

        @pl.when(stage == 0)
        def _():
            x_ref[...] = tok_ref[pl.ds(base, rows), :]

        @pl.when(stage != 0)
        def _():
            x_ref[...] = arr_ref[...]

        @pl.when(first)
        def _():
            s_out[...] = jnp.zeros_like(s_out)

        if s_in is not None:
            @pl.when(jnp.logical_not(first))
            def _():
                s_out[...] = s_in[...]

        send.put(x_ref, x_o.at[here, :])
        x = x_ref[...]
        cos = cos_ref[pl.ds(base, rows), :]
        sin = sin_ref[pl.ds(base, rows), :]
        loaded(1)
        q_raw = nn_dot(x, wq_ref[:, 0:D])
        k_raw = nn_dot(x, wq_ref[:, D:2 * D])
        v_ref[...] = nn_dot(x, wq_ref[:, 2 * D:]).astype(bf)
        send.put(v_ref, v_o.at[here, :])
        m_a = head_lanes(rows, 256)
        ri = lax.broadcasted_iota(jnp.int32, (rows, rows), 0)
        ci = lax.broadcasted_iota(jnp.int32, (rows, rows), 1)
        tril = ci <= ri
        diag = block_diag(256)
        ones = jnp.ones((rows, 128), bf)
        zero = jnp.zeros((), bf)
        for p in range(PAIRS):
            lanes = slice(128 * p, 128 * p + 128)
            wide = slice(256 * p, 256 * p + 256)
            q, sq = soft_pair(q_raw[:, lanes])
            k, sk = soft_pair(k_raw[:, lanes])
            qc, qs = q * cos, q * sin
            qf = jnp.concatenate([qc, qs], axis=1).astype(bf)
            kf = jnp.concatenate([k * cos, k * sin], axis=1).astype(bf)
            kf_ref[:, wide] = kf
            sg_ref[:, D + 128 * p:D + 128 * p + 128] = sk.astype(bf)
            ve = jnp.concatenate([v_ref[:, lanes], ones], axis=1)
            s_a = nt_dot(jnp.where(m_a, qf, zero), kf)
            s_b = nt_dot(jnp.where(m_a, zero, qf), kf)
            p_ab = jnp.concatenate([jnp.where(tril, s_a, 0.0), jnp.where(tril, s_b, 0.0)], axis=1).astype(bf)
            ve2 = jnp.concatenate([jnp.where(m_a, ve, zero), jnp.where(m_a, zero, ve)], axis=0)
            before = s_out[p].astype(bf)
            sb_ref[p] = before
            nd = nn_dot(p_ab, ve2) + nn_dot(qf, before)
            inv = 1.0 / nd[:, 128:]
            att_ref[:, lanes] = (nd[:, :128] * inv).astype(bf)
            qn_ref[:, wide] = jnp.concatenate([qc * inv, qs * inv], axis=1).astype(bf)
            sg_ref[:, lanes] = (sq * inv).astype(bf)
            s_out[p] = s_out[p] + jnp.where(diag, tn_dot(kf, ve), 0.0)
        send.put(kf_ref, kf_o.at[here, :])
        send.put(att_ref, att_o.at[here, :])
        send.put(qn_ref, qn_o.at[here, :])
        send.put(sg_ref, sg_o.at[here, :])
        send.put(sb_ref, sb_o.at[chunk])
        loaded(2)
        residual = x.astype(f32) + nn_dot(att_ref[...], wo_ref[...])
        n1, r1 = norm_rows(residual)
        n1_ref[...] = n1.astype(bf)
        hidden = n1 * gb_ref[0:1, :] + gb_ref[1:2, :]
        hb = hidden.astype(bf)
        hb_ref[...] = hb
        send.put(n1_ref, n1_o.at[here, :])
        send.put(hb_ref, hb_o.at[here, :])
        total = hidden
        loaded(3, 4)
        FB = 768
        for j in range(0, 4 * D, FB):
            cols = slice(j, j + FB)
            u = nn_dot(hb, wu_ref[:, cols])
            cdf = 0.5 + 0.5 * lax.erf(u * (1.0 / math.sqrt(2.0)))
            act = (u * cdf).astype(bf)
            act_ref[:, cols] = act
            gp_ref[:, cols] = (cdf + u * (jnp.exp(-0.5 * u * u) * (1.0 / math.sqrt(2.0 * math.pi)))).astype(bf)
            for i in range(j // TILE, (j + FB) // TILE):
                send.put(act_ref.at[:, i * TILE:(i + 1) * TILE], act_o.at[i, here, :])
            send.put(gp_ref.at[:, cols], gp_o.at[here, cols])
            total = total + nn_dot(act, wd_ref[cols, :])
        n2, r2 = norm_rows(total)
        n2_ref[...] = n2.astype(bf)
        lane = lax.broadcasted_iota(jnp.int32, (rows, 128), 1)
        rs_ref[...] = jnp.where(lane < 64, r1, r2)
        send.put(n2_ref, n2_o.at[here, :])
        send.put(rs_ref, rs_o.at[here, :])
        y_ref[...] = (n2 * gb_ref[2:3, :] + gb_ref[3:4, :]).astype(bf)
        send.put(y_ref, all_o.at[here, :])
        loaded(5, 6)
        send.finish()


def far(items):
    return [pltpu.with_memory_space_constraint(item, pltpu.HBM) for item in items]


def near(items):
    return [pltpu.with_memory_space_constraint(item, pltpu.VMEM) for item in items]


def forward_opening(delta, n, rows, *refs):
    ins, refs = refs[:12], refs[12:]
    outs, kept, scratch, load_sems = refs[:16], refs[16:25], refs[25:-1], refs[-1]
    tok, cot, cos, sin, *weights, gb = ins[3:]
    tok_v, cot_v, _, _, *weights_v, _ = kept
    head, tail = pl.ds(0, rows), pl.ds(rows, (n - 1) * rows)
    pairs = [(tok.at[head, :], tok_v.at[head, :])] + list(zip(weights, weights_v)) + [(tok.at[tail, :], tok_v.at[tail, :]), (cot, cot_v)]
    loads = [pltpu.make_async_copy(src, dst, load_sems.at[i]) for i, (src, dst) in enumerate(pairs)]
    for copy in loads:
        copy.start()
    forward_kernel(delta, n, rows, *ins[:2], tok_v, ins[2], cos, sin, *weights_v, gb, None, *outs, *scratch, loads=loads)


def forward_next(delta, n, rows, *refs):
    t, meta, arr, tok, cot, cos, sin, wq, wo, wu, wd, gb, s_in = refs[:13]
    forward_kernel(delta, n, rows, t, meta, tok, arr, cos, sin, wq, wo, wu, wd, gb, s_in, *refs[27:43], *refs[52:])


def saved_items(rows):
    return [((rows, D), bf)] * 3 + [((rows, 4 * D), bf), ((rows, 2 * D), bf), ((rows, 2 * D), bf), ((rows, D), bf), ((rows, 2 * D), bf),
                                    ((rows, D), bf), ((rows, 4 * D), bf), ((rows, D), bf), ((rows, 128), f32), ((PAIRS, 256, 256), bf)]


def kept_items(every):
    return [((every, D), bf), ((every, D), bf), ((every, 128), f32), ((every, 128), f32),
            ((D, 3 * D), bf), ((D, D), bf), ((D, 4 * D), bf), ((4 * D, D), bf), ((4, D), f32)]


def forward_call(rows, n, delta, opening, limit=22):
    V = pl.BlockSpec(memory_space=pltpu.VMEM)
    S = pl.BlockSpec(memory_space=pltpu.SMEM)
    A = pl.BlockSpec(memory_space=pl.ANY)
    sd = jax.ShapeDtypeStruct
    every = n * rows
    big = [pltpu.HBM((every, D), bf)] + [pltpu.HBM(*item) for item in saved_items(every)]
    big[4] = pltpu.HBM((TILES, every, TILE), bf)
    big[13] = pltpu.HBM((n, PAIRS, 256, 256), bf)
    aliases = {5: 18, 6: 19, 11: 24}
    if not opening:
        aliases = {12: 1, **{13 + i: 2 + i for i in range(14)}, **{3 + i: 16 + i for i in range(9)}}
    return pl.pallas_call(
        functools.partial(forward_opening if opening else forward_next, delta, n, rows),
        in_specs=[S, S, V, A, A, V, V, A, A, A, A, V] if opening else [S, S] + [V] * 11 + [A] * 14,
        out_specs=[V, V] + [A] * 14 + [V] * 9,
        out_shape=[sd((rows, D), bf), sd((PAIRS, 256, 256), f32)] + big + [pltpu.VMEM(*item) for item in kept_items(every)],
        scratch_shapes=[pltpu.VMEM(*item) for item in saved_items(rows)] + [pltpu.SemaphoreType.DMA((30,))] + [pltpu.SemaphoreType.DMA((7,))] * opening,
        input_output_aliases=aliases,
        cost_estimate=pl.CostEstimate(flops=rows * 2 * 9 * 10**6, bytes_accessed=4 * 2**20, transcendentals=0),
        compiler_params=pltpu.CompilerParams(vmem_limit_bytes=limit * 2**20),
        name="layer_forward",
    )


def norm_back(grad, normed, rstd, gain):
    scaled = grad * gain
    mean_one = jnp.mean(scaled, axis=-1, keepdims=True)
    mean_two = jnp.mean(scaled * normed, axis=-1, keepdims=True)
    return rstd * (scaled - mean_one - normed * mean_two)


def backward_kernel(delta, n, rows, stages, groups,
                    t_ref, meta_ref, cot_ref, arr_ref, cos_ref, sin_ref,
                    wq_ref, wo_ref, wu_ref, wd_ref, gb_ref, t_in, ga_in,
                    n2_i, rs_i, gp_i, n1_i, att_i, v_i, qn_i, kf_i, sg_i, sb_i,
                    ds_ref, t_out, ga_out, df_o, du_o, de_o, all_o,
                    df_ref, du_ref, de_ref, dm_ref, da_ref, g_ref,
                    n2_ref, rs_ref, gp_ref, n1_ref, att_ref, v_ref, qn_ref, kf_ref, sg_ref, sb_ref, sems, fetch_sems, loads=()):
    stage = meta_ref[0]
    chunk = n - 1 - t_ref[0] + delta * (stages - 1 - stage)
    valid = (chunk >= 0) & (chunk < n)

    def loaded(*which):
        for i in which:
            if loads:
                loads[i].wait()

    @pl.when(jnp.logical_not(valid))
    def _():
        loaded(*range(len(loads)))

    @pl.when(valid)
    def _():
        base = pl.multiple_of(chunk * rows, rows)
        here = pl.ds(base, rows)
        fetched = []
        quarters = [slice(j, j + D) for j in range(0, 4 * D, D)]
        pairs = [(n2_i.at[here, :], n2_ref), (rs_i.at[here, :], rs_ref)] + [(gp_i.at[here, cols], gp_ref.at[:, cols]) for cols in quarters]
        pairs += [(src.at[here, :], dst) for src, dst in ((n1_i, n1_ref), (att_i, att_ref), (v_i, v_ref), (qn_i, qn_ref), (kf_i, kf_ref), (sg_i, sg_ref))]
        pairs += [(sb_i.at[chunk], sb_ref)]
        for i, (src, dst) in enumerate(pairs):
            copy = pltpu.make_async_copy(src, dst, fetch_sems.at[i])
            copy.start()
            fetched.append(copy)
        send = Sender(sems)
        last = meta_ref[2 + n + chunk] != 0

        loaded(0)

        if cot_ref is None:
            g_ref[...] = arr_ref[...]
        else:
            @pl.when(stage == stages - 1)
            def _():
                g_ref[...] = cot_ref[pl.ds(base, rows), :]

            @pl.when(stage != stages - 1)
            def _():
                g_ref[...] = arr_ref[...]

        @pl.when(last)
        def _():
            t_out[...] = jnp.zeros_like(t_out)

        if t_in is not None:
            @pl.when(jnp.logical_not(last))
            def _():
                t_out[...] = t_in[...]

        @pl.when(chunk == n - 1)
        def _():
            ga_out[...] = jnp.zeros_like(ga_out)

        if ga_in is not None:
            @pl.when(chunk != n - 1)
            def _():
                ga_out[...] = ga_in[...]

        g = g_ref[...].astype(f32)
        fetched[0].wait()
        fetched[1].wait()
        n2 = n2_ref[...].astype(f32)
        r1 = rs_ref[:, 0:1]
        r2 = rs_ref[:, 64:65]
        ga_out[2:3, :] += jnp.sum(g * n2, axis=0, keepdims=True)
        ga_out[3:4, :] += jnp.sum(g, axis=0, keepdims=True)
        d_two = norm_back(g, n2, r2, gb_ref[2:3, :])
        df = d_two.astype(bf)
        df_ref[...] = df
        send.put(df_ref, df_o.at[here, :])
        total = d_two
        loaded(1, 2)
        for cols, copy in zip(quarters, fetched[2:6]):
            copy.wait()
            du = (nt_dot(df, wd_ref[cols, :]) * gp_ref[:, cols].astype(f32)).astype(bf)
            du_ref[:, cols] = du
            for i in range(cols.start // TILE, cols.stop // TILE):
                send.put(du_ref.at[:, i * TILE:(i + 1) * TILE], du_o.at[i, here, :])
            total = total + nt_dot(du, wu_ref[:, cols])
        fetched[6].wait()
        n1 = n1_ref[...].astype(f32)
        ga_out[0:1, :] += jnp.sum(total * n1, axis=0, keepdims=True)
        ga_out[1:2, :] += jnp.sum(total, axis=0, keepdims=True)
        d_res = norm_back(total, n1, r1, gb_ref[0:1, :])
        dp = d_res.astype(bf)
        loaded(3)
        da_ref[...] = nt_dot(dp, wo_ref[...]).astype(bf)
        for copy in fetched[7:]:
            copy.wait()
        cos = cos_ref[pl.ds(base, rows), :]
        sin = sin_ref[pl.ds(base, rows), :]
        m_a = head_lanes(rows, 256)
        lane = lax.broadcasted_iota(jnp.int32, (rows, 128), 1)
        ri = lax.broadcasted_iota(jnp.int32, (rows, rows), 0)
        ci = lax.broadcasted_iota(jnp.int32, (rows, rows), 1)
        tril = ci <= ri
        triu = ri <= ci
        diag = block_diag(256)
        ones = jnp.ones((rows, 128), bf)
        zero = jnp.zeros((), bf)
        for p in range(PAIRS):
            lanes = slice(128 * p, 128 * p + 128)
            wide = slice(256 * p, 256 * p + 256)
            d_o = da_ref[:, lanes]
            prod = d_o.astype(f32) * att_ref[:, lanes].astype(f32)
            in_a = jnp.sum(jnp.where(lane < 64, prod, 0.0), axis=1, keepdims=True)
            in_b = jnp.sum(jnp.where(lane < 64, 0.0, prod), axis=1, keepdims=True)
            inner = jnp.where(lane < 64, -in_a, -in_b)
            high = inner.astype(bf).astype(f32)
            ext = jnp.where((lane & 63) == 0, high, jnp.where((lane & 63) == 1, inner - high, 0.0)).astype(bf)
            left = jnp.concatenate([d_o, ext], axis=1)
            left_a, left_b = jnp.where(m_a, left, zero), jnp.where(m_a, zero, left)
            ve = jnp.concatenate([v_ref[:, lanes], ones], axis=1)
            qn = qn_ref[:, wide]
            kf = kf_ref[:, wide]
            qn_a, qn_b = jnp.where(m_a, qn, zero), jnp.where(m_a, zero, qn)
            kf_a, kf_b = jnp.where(m_a, kf, zero), jnp.where(m_a, zero, kf)
            pt = jnp.concatenate([jnp.where(triu, nt_dot(kf, qn_a), 0.0), jnp.where(triu, nt_dot(kf, qn_b), 0.0)], axis=1).astype(bf)
            gg = jnp.concatenate([jnp.where(tril, nt_dot(left_a, ve), 0.0), jnp.where(tril, nt_dot(left_b, ve), 0.0)], axis=1).astype(bf)
            gt = jnp.concatenate([jnp.where(triu, nt_dot(ve, left_a), 0.0), jnp.where(triu, nt_dot(ve, left_b), 0.0)], axis=1).astype(bf)
            after = t_out[p].astype(bf)
            dv = nn_dot(pt, jnp.concatenate([left_a[:, :128], left_b[:, :128]], axis=0)) + nn_dot(kf, after[:, :128])
            dq = nn_dot(gg, jnp.concatenate([kf_a, kf_b], axis=0)) + nt_dot(left, sb_ref[p])
            dk = nn_dot(gt, jnp.concatenate([qn_a, qn_b], axis=0)) + nt_dot(ve, after)
            t_out[p] = t_out[p] + jnp.where(diag, tn_dot(qn, left), 0.0)
            sq = sg_ref[:, lanes].astype(f32)
            sk = sg_ref[:, D + 128 * p:D + 128 * p + 128].astype(f32)
            dm_ref[:, lanes] = ((dq[:, :128] * cos + dq[:, 128:] * sin) * sq).astype(bf)
            dm_ref[:, D + 128 * p:D + 128 * p + 128] = ((dk[:, :128] * cos + dk[:, 128:] * sin) * sk).astype(bf)
            dm_ref[:, 2 * D + 128 * p:2 * D + 128 * p + 128] = dv.astype(bf)
        loaded(4, 5)
        dm = dm_ref[...]
        for g in range(groups):
            odd = g & 1
            part, rest = 9 * g, 3 * g
            inner, outer = part + odd, rest + odd
            de_ref[:, g * D:g * D + 4 * 128] = dm[:, inner * 64:inner * 64 + 4 * 128]
            de_ref[:, g * D + 5 * 128:(g + 1) * D] = dp[:, outer * 64:outer * 64 + 128]
            one = dm[:, (part if odd else part + 8) // 2 * 128:][:, :128].astype(f32)
            two = dp[:, (rest if odd else rest + 2) // 2 * 128:][:, :128].astype(f32)
            if odd:
                one = pltpu.roll(one, 64, 1)
            else:
                two = pltpu.roll(two, 64, 1)
            de_ref[:, g * D + 4 * 128:g * D + 5 * 128] = jnp.where(lane < 64, one, two).astype(bf)
        for i in range(TILES):
            send.put(de_ref.at[:, i * TILE:(i + 1) * TILE], de_o.at[i, here, :])
        ds_ref[...] = (d_res + nt_dot(dm, wq_ref[...])).astype(bf)
        send.put(ds_ref, all_o.at[here, :])
        send.finish()


def backward_opening(delta, n, rows, stages, groups, *refs):
    t, meta, arr, cot = refs[:4]
    backward_kernel(delta, n, rows, stages, groups, t, meta, cot, arr, *refs[4:11], None, None, *refs[11:28], *refs[36:])


def backward_next(delta, n, rows, stages, groups, *refs):
    t, meta, arr, cot = refs[:4]
    backward_kernel(delta, n, rows, stages, groups, t, meta, cot, arr, *refs[4:23], *refs[27:34], *refs[42:])


def backward_closing(delta, n, rows, stages, groups, *refs):
    t, meta, arr = refs[:3]
    act, refs, outs = refs[26], refs[3:22] + refs[27:], refs[27:34]
    act_v, rest, sem = refs[19 + 14], refs[19 + 15:-1], refs[-1]
    copies = [pltpu.make_async_copy(act.at[i], act_v.at[i], sem.at[i]) for i in range(TILES)]
    for copy in copies:
        copy.start()
    backward_kernel(delta, n, rows, stages, groups, t, meta, None, arr, *refs[:19], *outs, *rest)
    for copy in copies:
        copy.wait()


def backward_call(rows, n, delta, stages, groups, opening, closing, limit=22):
    V = pl.BlockSpec(memory_space=pltpu.VMEM)
    S = pl.BlockSpec(memory_space=pltpu.SMEM)
    A = pl.BlockSpec(memory_space=pl.ANY)
    sd = jax.ShapeDtypeStruct
    every = n * rows
    made = [((rows, D), bf), ((rows, 4 * D), bf), ((rows, 4 * D), bf)]
    saved = [((rows, D), bf), ((rows, 128), f32), ((rows, 4 * D), bf), ((rows, D), bf), ((rows, D), bf), ((rows, D), bf),
             ((rows, 2 * D), bf), ((rows, 2 * D), bf), ((rows, 2 * D), bf), ((PAIRS, 256, 256), bf)]
    own = [((rows, 3 * D), bf), ((rows, D), bf), ((rows, D), bf)]
    big = [pltpu.HBM((every, D), bf), pltpu.HBM((TILES, every, TILE), bf), pltpu.HBM((TILES, every, TILE), bf), pltpu.HBM((every, D), bf)]
    return pl.pallas_call(
        functools.partial(backward_opening if opening else backward_closing if closing else backward_next, delta, n, rows, stages, groups),
        in_specs=[S, S] + [V] * 9 + [A] * 10 if opening else [S, S] + [V] * (11 - closing) + [A] * (14 + closing),
        out_specs=[V] * 3 + [A] * 4 + [V] * 8,
        out_shape=[sd((rows, D), bf), sd((PAIRS, 256, 256), f32), sd((8, D), f32)] + big
        + [pltpu.VMEM(*item) for item in kept_items(every)[1 + closing:]] + [pltpu.VMEM((TILES, every, TILE), bf)] * closing,
        scratch_shapes=[pltpu.VMEM(*item) for item in made + own + saved] + [pltpu.SemaphoreType.DMA((30,)), pltpu.SemaphoreType.DMA((13,))]
        + [pltpu.SemaphoreType.DMA((TILES,))] * closing,
        input_output_aliases={**{3 + i: 7 + i for i in range(8 - closing)}, **({} if opening else {11 - closing: 1, 12 - closing: 2, **{23 - closing + i: 3 + i for i in range(4)}})},
        cost_estimate=pl.CostEstimate(flops=rows * 2 * 10 * 10**6, bytes_accessed=4 * 2**20, transcendentals=0),
        compiler_params=pltpu.CompilerParams(vmem_limit_bytes=limit * 2**20),
        name="layer_backward",
    )


HALF = D // 2


def weight_kernel(groups, mixed, waits, meta_ref, left, *refs):
    raws, refs = refs[:1 + mixed], refs[1 + mixed + waits:]
    outs, (turned, out_buf, out_sem) = refs[:4], refs[4:]
    me = meta_ref[1]
    share = TILES // groups
    for j, raw in enumerate(raws):
        for k in range(0, raw.shape[0], 256):
            turned[j, :, k:k + 256] = raw[k:k + 256, :].T
    for g in range(groups):
        for i in range(share):
            cols = slice(i * TILE, (i + 1) * TILE)
            value = nn_dot(turned[0], left[g * share + i])
            if mixed and i == share - 1:
                other = nn_dot(turned[1], left[g * share + i])
                lane = lax.broadcasted_iota(jnp.int32, other.shape, 1)
                value = jnp.where(lane < 3 * D // groups - i * TILE, value, other)
            out_buf[g, :, cols] = value.astype(bf)
        rel = g ^ me
        for half in range(2):
            part = out_buf.at[g, half * HALF:(half + 1) * HALF, :]

            @pl.when((rel & 1) == 0)
            def _():
                pltpu.make_async_copy(part, outs[2 * half].at[rel >> 1], out_sem).start()

            @pl.when((rel & 1) == 1)
            def _():
                pltpu.make_async_copy(part, outs[2 * half + 1].at[rel >> 1], out_sem).start()
    pltpu.make_async_copy(out_buf, out_buf, out_sem).wait()


def weight_call(every, groups, mixed, waits, limit=22):
    V = pl.BlockSpec(memory_space=pltpu.VMEM)
    S = pl.BlockSpec(memory_space=pltpu.SMEM)
    A = pl.BlockSpec(memory_space=pl.ANY)
    raws = 1 + mixed
    return pl.pallas_call(
        functools.partial(weight_kernel, groups, mixed, waits),
        in_specs=[S] + [V] * (1 + raws) + [A] * waits,
        out_specs=[A] * 4,
        out_shape=[pltpu.HBM((2, HALF, D), bf)] * 4,
        scratch_shapes=[pltpu.VMEM((raws, D, every), bf), pltpu.VMEM((groups, D, D), bf), pltpu.SemaphoreType.DMA],
        cost_estimate=pl.CostEstimate(flops=2 * every * D * 4 * D, bytes_accessed=every * 5 * D * 2, transcendentals=0),
        compiler_params=pltpu.CompilerParams(vmem_limit_bytes=limit * 2**20),
        name="weight_grad",
    )


MB_ROWS = 1024
MICRO = 2
ROWS = 256
DELTA = 2


def geometry(doc_ids):
    quarter = MB_ROWS // 4
    marks = doc_ids.reshape(-1, MB_ROWS)[:, ::quarter]
    pieces = 1 + jnp.sum((marks[:, 1:] != marks[:, :-1]).astype(jnp.int32), axis=1)
    length = MB_ROWS // pieces
    row = jnp.arange(MB_ROWS, dtype=jnp.int32)
    position = row[None, :] % length[:, None]
    angle = (0.5 * math.pi) * position.astype(f32) / length[:, None].astype(f32)
    angle = angle.reshape(-1, 1)
    starts = jnp.arange(0, MB_ROWS, ROWS, dtype=jnp.int32)
    first = (starts[None, :] % length[:, None]) == 0
    last = ((starts[None, :] + ROWS) % length[:, None]) == 0
    wide = (angle.shape[0], 128)
    return (jnp.broadcast_to(jnp.cos(angle), wide), jnp.broadcast_to(jnp.sin(angle), wide),
            first.reshape(-1).astype(jnp.int32), last.reshape(-1).astype(jnp.int32))


def exchange(block, axis, flip):
    route = [(i, i ^ flip) for i in range(lax.axis_size(axis))]
    return lax.ppermute(block, axis, route)


def reduced(keep, send, wire):
    got = exchange(send, "group", 1)
    away = lax.optimization_barrier((keep[1].astype(f32) + got[1].astype(f32)).astype(wire))
    back = exchange(away, "group", 2)
    own = lax.optimization_barrier((keep[0].astype(f32) + got[0].astype(f32) + back.astype(f32)).astype(wire))
    if lax.axis_size("dp") == 2:
        return away, own, own.astype(f32) + exchange(own, "dp", 1).astype(f32)
    return away, own, lax.psum(own, "dp").astype(f32)


def local(tokens, doc_ids, cotangent, w_qkv, w_out, w_up, w_down,
          first_gain, first_bias, second_gain, second_bias):
    stages = lax.axis_size("pipe")
    groups = lax.axis_size("group")
    stage = lax.axis_index("pipe").astype(jnp.int32)
    me = lax.axis_index("group").astype(jnp.int32)
    n = tokens.shape[0] // ROWS
    ticks = n + DELTA * (stages - 1)
    cos, sin, first, last = geometry(doc_ids)
    meta = jnp.concatenate([stage[None], me[None], first, last])
    resident = far((tokens, cotangent)) + [cos, sin] + far((w_qkv[0], w_out[0], w_up[0], w_down[0]))
    gb = jnp.concatenate([first_gain, first_bias, second_gain, second_bias], axis=0)
    blank = jnp.zeros((ROWS, D), bf)
    arriving = [blank] * DELTA
    resident = resident + [gb]
    state, big = (), ()
    for t in range(ticks):
        made = forward_call(ROWS, n, DELTA, t == 0)(jnp.full((1,), t, jnp.int32), meta, arriving.pop(0), *resident, *state, *big)
        state, big, resident = made[1:2], made[2:16], made[16:]
        route = [(a, a + 1) for a in range(stages - 1) if 0 <= t - a * DELTA < n]
        arriving.append(lax.ppermute(made[0], "pipe", route) if route else made[0])
    block_out, x, att, hb, act, qn, kf, v, sg, n1, gp, n2, rs, sb = big
    arriving = [made[0]] * DELTA
    state, big, resident = (), (), resident[1:]
    for t in range(ticks):
        closing = t == ticks - 1
        made = backward_call(ROWS, n, DELTA, stages, groups, t == 0, closing)(
            jnp.full((1,), t, jnp.int32), meta, arriving.pop(0), *resident[closing:], *state,
            *far((n2, rs, gp, n1, att, v, qn, kf, sg, sb)), *big, *far([act] * closing))
        state, big, resident = made[1:3], made[3:7], made[7:]
        route = [(a, a - 1) for a in range(1, stages) if 0 <= t - (stages - 1 - a) * DELTA < n]
        arriving.append(lax.ppermute(made[0], "pipe", route) if route else made[0])
    df, du, de, input_grad = big
    act = resident[7]
    aways, owns, parts = [], [], []
    for left, rights in ((act, (df,)), (de, (x, att)), (du, (hb,))):
        waits = aways[-2:] + owns[-2:-1]
        made = weight_call(n * ROWS, groups, len(rights) == 2, len(waits))(meta, left, *rights, *waits)
        for half in range(2):
            away, own, part = reduced(made[2 * half], made[2 * half + 1], bf)
            aways.append(away)
            owns.append(own)
            parts.append(part)
    vectors = state[1][:4].reshape(4, groups, D // groups).swapaxes(0, 1).reshape(groups, 1, D)
    ordered = [lax.dynamic_index_in_dim(vectors, me ^ rel, 0, keepdims=False) for rel in range(4)]
    mine = reduced(jnp.stack(ordered[0::2]), jnp.stack(ordered[1::2]), f32)[2].reshape(4, D // groups)
    g_down, g_mixed, g_up = (jnp.concatenate(parts[i:i + 2], axis=0) for i in (0, 2, 4))
    odd = (me & 1) == 1
    swap = lambda a, b: jnp.concatenate([g_mixed[:, a], g_mixed[:, b]], axis=1)
    low, one, two, high = slice(0, 512), slice(512, 576), slice(576, 640), slice(640, 768)
    g_qkv = jnp.where(odd, swap(one, low), swap(low, one))
    g_out = jnp.where(odd, swap(two, high), swap(high, two))
    return (block_out[None], input_grad[None], g_qkv[None], g_out[None], g_up[None], g_down.T[None],
            mine[0:1], mine[1:2], mine[2:3], mine[3:4])


def solution(mesh):
    rows = ("group", "dp")
    whole = P("pipe", None, None)
    vector = P("pipe", None)
    return jax.shard_map(
        local,
        mesh=mesh,
        in_specs=(P(rows, None), P(rows), P(rows, None)) + (whole,) * 4 + (vector,) * 4,
        out_specs=(P("pipe", rows, None), P("pipe", rows, None), P("pipe", None, "group"), P("pipe", None, "group"),
                   P("pipe", None, "group"), P("pipe", "group", None)) + (P("pipe", "group"),) * 4,
        check_vma=False,
    )
```

```python
import functools, math
import jax, jax.numpy as jnp
from jax import lax
from jax.experimental import pallas as pl
from jax.experimental.pallas import tpu as pltpu
from jax.sharding import PartitionSpec as P

bf = jnp.bfloat16
f32 = jnp.float32
EPS = 1e-05
D = 768
PAIRS = 6
TILE = 256
TILES = 4 * D // TILE
NT = (((1,), (1,)), ((), ()))
TN = (((0,), (0,)), ((), ()))


def nn_dot(a, b):
    return jnp.dot(a, b, preferred_element_type=f32)


def nt_dot(a, b):
    return lax.dot_general(a, b, NT, preferred_element_type=f32)


def tn_dot(a, b):
    return lax.dot_general(a, b, TN, preferred_element_type=f32)


def head_lanes(rows, lanes):
    lane = lax.broadcasted_iota(jnp.int32, (rows, lanes), 1)
    return (lane & 64) == 0


def block_diag(size):
    r = lax.broadcasted_iota(jnp.int32, (size, size), 0)
    c = lax.broadcasted_iota(jnp.int32, (size, size), 1)
    return ((r ^ c) & 64) == 0


def soft_pair(raw):
    e = jnp.exp(-jnp.abs(raw))
    one = 1.0 + e
    tail = jnp.where(e < 1e-3, e * (1.0 - e * (0.5 - e * (1.0 / 3.0))), jnp.log(one))
    soft = jnp.maximum(raw, 0.0) + tail
    sig = jnp.where(raw >= 0.0, 1.0, e) / one
    return soft, sig


def norm_rows(v):
    centre = jnp.mean(v, axis=-1, keepdims=True)
    centred = v - centre
    spread = jnp.mean(centred * centred, axis=-1, keepdims=True)
    rstd = lax.rsqrt(spread + EPS)
    return centred * rstd, rstd


class Sender:
    def __init__(self, sems):
        self.sems, self.copies = sems, []

    def put(self, src, dst):
        copy = pltpu.make_async_copy(src, dst, self.sems.at[len(self.copies)])
        copy.start()
        self.copies.append(copy)

    def finish(self):
        for copy in self.copies:
            copy.wait()


def forward_kernel(delta, n, rows,
                   t_ref, meta_ref, tok_ref, arr_ref, cos_ref, sin_ref,
                   wq_ref, wo_ref, wu_ref, wd_ref, gb_ref, s_in,
                   y_ref, s_out, all_o, x_o, att_o, hb_o, act_o, qn_o, kf_o, v_o, sg_o, n1_o, gp_o, n2_o, rs_o, sb_o,
                   x_ref, att_ref, hb_ref, act_ref, qn_ref, kf_ref, v_ref, sg_ref, n1_ref, gp_ref, n2_ref, rs_ref, sb_ref, sems, loads=()):
    stage = meta_ref[0]
    chunk = t_ref[0] - delta * stage
    valid = (chunk >= 0) & (chunk < n)

    def loaded(*which):
        for i in which:
            if loads:
                loads[i].wait()

    @pl.when(jnp.logical_not(valid))
    def _():
        loaded(*range(len(loads)))

    @pl.when(valid)
    def _():
        send = Sender(sems)
        base = pl.multiple_of(chunk * rows, rows)
        here = pl.ds(base, rows)
        first = meta_ref[2 + chunk] != 0
        loaded(0)

        @pl.when(stage == 0)
        def _():
            x_ref[...] = tok_ref[pl.ds(base, rows), :]

        @pl.when(stage != 0)
        def _():
            x_ref[...] = arr_ref[...]

        @pl.when(first)
        def _():
            s_out[...] = jnp.zeros_like(s_out)

        if s_in is not None:
            @pl.when(jnp.logical_not(first))
            def _():
                s_out[...] = s_in[...]

        send.put(x_ref, x_o.at[here, :])
        x = x_ref[...]
        cos = cos_ref[pl.ds(base, rows), :]
        sin = sin_ref[pl.ds(base, rows), :]
        loaded(1)
        q_raw = nn_dot(x, wq_ref[:, 0:D])
        k_raw = nn_dot(x, wq_ref[:, D:2 * D])
        v_ref[...] = nn_dot(x, wq_ref[:, 2 * D:]).astype(bf)
        send.put(v_ref, v_o.at[here, :])
        m_a = head_lanes(rows, 256)
        ri = lax.broadcasted_iota(jnp.int32, (rows, rows), 0)
        ci = lax.broadcasted_iota(jnp.int32, (rows, rows), 1)
        tril = ci <= ri
        diag = block_diag(256)
        ones = jnp.ones((rows, 128), bf)
        zero = jnp.zeros((), bf)
        for p in range(PAIRS):
            lanes = slice(128 * p, 128 * p + 128)
            wide = slice(256 * p, 256 * p + 256)
            q, sq = soft_pair(q_raw[:, lanes])
            k, sk = soft_pair(k_raw[:, lanes])
            qc, qs = q * cos, q * sin
            qf = jnp.concatenate([qc, qs], axis=1).astype(bf)
            kf = jnp.concatenate([k * cos, k * sin], axis=1).astype(bf)
            kf_ref[:, wide] = kf
            sg_ref[:, D + 128 * p:D + 128 * p + 128] = sk.astype(bf)
            ve = jnp.concatenate([v_ref[:, lanes], ones], axis=1)
            s_a = nt_dot(jnp.where(m_a, qf, zero), kf)
            s_b = nt_dot(jnp.where(m_a, zero, qf), kf)
            p_ab = jnp.concatenate([jnp.where(tril, s_a, 0.0), jnp.where(tril, s_b, 0.0)], axis=1).astype(bf)
            ve2 = jnp.concatenate([jnp.where(m_a, ve, zero), jnp.where(m_a, zero, ve)], axis=0)
            before = s_out[p].astype(bf)
            sb_ref[p] = before
            nd = nn_dot(p_ab, ve2) + nn_dot(qf, before)
            inv = 1.0 / nd[:, 128:]
            att_ref[:, lanes] = (nd[:, :128] * inv).astype(bf)
            qn_ref[:, wide] = jnp.concatenate([qc * inv, qs * inv], axis=1).astype(bf)
            sg_ref[:, lanes] = (sq * inv).astype(bf)
            s_out[p] = s_out[p] + jnp.where(diag, tn_dot(kf, ve), 0.0)
        send.put(kf_ref, kf_o.at[here, :])
        send.put(att_ref, att_o.at[here, :])
        send.put(qn_ref, qn_o.at[here, :])
        send.put(sg_ref, sg_o.at[here, :])
        send.put(sb_ref, sb_o.at[chunk])
        loaded(2)
        residual = x.astype(f32) + nn_dot(att_ref[...], wo_ref[...])
        n1, r1 = norm_rows(residual)
        n1_ref[...] = n1.astype(bf)
        hidden = n1 * gb_ref[0:1, :] + gb_ref[1:2, :]
        hb = hidden.astype(bf)
        hb_ref[...] = hb
        send.put(n1_ref, n1_o.at[here, :])
        send.put(hb_ref, hb_o.at[here, :])
        total = hidden
        loaded(3, 4)
        FB = 768
        for j in range(0, 4 * D, FB):
            cols = slice(j, j + FB)
            u = nn_dot(hb, wu_ref[:, cols])
            cdf = 0.5 + 0.5 * lax.erf(u * (1.0 / math.sqrt(2.0)))
            act = (u * cdf).astype(bf)
            act_ref[:, cols] = act
            gp_ref[:, cols] = (cdf + u * (jnp.exp(-0.5 * u * u) * (1.0 / math.sqrt(2.0 * math.pi)))).astype(bf)
            for i in range(j // TILE, (j + FB) // TILE):
                send.put(act_ref.at[:, i * TILE:(i + 1) * TILE], act_o.at[i, here, :])
            send.put(gp_ref.at[:, cols], gp_o.at[here, cols])
            total = total + nn_dot(act, wd_ref[cols, :])
        n2, r2 = norm_rows(total)
        n2_ref[...] = n2.astype(bf)
        lane = lax.broadcasted_iota(jnp.int32, (rows, 128), 1)
        rs_ref[...] = jnp.where(lane < 64, r1, r2)
        send.put(n2_ref, n2_o.at[here, :])
        send.put(rs_ref, rs_o.at[here, :])
        y_ref[...] = (n2 * gb_ref[2:3, :] + gb_ref[3:4, :]).astype(bf)
        send.put(y_ref, all_o.at[here, :])
        loaded(5)
        send.finish()


def far(items):
    return [pltpu.with_memory_space_constraint(item, pltpu.HBM) for item in items]


def near(items):
    return [pltpu.with_memory_space_constraint(item, pltpu.VMEM) for item in items]


def forward_opening(delta, n, rows, *refs):
    ins, refs = refs[:11], refs[11:]
    outs, kept, scratch, load_sems = refs[:16], refs[16:24], refs[24:-1], refs[-1]
    tok, cos, sin, *weights, gb = ins[3:]
    tok_v, _, _, *weights_v = kept[:7]
    head, tail = pl.ds(0, rows), pl.ds(rows, (n - 1) * rows)
    pairs = [(tok.at[head, :], tok_v.at[head, :])] + list(zip(weights, weights_v)) + [(tok.at[tail, :], tok_v.at[tail, :])]
    loads = [pltpu.make_async_copy(src, dst, load_sems.at[i]) for i, (src, dst) in enumerate(pairs)]
    for copy in loads:
        copy.start()
    forward_kernel(delta, n, rows, *ins[:2], tok_v, ins[2], cos, sin, *weights_v, gb, None, *outs, *scratch, loads=loads)


def forward_next(delta, n, rows, *refs):
    t, meta, arr, tok = refs[:4]
    forward_kernel(delta, n, rows, t, meta, tok, arr, *refs[4:12], *refs[26:42], *refs[50:])


def saved_items(rows):
    return [((rows, D), bf)] * 3 + [((rows, 4 * D), bf), ((rows, 2 * D), bf), ((rows, 2 * D), bf), ((rows, D), bf), ((rows, 2 * D), bf),
                                    ((rows, D), bf), ((rows, 4 * D), bf), ((rows, D), bf), ((rows, 128), f32), ((PAIRS, 256, 256), bf)]


def kept_items(every):
    return [((every, D), bf), ((every, 128), f32), ((every, 128), f32), ((D, 3 * D), bf), ((D, D), bf), ((D, 4 * D), bf), ((4 * D, D), bf),
            ((4, D), f32)]


def forward_call(rows, n, delta, opening, limit=20):
    V = pl.BlockSpec(memory_space=pltpu.VMEM)
    S = pl.BlockSpec(memory_space=pltpu.SMEM)
    A = pl.BlockSpec(memory_space=pl.ANY)
    sd = jax.ShapeDtypeStruct
    every = n * rows
    big = [pltpu.HBM((every, D), bf)] + [pltpu.HBM(*item) for item in saved_items(every)]
    big[4] = pltpu.HBM((TILES, every, TILE), bf)
    big[13] = pltpu.HBM((n, PAIRS, 256, 256), bf)
    aliases = {4: 17, 5: 18, 10: 23}
    if not opening:
        aliases = {11: 1, **{12 + i: 2 + i for i in range(14)}, **{3 + i: 16 + i for i in range(8)}}
    return pl.pallas_call(
        functools.partial(forward_opening if opening else forward_next, delta, n, rows),
        in_specs=[S, S, V, A, V, V, A, A, A, A, V] if opening else [S, S] + [V] * 10 + [A] * 14,
        out_specs=[V, V] + [A] * 14 + [V] * 8,
        out_shape=[sd((rows, D), bf), sd((PAIRS, 256, 256), f32)] + big + [pltpu.VMEM(*item) for item in kept_items(every)],
        scratch_shapes=[pltpu.VMEM(*item) for item in saved_items(rows)] + [pltpu.SemaphoreType.DMA((30,))] + [pltpu.SemaphoreType.DMA((6,))] * opening,
        input_output_aliases=aliases,
        cost_estimate=pl.CostEstimate(flops=rows * 2 * 9 * 10**6, bytes_accessed=4 * 2**20, transcendentals=0),
        compiler_params=pltpu.CompilerParams(vmem_limit_bytes=limit * 2**20),
        name="layer_forward",
    )


def norm_back(grad, normed, rstd, gain):
    scaled = grad * gain
    mean_one = jnp.mean(scaled, axis=-1, keepdims=True)
    mean_two = jnp.mean(scaled * normed, axis=-1, keepdims=True)
    return rstd * (scaled - mean_one - normed * mean_two)


def backward_kernel(delta, n, rows, stages, groups,
                    t_ref, meta_ref, cot_ref, arr_ref, cos_ref, sin_ref,
                    wq_ref, wo_ref, wu_ref, wd_ref, gb_ref, t_in, ga_in,
                    n2_i, rs_i, gp_i, n1_i, att_i, v_i, qn_i, kf_i, sg_i, sb_i,
                    ds_ref, t_out, ga_out, df_o, du_o, de_o, all_o,
                    df_ref, du_ref, de_ref, dm_ref, da_ref, g_ref,
                    n2_ref, rs_ref, gp_ref, n1_ref, att_ref, v_ref, qn_ref, kf_ref, sg_ref, sb_ref, sems, fetch_sems, loads=()):
    stage = meta_ref[0]
    chunk = n - 1 - t_ref[0] + delta * (stages - 1 - stage)
    valid = (chunk >= 0) & (chunk < n)

    def loaded(*which):
        for i in which:
            if loads:
                loads[i].wait()

    @pl.when(jnp.logical_not(valid))
    def _():
        loaded(*range(len(loads)))

    @pl.when(valid)
    def _():
        base = pl.multiple_of(chunk * rows, rows)
        here = pl.ds(base, rows)
        fetched = []
        quarters = [slice(j, j + D) for j in range(0, 4 * D, D)]
        pairs = [(n2_i.at[here, :], n2_ref), (rs_i.at[here, :], rs_ref)] + [(gp_i.at[here, cols], gp_ref.at[:, cols]) for cols in quarters]
        pairs += [(src.at[here, :], dst) for src, dst in ((n1_i, n1_ref), (att_i, att_ref), (v_i, v_ref), (qn_i, qn_ref), (kf_i, kf_ref), (sg_i, sg_ref))]
        pairs += [(sb_i.at[chunk], sb_ref)]
        for i, (src, dst) in enumerate(pairs):
            copy = pltpu.make_async_copy(src, dst, fetch_sems.at[i])
            copy.start()
            fetched.append(copy)
        send = Sender(sems)
        last = meta_ref[2 + n + chunk] != 0

        loaded(0)

        if cot_ref is None:
            g_ref[...] = arr_ref[...]
        else:
            @pl.when(stage == stages - 1)
            def _():
                g_ref[...] = cot_ref[pl.ds(base, rows), :]

            @pl.when(stage != stages - 1)
            def _():
                g_ref[...] = arr_ref[...]

        @pl.when(last)
        def _():
            t_out[...] = jnp.zeros_like(t_out)

        if t_in is not None:
            @pl.when(jnp.logical_not(last))
            def _():
                t_out[...] = t_in[...]

        @pl.when(chunk == n - 1)
        def _():
            ga_out[...] = jnp.zeros_like(ga_out)

        if ga_in is not None:
            @pl.when(chunk != n - 1)
            def _():
                ga_out[...] = ga_in[...]

        g = g_ref[...].astype(f32)
        fetched[0].wait()
        fetched[1].wait()
        n2 = n2_ref[...].astype(f32)
        r1 = rs_ref[:, 0:1]
        r2 = rs_ref[:, 64:65]
        ga_out[2:3, :] += jnp.sum(g * n2, axis=0, keepdims=True)
        ga_out[3:4, :] += jnp.sum(g, axis=0, keepdims=True)
        d_two = norm_back(g, n2, r2, gb_ref[2:3, :])
        df = d_two.astype(bf)
        df_ref[...] = df
        send.put(df_ref, df_o.at[here, :])
        total = d_two
        for cols, copy in zip(quarters, fetched[2:6]):
            copy.wait()
            du = (nt_dot(df, wd_ref[cols, :]) * gp_ref[:, cols].astype(f32)).astype(bf)
            du_ref[:, cols] = du
            for i in range(cols.start // TILE, cols.stop // TILE):
                send.put(du_ref.at[:, i * TILE:(i + 1) * TILE], du_o.at[i, here, :])
            total = total + nt_dot(du, wu_ref[:, cols])
        fetched[6].wait()
        n1 = n1_ref[...].astype(f32)
        ga_out[0:1, :] += jnp.sum(total * n1, axis=0, keepdims=True)
        ga_out[1:2, :] += jnp.sum(total, axis=0, keepdims=True)
        d_res = norm_back(total, n1, r1, gb_ref[0:1, :])
        dp = d_res.astype(bf)
        da_ref[...] = nt_dot(dp, wo_ref[...]).astype(bf)
        for copy in fetched[7:]:
            copy.wait()
        cos = cos_ref[pl.ds(base, rows), :]
        sin = sin_ref[pl.ds(base, rows), :]
        m_a = head_lanes(rows, 256)
        lane = lax.broadcasted_iota(jnp.int32, (rows, 128), 1)
        ri = lax.broadcasted_iota(jnp.int32, (rows, rows), 0)
        ci = lax.broadcasted_iota(jnp.int32, (rows, rows), 1)
        tril = ci <= ri
        triu = ri <= ci
        diag = block_diag(256)
        ones = jnp.ones((rows, 128), bf)
        zero = jnp.zeros((), bf)
        for p in range(PAIRS):
            lanes = slice(128 * p, 128 * p + 128)
            wide = slice(256 * p, 256 * p + 256)
            d_o = da_ref[:, lanes]
            prod = d_o.astype(f32) * att_ref[:, lanes].astype(f32)
            in_a = jnp.sum(jnp.where(lane < 64, prod, 0.0), axis=1, keepdims=True)
            in_b = jnp.sum(jnp.where(lane < 64, 0.0, prod), axis=1, keepdims=True)
            inner = jnp.where(lane < 64, -in_a, -in_b)
            high = inner.astype(bf).astype(f32)
            ext = jnp.where((lane & 63) == 0, high, jnp.where((lane & 63) == 1, inner - high, 0.0)).astype(bf)
            left = jnp.concatenate([d_o, ext], axis=1)
            left_a, left_b = jnp.where(m_a, left, zero), jnp.where(m_a, zero, left)
            ve = jnp.concatenate([v_ref[:, lanes], ones], axis=1)
            qn = qn_ref[:, wide]
            kf = kf_ref[:, wide]
            qn_a, qn_b = jnp.where(m_a, qn, zero), jnp.where(m_a, zero, qn)
            kf_a, kf_b = jnp.where(m_a, kf, zero), jnp.where(m_a, zero, kf)
            pt = jnp.concatenate([jnp.where(triu, nt_dot(kf, qn_a), 0.0), jnp.where(triu, nt_dot(kf, qn_b), 0.0)], axis=1).astype(bf)
            gg = jnp.concatenate([jnp.where(tril, nt_dot(left_a, ve), 0.0), jnp.where(tril, nt_dot(left_b, ve), 0.0)], axis=1).astype(bf)
            gt = jnp.concatenate([jnp.where(triu, nt_dot(ve, left_a), 0.0), jnp.where(triu, nt_dot(ve, left_b), 0.0)], axis=1).astype(bf)
            after = t_out[p].astype(bf)
            dv = nn_dot(pt, jnp.concatenate([left_a[:, :128], left_b[:, :128]], axis=0)) + nn_dot(kf, after[:, :128])
            dq = nn_dot(gg, jnp.concatenate([kf_a, kf_b], axis=0)) + nt_dot(left, sb_ref[p])
            dk = nn_dot(gt, jnp.concatenate([qn_a, qn_b], axis=0)) + nt_dot(ve, after)
            t_out[p] = t_out[p] + jnp.where(diag, tn_dot(qn, left), 0.0)
            sq = sg_ref[:, lanes].astype(f32)
            sk = sg_ref[:, D + 128 * p:D + 128 * p + 128].astype(f32)
            dm_ref[:, lanes] = ((dq[:, :128] * cos + dq[:, 128:] * sin) * sq).astype(bf)
            dm_ref[:, D + 128 * p:D + 128 * p + 128] = ((dk[:, :128] * cos + dk[:, 128:] * sin) * sk).astype(bf)
            dm_ref[:, 2 * D + 128 * p:2 * D + 128 * p + 128] = dv.astype(bf)
        loaded(1)
        dm = dm_ref[...]
        for g in range(groups):
            odd = g & 1
            part, rest = 9 * g, 3 * g
            inner, outer = part + odd, rest + odd
            de_ref[:, g * D:g * D + 4 * 128] = dm[:, inner * 64:inner * 64 + 4 * 128]
            de_ref[:, g * D + 5 * 128:(g + 1) * D] = dp[:, outer * 64:outer * 64 + 128]
            one = dm[:, (part if odd else part + 8) // 2 * 128:][:, :128].astype(f32)
            two = dp[:, (rest if odd else rest + 2) // 2 * 128:][:, :128].astype(f32)
            if odd:
                one = pltpu.roll(one, 64, 1)
            else:
                two = pltpu.roll(two, 64, 1)
            de_ref[:, g * D + 4 * 128:g * D + 5 * 128] = jnp.where(lane < 64, one, two).astype(bf)
        for i in range(TILES):
            send.put(de_ref.at[:, i * TILE:(i + 1) * TILE], de_o.at[i, here, :])
        ds_ref[...] = (d_res + nt_dot(dm, wq_ref[...])).astype(bf)
        send.put(ds_ref, all_o.at[here, :])
        send.finish()


def backward_opening(delta, n, rows, stages, groups, *refs):
    t, meta, arr = refs[:3]
    cot, cot_v, load_sems, refs = refs[21], refs[29], refs[-1], refs[:-1]
    head, tail = pl.ds((n - 1) * rows, rows), pl.ds(0, (n - 1) * rows)
    loads = [pltpu.make_async_copy(cot.at[part, :], cot_v.at[part, :], load_sems.at[i]) for i, part in enumerate((head, tail))]
    for copy in loads:
        copy.start()
    backward_kernel(delta, n, rows, stages, groups, t, meta, cot_v, arr, *refs[4:11], None, None, *refs[11:21], *refs[22:29], *refs[37:], loads=loads)


def backward_next(delta, n, rows, stages, groups, *refs):
    t, meta, arr, cot = refs[:4]
    backward_kernel(delta, n, rows, stages, groups, t, meta, cot, arr, *refs[4:23], *refs[27:34], *refs[42:])


def backward_call(rows, n, delta, stages, groups, opening, limit=20):
    V = pl.BlockSpec(memory_space=pltpu.VMEM)
    S = pl.BlockSpec(memory_space=pltpu.SMEM)
    A = pl.BlockSpec(memory_space=pl.ANY)
    sd = jax.ShapeDtypeStruct
    every = n * rows
    made = [((rows, D), bf), ((rows, 4 * D), bf), ((rows, 4 * D), bf)]
    saved = [((rows, D), bf), ((rows, 128), f32), ((rows, 4 * D), bf), ((rows, D), bf), ((rows, D), bf), ((rows, D), bf),
             ((rows, 2 * D), bf), ((rows, 2 * D), bf), ((rows, 2 * D), bf), ((PAIRS, 256, 256), bf)]
    own = [((rows, 3 * D), bf), ((rows, D), bf), ((rows, D), bf)]
    big = [pltpu.HBM((every, D), bf), pltpu.HBM((TILES, every, TILE), bf), pltpu.HBM((TILES, every, TILE), bf), pltpu.HBM((every, D), bf)]
    if opening:
        aliases = {3 + i: 7 + i for i in range(8)}
    else:
        aliases = {**{3 + i: 7 + i for i in range(8)}, 11: 1, 12: 2, **{23 + i: 3 + i for i in range(4)}}
    return pl.pallas_call(
        functools.partial(backward_opening if opening else backward_next, delta, n, rows, stages, groups),
        in_specs=[S, S] + [V] * 9 + [A] * 11 if opening else [S, S] + [V] * 11 + [A] * 14,
        out_specs=[V] * 3 + [A] * 4 + [V] * 8,
        out_shape=[sd((rows, D), bf), sd((PAIRS, 256, 256), f32), sd((8, D), f32)] + big
        + [pltpu.VMEM(*item) for item in kept_items(every)],
        scratch_shapes=[pltpu.VMEM(*item) for item in made + own + saved] + [pltpu.SemaphoreType.DMA((30,)), pltpu.SemaphoreType.DMA((13,))]
        + [pltpu.SemaphoreType.DMA((2,))] * opening,
        input_output_aliases=aliases,
        cost_estimate=pl.CostEstimate(flops=rows * 2 * 10 * 10**6, bytes_accessed=4 * 2**20, transcendentals=0),
        compiler_params=pltpu.CompilerParams(vmem_limit_bytes=limit * 2**20),
        name="layer_backward",
    )


HALF = D // 2


def weight_kernel(groups, half, mixed, waits, fetch, meta_ref, left, *refs):
    raws, refs = refs[:1 + mixed], refs[1 + mixed + waits:]
    keep_o, send_o, refs = refs[0], refs[1], refs[2:]
    kept, (turned, out_buf, out_sem, *load_sems) = refs[:2 * fetch], refs[2 * fetch:]
    me = meta_ref[1]
    share = TILES // groups
    raw_copies, left_copies = [], []
    if fetch:
        left_v, raw_v = kept
        raw_copies = [pltpu.make_async_copy(raws[0].at[k:k + 256, :], raw_v.at[k:k + 256, :], load_sems[0].at[k // 256]) for k in range(0, raw_v.shape[0], 256)]
        left_copies = [pltpu.make_async_copy(left.at[i], left_v.at[i], load_sems[1].at[i]) for i in range(TILES)]
        for copy in raw_copies + left_copies:
            copy.start()
        left, raws = left_v, (raw_v,)
    for j, raw in enumerate(raws):
        for k in range(0, raw.shape[0], 256):
            if fetch:
                raw_copies[k // 256].wait()
            turned[j, :, k:k + 256] = raw[k:k + 256, half * HALF:(half + 1) * HALF].T
    for copy in left_copies:
        copy.wait()
    for g in range(groups):
        for i in range(share):
            cols = slice(i * TILE, (i + 1) * TILE)
            value = nn_dot(turned[0], left[g * share + i])
            if mixed and i == share - 1:
                other = nn_dot(turned[1], left[g * share + i])
                lane = lax.broadcasted_iota(jnp.int32, other.shape, 1)
                value = jnp.where(lane < 3 * D // groups - i * TILE, value, other)
            out_buf[g, :, cols] = value.astype(bf)
        rel = g ^ me

        @pl.when((rel & 1) == 0)
        def _():
            pltpu.make_async_copy(out_buf.at[g], keep_o.at[rel >> 1], out_sem).start()

        @pl.when((rel & 1) == 1)
        def _():
            pltpu.make_async_copy(out_buf.at[g], send_o.at[rel >> 1], out_sem).start()
    pltpu.make_async_copy(out_buf, out_buf, out_sem).wait()


def weight_call(every, groups, half, mixed, waits, fetch, limit=12):
    V = pl.BlockSpec(memory_space=pltpu.VMEM)
    S = pl.BlockSpec(memory_space=pltpu.SMEM)
    A = pl.BlockSpec(memory_space=pl.ANY)
    raws = 1 + mixed
    return pl.pallas_call(
        functools.partial(weight_kernel, groups, half, mixed, waits, fetch),
        in_specs=[S] + [A if fetch else V] * (1 + raws) + [A] * waits,
        out_specs=[A] * 2 + [V] * 2 * fetch,
        out_shape=[pltpu.HBM((2, HALF, D), bf)] * 2 + [pltpu.VMEM((TILES, every, TILE), bf), pltpu.VMEM((every, D), bf)] * fetch,
        scratch_shapes=[pltpu.VMEM((raws, HALF, every), bf), pltpu.VMEM((groups, HALF, D), bf), pltpu.SemaphoreType.DMA]
        + [pltpu.SemaphoreType.DMA((every // 256,)), pltpu.SemaphoreType.DMA((TILES,))] * fetch,
        cost_estimate=pl.CostEstimate(flops=2 * every * HALF * 4 * D, bytes_accessed=every * 5 * D * 2, transcendentals=0),
        compiler_params=pltpu.CompilerParams(vmem_limit_bytes=limit * 2**20),
        name="weight_grad",
    )


MB_ROWS = 1024
MICRO = 2
ROWS = 256
DELTA = 2


def geometry(doc_ids):
    quarter = MB_ROWS // 4
    marks = doc_ids.reshape(-1, MB_ROWS)[:, ::quarter]
    pieces = 1 + jnp.sum((marks[:, 1:] != marks[:, :-1]).astype(jnp.int32), axis=1)
    length = MB_ROWS // pieces
    row = jnp.arange(MB_ROWS, dtype=jnp.int32)
    position = row[None, :] % length[:, None]
    angle = (0.5 * math.pi) * position.astype(f32) / length[:, None].astype(f32)
    angle = angle.reshape(-1, 1)
    starts = jnp.arange(0, MB_ROWS, ROWS, dtype=jnp.int32)
    first = (starts[None, :] % length[:, None]) == 0
    last = ((starts[None, :] + ROWS) % length[:, None]) == 0
    wide = (angle.shape[0], 128)
    return (jnp.broadcast_to(jnp.cos(angle), wide), jnp.broadcast_to(jnp.sin(angle), wide),
            first.reshape(-1).astype(jnp.int32), last.reshape(-1).astype(jnp.int32))


def exchange(block, axis, flip):
    route = [(i, i ^ flip) for i in range(lax.axis_size(axis))]
    return lax.ppermute(block, axis, route)


def reduced(keep, send, wire):
    got = exchange(send, "group", 1)
    away = lax.optimization_barrier((keep[1].astype(f32) + got[1].astype(f32)).astype(wire))
    back = exchange(away, "group", 2)
    own = lax.optimization_barrier((keep[0].astype(f32) + got[0].astype(f32) + back.astype(f32)).astype(wire))
    if lax.axis_size("dp") == 2:
        return away, own, own.astype(f32) + exchange(own, "dp", 1).astype(f32)
    return away, own, lax.psum(own, "dp").astype(f32)


def local(tokens, doc_ids, cotangent, w_qkv, w_out, w_up, w_down,
          first_gain, first_bias, second_gain, second_bias):
    stages = lax.axis_size("pipe")
    groups = lax.axis_size("group")
    stage = lax.axis_index("pipe").astype(jnp.int32)
    me = lax.axis_index("group").astype(jnp.int32)
    n = tokens.shape[0] // ROWS
    ticks = n + DELTA * (stages - 1)
    cos, sin, first, last = geometry(doc_ids)
    meta = jnp.concatenate([stage[None], me[None], first, last])
    resident = far((tokens,)) + [cos, sin] + far((w_qkv[0], w_out[0], w_up[0], w_down[0]))
    gb = jnp.concatenate([first_gain, first_bias, second_gain, second_bias], axis=0)
    blank = jnp.zeros((ROWS, D), bf)
    arriving = [blank] * DELTA
    resident = resident + [gb]
    state, big = (), ()
    for t in range(ticks):
        made = forward_call(ROWS, n, DELTA, t == 0)(jnp.full((1,), t, jnp.int32), meta, arriving.pop(0), *resident, *state, *big)
        state, big, resident = made[1:2], made[2:16], made[16:]
        route = [(a, a + 1) for a in range(stages - 1) if 0 <= t - a * DELTA < n]
        arriving.append(lax.ppermute(made[0], "pipe", route) if route else made[0])
    block_out, x, att, hb, act, qn, kf, v, sg, n1, gp, n2, rs, sb = big
    arriving = [made[0]] * DELTA
    state, big = (), ()
    for t in range(ticks):
        made = backward_call(ROWS, n, DELTA, stages, groups, t == 0)(
            jnp.full((1,), t, jnp.int32), meta, arriving.pop(0), *resident, *state,
            *far((n2, rs, gp, n1, att, v, qn, kf, sg, sb)), *big, *far([cotangent] * (t == 0)))
        state, big, resident = made[1:3], made[3:7], made[7:]
        route = [(a, a - 1) for a in range(1, stages) if 0 <= t - (stages - 1 - a) * DELTA < n]
        arriving.append(lax.ppermute(made[0], "pipe", route) if route else made[0])
    df, du, de, input_grad = big
    aways, owns, parts = [], [], []
    for left, rights in ((act, (df,)), (de, (x, att)), (du, (hb,))):
        for half in range(2):
            waits = aways[-2:-1] + owns[-4:-3]
            fetch = not parts
            operands = far((left,) + rights) if fetch else (left,) + rights
            keep, send, *loaded = weight_call(n * ROWS, groups, half, len(rights) == 2, len(waits), fetch)(meta, *operands, *waits)
            if fetch:
                left, rights = loaded[0], tuple(loaded[1:])
            away, own, part = reduced(keep, send, bf)
            aways.append(away)
            owns.append(own)
            parts.append(part)
    vectors = state[1][:4].reshape(4, groups, D // groups).swapaxes(0, 1).reshape(groups, 1, D)
    ordered = [lax.dynamic_index_in_dim(vectors, me ^ rel, 0, keepdims=False) for rel in range(4)]
    mine = reduced(jnp.stack(ordered[0::2]), jnp.stack(ordered[1::2]), f32)[2].reshape(4, D // groups)
    g_down, g_mixed, g_up = (jnp.concatenate(parts[i:i + 2], axis=0) for i in (0, 2, 4))
    odd = (me & 1) == 1
    swap = lambda a, b: jnp.concatenate([g_mixed[:, a], g_mixed[:, b]], axis=1)
    low, one, two, high = slice(0, 512), slice(512, 576), slice(576, 640), slice(640, 768)
    g_qkv = jnp.where(odd, swap(one, low), swap(low, one))
    g_out = jnp.where(odd, swap(two, high), swap(high, two))
    return (block_out[None], input_grad[None], g_qkv[None], g_out[None], g_up[None], g_down.T[None],
            mine[0:1], mine[1:2], mine[2:3], mine[3:4])


def solution(mesh):
    rows = ("group", "dp")
    whole = P("pipe", None, None)
    vector = P("pipe", None)
    return jax.shard_map(
        local,
        mesh=mesh,
        in_specs=(P(rows, None), P(rows), P(rows, None)) + (whole,) * 4 + (vector,) * 4,
        out_specs=(P("pipe", rows, None), P("pipe", rows, None), P("pipe", None, "group"), P("pipe", None, "group"),
                   P("pipe", None, "group"), P("pipe", "group", None)) + (P("pipe", "group"),) * 4,
        check_vma=False,
    )
```

```python
import functools, math
import jax, jax.numpy as jnp
from jax import lax
from jax.experimental import pallas as pl
from jax.experimental.pallas import tpu as pltpu
from jax.sharding import PartitionSpec as P

bf = jnp.bfloat16
f32 = jnp.float32
EPS = 1e-05
D = 768
PAIRS = 6
TILE = 256
TILES = 4 * D // TILE
NT = (((1,), (1,)), ((), ()))
TN = (((0,), (0,)), ((), ()))


def nn_dot(a, b):
    return jnp.dot(a, b, preferred_element_type=f32)


def nt_dot(a, b):
    return lax.dot_general(a, b, NT, preferred_element_type=f32)


def tn_dot(a, b):
    return lax.dot_general(a, b, TN, preferred_element_type=f32)


def head_lanes(rows, lanes):
    lane = lax.broadcasted_iota(jnp.int32, (rows, lanes), 1)
    return (lane & 64) == 0


def block_diag(size):
    r = lax.broadcasted_iota(jnp.int32, (size, size), 0)
    c = lax.broadcasted_iota(jnp.int32, (size, size), 1)
    return ((r ^ c) & 64) == 0


def soft_pair(raw):
    e = jnp.exp(-jnp.abs(raw))
    one = 1.0 + e
    tail = jnp.where(e < 1e-3, e * (1.0 - e * (0.5 - e * (1.0 / 3.0))), jnp.log(one))
    soft = jnp.maximum(raw, 0.0) + tail
    sig = jnp.where(raw >= 0.0, 1.0, e) / one
    return soft, sig


def norm_rows(v):
    centre = jnp.mean(v, axis=-1, keepdims=True)
    centred = v - centre
    spread = jnp.mean(centred * centred, axis=-1, keepdims=True)
    rstd = lax.rsqrt(spread + EPS)
    return centred * rstd, rstd


class Sender:
    def __init__(self, sems):
        self.sems, self.copies = sems, []

    def put(self, src, dst):
        copy = pltpu.make_async_copy(src, dst, self.sems.at[len(self.copies)])
        copy.start()
        self.copies.append(copy)

    def finish(self):
        for copy in self.copies:
            copy.wait()


def forward_kernel(delta, n, rows,
                   t_ref, meta_ref, tok_ref, arr_ref, cos_ref, sin_ref,
                   wq_ref, wo_ref, wu_ref, wd_ref, gb_ref, s_in,
                   y_ref, s_out, all_o, x_o, att_o, hb_o, act_o, qn_o, kf_o, v_o, sg_o, n1_o, gp_o, n2_o, rs_o, sb_o,
                   x_ref, att_ref, hb_ref, act_ref, qn_ref, kf_ref, v_ref, sg_ref, n1_ref, gp_ref, n2_ref, rs_ref, sb_ref, sems, loads=()):
    stage = meta_ref[0]
    chunk = t_ref[0] - delta * stage
    valid = (chunk >= 0) & (chunk < n)

    def loaded(*which):
        for i in which:
            if loads:
                loads[i].wait()

    @pl.when(jnp.logical_not(valid))
    def _():
        loaded(*range(len(loads)))

    @pl.when(valid)
    def _():
        send = Sender(sems)
        base = pl.multiple_of(chunk * rows, rows)
        here = pl.ds(base, rows)
        first = meta_ref[2 + chunk] != 0
        loaded(0)

        @pl.when(stage == 0)
        def _():
            x_ref[...] = tok_ref[pl.ds(base, rows), :]

        @pl.when(stage != 0)
        def _():
            x_ref[...] = arr_ref[...]

        @pl.when(first)
        def _():
            s_out[...] = jnp.zeros_like(s_out)

        if s_in is not None:
            @pl.when(jnp.logical_not(first))
            def _():
                s_out[...] = s_in[...]

        send.put(x_ref, x_o.at[here, :])
        x = x_ref[...]
        cos = cos_ref[pl.ds(base, rows), :]
        sin = sin_ref[pl.ds(base, rows), :]
        loaded(1)
        q_raw = nn_dot(x, wq_ref[:, 0:D])
        k_raw = nn_dot(x, wq_ref[:, D:2 * D])
        v_ref[...] = nn_dot(x, wq_ref[:, 2 * D:]).astype(bf)
        send.put(v_ref, v_o.at[here, :])
        m_a = head_lanes(rows, 256)
        ri = lax.broadcasted_iota(jnp.int32, (rows, rows), 0)
        ci = lax.broadcasted_iota(jnp.int32, (rows, rows), 1)
        tril = ci <= ri
        diag = block_diag(256)
        ones = jnp.ones((rows, 128), bf)
        zero = jnp.zeros((), bf)
        for p in range(PAIRS):
            lanes = slice(128 * p, 128 * p + 128)
            wide = slice(256 * p, 256 * p + 256)
            q, sq = soft_pair(q_raw[:, lanes])
            k, sk = soft_pair(k_raw[:, lanes])
            qc, qs = q * cos, q * sin
            qf = jnp.concatenate([qc, qs], axis=1).astype(bf)
            kf = jnp.concatenate([k * cos, k * sin], axis=1).astype(bf)
            kf_ref[:, wide] = kf
            sg_ref[:, D + 128 * p:D + 128 * p + 128] = sk.astype(bf)
            ve = jnp.concatenate([v_ref[:, lanes], ones], axis=1)
            s_a = nt_dot(jnp.where(m_a, qf, zero), kf)
            s_b = nt_dot(jnp.where(m_a, zero, qf), kf)
            p_ab = jnp.concatenate([jnp.where(tril, s_a, 0.0), jnp.where(tril, s_b, 0.0)], axis=1).astype(bf)
            ve2 = jnp.concatenate([jnp.where(m_a, ve, zero), jnp.where(m_a, zero, ve)], axis=0)
            before = s_out[p].astype(bf)
            sb_ref[p] = before
            nd = nn_dot(p_ab, ve2) + nn_dot(qf, before)
            inv = 1.0 / nd[:, 128:]
            att_ref[:, lanes] = (nd[:, :128] * inv).astype(bf)
            qn_ref[:, wide] = jnp.concatenate([qc * inv, qs * inv], axis=1).astype(bf)
            sg_ref[:, lanes] = (sq * inv).astype(bf)
            s_out[p] = s_out[p] + jnp.where(diag, tn_dot(kf, ve), 0.0)
        send.put(kf_ref, kf_o.at[here, :])
        send.put(att_ref, att_o.at[here, :])
        send.put(qn_ref, qn_o.at[here, :])
        send.put(sg_ref, sg_o.at[here, :])
        send.put(sb_ref, sb_o.at[chunk])
        loaded(2)
        residual = x.astype(f32) + nn_dot(att_ref[...], wo_ref[...])
        n1, r1 = norm_rows(residual)
        n1_ref[...] = n1.astype(bf)
        hidden = n1 * gb_ref[0:1, :] + gb_ref[1:2, :]
        hb = hidden.astype(bf)
        hb_ref[...] = hb
        send.put(n1_ref, n1_o.at[here, :])
        send.put(hb_ref, hb_o.at[here, :])
        total = hidden
        loaded(3, 4)
        FB = 768
        for j in range(0, 4 * D, FB):
            cols = slice(j, j + FB)
            u = nn_dot(hb, wu_ref[:, cols])
            cdf = 0.5 + 0.5 * lax.erf(u * (1.0 / math.sqrt(2.0)))
            act = (u * cdf).astype(bf)
            act_ref[:, cols] = act
            gp_ref[:, cols] = (cdf + u * (jnp.exp(-0.5 * u * u) * (1.0 / math.sqrt(2.0 * math.pi)))).astype(bf)
            for i in range(j // TILE, (j + FB) // TILE):
                send.put(act_ref.at[:, i * TILE:(i + 1) * TILE], act_o.at[i, here, :])
            send.put(gp_ref.at[:, cols], gp_o.at[here, cols])
            total = total + nn_dot(act, wd_ref[cols, :])
        n2, r2 = norm_rows(total)
        n2_ref[...] = n2.astype(bf)
        lane = lax.broadcasted_iota(jnp.int32, (rows, 128), 1)
        rs_ref[...] = jnp.where(lane < 64, r1, r2)
        send.put(n2_ref, n2_o.at[here, :])
        send.put(rs_ref, rs_o.at[here, :])
        y_ref[...] = (n2 * gb_ref[2:3, :] + gb_ref[3:4, :]).astype(bf)
        send.put(y_ref, all_o.at[here, :])
        loaded(5)
        send.finish()


def far(items):
    return [pltpu.with_memory_space_constraint(item, pltpu.HBM) for item in items]


def near(items):
    return [pltpu.with_memory_space_constraint(item, pltpu.VMEM) for item in items]


def forward_opening(delta, n, rows, *refs):
    ins, refs = refs[:11], refs[11:]
    outs, kept, scratch, load_sems = refs[:16], refs[16:25], refs[25:-1], refs[-1]
    tok, cos, sin, *weights, gb = ins[3:]
    tok_v, _, _, *weights_v = kept[:7]
    head, tail = pl.ds(0, rows), pl.ds(rows, (n - 1) * rows)
    pairs = [(tok.at[head, :], tok_v.at[head, :])] + list(zip(weights, weights_v)) + [(tok.at[tail, :], tok_v.at[tail, :])]
    loads = [pltpu.make_async_copy(src, dst, load_sems.at[i]) for i, (src, dst) in enumerate(pairs)]
    for copy in loads:
        copy.start()
    forward_kernel(delta, n, rows, *ins[:2], tok_v, ins[2], cos, sin, *weights_v, gb, None, *outs, *scratch, loads=loads)


def forward_next(delta, n, rows, *refs):
    t, meta, arr, tok, cos, sin, wq, wo, wu, wd, gb, _, s_in = refs[:13]
    forward_kernel(delta, n, rows, t, meta, tok, arr, cos, sin, wq, wo, wu, wd, gb, s_in, *refs[27:43], *refs[52:])


def saved_items(rows):
    return [((rows, D), bf)] * 3 + [((rows, 4 * D), bf), ((rows, 2 * D), bf), ((rows, 2 * D), bf), ((rows, D), bf), ((rows, 2 * D), bf),
                                    ((rows, D), bf), ((rows, 4 * D), bf), ((rows, D), bf), ((rows, 128), f32), ((PAIRS, 256, 256), bf)]


def kept_items(every):
    return [((every, D), bf), ((every, 128), f32), ((every, 128), f32), ((D, 3 * D), bf), ((D, D), bf), ((D, 4 * D), bf), ((4 * D, D), bf),
            ((4, D), f32), ((TILES, every, TILE), bf)]


def forward_call(rows, n, delta, opening, limit=19):
    V = pl.BlockSpec(memory_space=pltpu.VMEM)
    S = pl.BlockSpec(memory_space=pltpu.SMEM)
    A = pl.BlockSpec(memory_space=pl.ANY)
    sd = jax.ShapeDtypeStruct
    every = n * rows
    big = [pltpu.HBM((every, D), bf)] + [pltpu.HBM(*item) for item in saved_items(every)]
    big[4] = pltpu.HBM((TILES, every, TILE), bf)
    big[13] = pltpu.HBM((n, PAIRS, 256, 256), bf)
    aliases = {4: 17, 5: 18, 10: 23}
    if not opening:
        aliases = {12: 1, **{13 + i: 2 + i for i in range(14)}, **{3 + i: 16 + i for i in range(9)}}
    return pl.pallas_call(
        functools.partial(forward_opening if opening else forward_next, delta, n, rows),
        in_specs=[S, S, V, A, V, V, A, A, A, A, V] if opening else [S, S] + [V] * 11 + [A] * 14,
        out_specs=[V, V] + [A] * 14 + [V] * 9,
        out_shape=[sd((rows, D), bf), sd((PAIRS, 256, 256), f32)] + big + [pltpu.VMEM(*item) for item in kept_items(every)],
        scratch_shapes=[pltpu.VMEM(*item) for item in saved_items(rows)] + [pltpu.SemaphoreType.DMA((30,))] + [pltpu.SemaphoreType.DMA((6,))] * opening,
        input_output_aliases=aliases,
        cost_estimate=pl.CostEstimate(flops=rows * 2 * 9 * 10**6, bytes_accessed=4 * 2**20, transcendentals=0),
        compiler_params=pltpu.CompilerParams(vmem_limit_bytes=limit * 2**20),
        name="layer_forward",
    )


def norm_back(grad, normed, rstd, gain):
    scaled = grad * gain
    mean_one = jnp.mean(scaled, axis=-1, keepdims=True)
    mean_two = jnp.mean(scaled * normed, axis=-1, keepdims=True)
    return rstd * (scaled - mean_one - normed * mean_two)


def backward_kernel(delta, n, rows, stages, groups,
                    t_ref, meta_ref, cot_ref, arr_ref, cos_ref, sin_ref,
                    wq_ref, wo_ref, wu_ref, wd_ref, gb_ref, t_in, ga_in,
                    n2_i, rs_i, gp_i, n1_i, att_i, v_i, qn_i, kf_i, sg_i, sb_i,
                    ds_ref, t_out, ga_out, df_o, du_o, de_o, all_o,
                    df_ref, du_ref, de_ref, dm_ref, da_ref, g_ref,
                    n2_ref, rs_ref, gp_ref, n1_ref, att_ref, v_ref, qn_ref, kf_ref, sg_ref, sb_ref, sems, fetch_sems, loads=()):
    stage = meta_ref[0]
    chunk = n - 1 - t_ref[0] + delta * (stages - 1 - stage)
    valid = (chunk >= 0) & (chunk < n)

    def loaded(*which):
        for i in which:
            if loads:
                loads[i].wait()

    @pl.when(jnp.logical_not(valid))
    def _():
        loaded(*range(len(loads)))

    @pl.when(valid)
    def _():
        base = pl.multiple_of(chunk * rows, rows)
        here = pl.ds(base, rows)
        fetched = []
        quarters = [slice(j, j + D) for j in range(0, 4 * D, D)]
        pairs = [(n2_i.at[here, :], n2_ref), (rs_i.at[here, :], rs_ref)] + [(gp_i.at[here, cols], gp_ref.at[:, cols]) for cols in quarters]
        pairs += [(src.at[here, :], dst) for src, dst in ((n1_i, n1_ref), (att_i, att_ref), (v_i, v_ref), (qn_i, qn_ref), (kf_i, kf_ref), (sg_i, sg_ref))]
        pairs += [(sb_i.at[chunk], sb_ref)]
        for i, (src, dst) in enumerate(pairs):
            copy = pltpu.make_async_copy(src, dst, fetch_sems.at[i])
            copy.start()
            fetched.append(copy)
        send = Sender(sems)
        last = meta_ref[2 + n + chunk] != 0

        loaded(0)

        if cot_ref is None:
            g_ref[...] = arr_ref[...]
        else:
            @pl.when(stage == stages - 1)
            def _():
                g_ref[...] = cot_ref[pl.ds(base, rows), :]

            @pl.when(stage != stages - 1)
            def _():
                g_ref[...] = arr_ref[...]

        @pl.when(last)
        def _():
            t_out[...] = jnp.zeros_like(t_out)

        if t_in is not None:
            @pl.when(jnp.logical_not(last))
            def _():
                t_out[...] = t_in[...]

        @pl.when(chunk == n - 1)
        def _():
            ga_out[...] = jnp.zeros_like(ga_out)

        if ga_in is not None:
            @pl.when(chunk != n - 1)
            def _():
                ga_out[...] = ga_in[...]

        g = g_ref[...].astype(f32)
        fetched[0].wait()
        fetched[1].wait()
        n2 = n2_ref[...].astype(f32)
        r1 = rs_ref[:, 0:1]
        r2 = rs_ref[:, 64:65]
        ga_out[2:3, :] += jnp.sum(g * n2, axis=0, keepdims=True)
        ga_out[3:4, :] += jnp.sum(g, axis=0, keepdims=True)
        d_two = norm_back(g, n2, r2, gb_ref[2:3, :])
        df = d_two.astype(bf)
        df_ref[...] = df
        send.put(df_ref, df_o.at[here, :])
        total = d_two
        for cols, copy in zip(quarters, fetched[2:6]):
            copy.wait()
            du = (nt_dot(df, wd_ref[cols, :]) * gp_ref[:, cols].astype(f32)).astype(bf)
            du_ref[:, cols] = du
            for i in range(cols.start // TILE, cols.stop // TILE):
                send.put(du_ref.at[:, i * TILE:(i + 1) * TILE], du_o.at[i, here, :])
            total = total + nt_dot(du, wu_ref[:, cols])
        fetched[6].wait()
        n1 = n1_ref[...].astype(f32)
        ga_out[0:1, :] += jnp.sum(total * n1, axis=0, keepdims=True)
        ga_out[1:2, :] += jnp.sum(total, axis=0, keepdims=True)
        d_res = norm_back(total, n1, r1, gb_ref[0:1, :])
        dp = d_res.astype(bf)
        da_ref[...] = nt_dot(dp, wo_ref[...]).astype(bf)
        for copy in fetched[7:]:
            copy.wait()
        cos = cos_ref[pl.ds(base, rows), :]
        sin = sin_ref[pl.ds(base, rows), :]
        m_a = head_lanes(rows, 256)
        lane = lax.broadcasted_iota(jnp.int32, (rows, 128), 1)
        ri = lax.broadcasted_iota(jnp.int32, (rows, rows), 0)
        ci = lax.broadcasted_iota(jnp.int32, (rows, rows), 1)
        tril = ci <= ri
        triu = ri <= ci
        diag = block_diag(256)
        ones = jnp.ones((rows, 128), bf)
        zero = jnp.zeros((), bf)
        for p in range(PAIRS):
            lanes = slice(128 * p, 128 * p + 128)
            wide = slice(256 * p, 256 * p + 256)
            d_o = da_ref[:, lanes]
            prod = d_o.astype(f32) * att_ref[:, lanes].astype(f32)
            in_a = jnp.sum(jnp.where(lane < 64, prod, 0.0), axis=1, keepdims=True)
            in_b = jnp.sum(jnp.where(lane < 64, 0.0, prod), axis=1, keepdims=True)
            inner = jnp.where(lane < 64, -in_a, -in_b)
            high = inner.astype(bf).astype(f32)
            ext = jnp.where((lane & 63) == 0, high, jnp.where((lane & 63) == 1, inner - high, 0.0)).astype(bf)
            left = jnp.concatenate([d_o, ext], axis=1)
            left_a, left_b = jnp.where(m_a, left, zero), jnp.where(m_a, zero, left)
            ve = jnp.concatenate([v_ref[:, lanes], ones], axis=1)
            qn = qn_ref[:, wide]
            kf = kf_ref[:, wide]
            qn_a, qn_b = jnp.where(m_a, qn, zero), jnp.where(m_a, zero, qn)
            kf_a, kf_b = jnp.where(m_a, kf, zero), jnp.where(m_a, zero, kf)
            pt = jnp.concatenate([jnp.where(triu, nt_dot(kf, qn_a), 0.0), jnp.where(triu, nt_dot(kf, qn_b), 0.0)], axis=1).astype(bf)
            gg = jnp.concatenate([jnp.where(tril, nt_dot(left_a, ve), 0.0), jnp.where(tril, nt_dot(left_b, ve), 0.0)], axis=1).astype(bf)
            gt = jnp.concatenate([jnp.where(triu, nt_dot(ve, left_a), 0.0), jnp.where(triu, nt_dot(ve, left_b), 0.0)], axis=1).astype(bf)
            after = t_out[p].astype(bf)
            dv = nn_dot(pt, jnp.concatenate([left_a[:, :128], left_b[:, :128]], axis=0)) + nn_dot(kf, after[:, :128])
            dq = nn_dot(gg, jnp.concatenate([kf_a, kf_b], axis=0)) + nt_dot(left, sb_ref[p])
            dk = nn_dot(gt, jnp.concatenate([qn_a, qn_b], axis=0)) + nt_dot(ve, after)
            t_out[p] = t_out[p] + jnp.where(diag, tn_dot(qn, left), 0.0)
            sq = sg_ref[:, lanes].astype(f32)
            sk = sg_ref[:, D + 128 * p:D + 128 * p + 128].astype(f32)
            dm_ref[:, lanes] = ((dq[:, :128] * cos + dq[:, 128:] * sin) * sq).astype(bf)
            dm_ref[:, D + 128 * p:D + 128 * p + 128] = ((dk[:, :128] * cos + dk[:, 128:] * sin) * sk).astype(bf)
            dm_ref[:, 2 * D + 128 * p:2 * D + 128 * p + 128] = dv.astype(bf)
        loaded(1)
        dm = dm_ref[...]
        for g in range(groups):
            odd = g & 1
            part, rest = 9 * g, 3 * g
            inner, outer = part + odd, rest + odd
            de_ref[:, g * D:g * D + 4 * 128] = dm[:, inner * 64:inner * 64 + 4 * 128]
            de_ref[:, g * D + 5 * 128:(g + 1) * D] = dp[:, outer * 64:outer * 64 + 128]
            one = dm[:, (part if odd else part + 8) // 2 * 128:][:, :128].astype(f32)
            two = dp[:, (rest if odd else rest + 2) // 2 * 128:][:, :128].astype(f32)
            if odd:
                one = pltpu.roll(one, 64, 1)
            else:
                two = pltpu.roll(two, 64, 1)
            de_ref[:, g * D + 4 * 128:g * D + 5 * 128] = jnp.where(lane < 64, one, two).astype(bf)
        for i in range(TILES):
            send.put(de_ref.at[:, i * TILE:(i + 1) * TILE], de_o.at[i, here, :])
        ds_ref[...] = (d_res + nt_dot(dm, wq_ref[...])).astype(bf)
        send.put(ds_ref, all_o.at[here, :])
        send.finish()


def backward_opening(delta, n, rows, stages, groups, *refs):
    t, meta, arr = refs[:3]
    cot, cot_v, load_sems, refs = refs[22], refs[30], refs[-1], refs[:-1]
    head, tail = pl.ds((n - 1) * rows, rows), pl.ds(0, (n - 1) * rows)
    loads = [pltpu.make_async_copy(cot.at[part, :], cot_v.at[part, :], load_sems.at[i]) for i, part in enumerate((head, tail))]
    for copy in loads:
        copy.start()
    backward_kernel(delta, n, rows, stages, groups, t, meta, cot_v, arr, *refs[4:11], None, None, *refs[12:22], *refs[23:30], *refs[39:], loads=loads)


def backward_next(delta, n, rows, stages, groups, *refs):
    t, meta, arr, cot = refs[:4]
    act, act_v, sem, refs = refs[28], refs[44], refs[-1], refs[:-1]
    fill = (t[0] >= 1) & (t[0] <= TILES)
    tile = jnp.clip(t[0] - 1, 0, TILES - 1)
    copy = pltpu.make_async_copy(act.at[tile], act_v.at[tile], sem)

    @pl.when(fill)
    def _():
        copy.start()

    backward_kernel(delta, n, rows, stages, groups, t, meta, cot, arr, *refs[4:11], *refs[12:24], *refs[29:36], *refs[45:])

    @pl.when(fill)
    def _():
        copy.wait()


def backward_call(rows, n, delta, stages, groups, opening, limit=19):
    V = pl.BlockSpec(memory_space=pltpu.VMEM)
    S = pl.BlockSpec(memory_space=pltpu.SMEM)
    A = pl.BlockSpec(memory_space=pl.ANY)
    sd = jax.ShapeDtypeStruct
    every = n * rows
    made = [((rows, D), bf), ((rows, 4 * D), bf), ((rows, 4 * D), bf)]
    saved = [((rows, D), bf), ((rows, 128), f32), ((rows, 4 * D), bf), ((rows, D), bf), ((rows, D), bf), ((rows, D), bf),
             ((rows, 2 * D), bf), ((rows, 2 * D), bf), ((rows, 2 * D), bf), ((PAIRS, 256, 256), bf)]
    own = [((rows, 3 * D), bf), ((rows, D), bf), ((rows, D), bf)]
    big = [pltpu.HBM((every, D), bf), pltpu.HBM((TILES, every, TILE), bf), pltpu.HBM((TILES, every, TILE), bf), pltpu.HBM((every, D), bf)]
    if opening:
        aliases = {3 + i: 7 + i for i in range(9)}
    else:
        aliases = {**{3 + i: 7 + i for i in range(9)}, 12: 1, 13: 2, **{24 + i: 3 + i for i in range(4)}}
    return pl.pallas_call(
        functools.partial(backward_opening if opening else backward_next, delta, n, rows, stages, groups),
        in_specs=[S, S] + [V] * 10 + [A] * 11 if opening else [S, S] + [V] * 12 + [A] * 15,
        out_specs=[V] * 3 + [A] * 4 + [V] * 9,
        out_shape=[sd((rows, D), bf), sd((PAIRS, 256, 256), f32), sd((8, D), f32)] + big
        + [pltpu.VMEM(*item) for item in kept_items(every)],
        scratch_shapes=[pltpu.VMEM(*item) for item in made + own + saved] + [pltpu.SemaphoreType.DMA((30,)), pltpu.SemaphoreType.DMA((13,))]
        + [pltpu.SemaphoreType.DMA((2,)) if opening else pltpu.SemaphoreType.DMA],
        input_output_aliases=aliases,
        cost_estimate=pl.CostEstimate(flops=rows * 2 * 10 * 10**6, bytes_accessed=4 * 2**20, transcendentals=0),
        compiler_params=pltpu.CompilerParams(vmem_limit_bytes=limit * 2**20),
        name="layer_backward",
    )


HALF = D // 2


def weight_kernel(groups, half, mixed, waits, fetch, ahead, meta_ref, left, *refs):
    raws, refs = refs[:1 + mixed], refs[1 + mixed + waits:]
    sources, refs = refs[:ahead], refs[ahead:]
    keep_o, send_o, refs = refs[0], refs[1], refs[2:]
    kept, refs = refs[:fetch], refs[fetch:]
    targets, refs = refs[:ahead], refs[ahead:]
    turned, out_buf, out_sem, raw_sem, ahead_sem = refs
    me = meta_ref[1]
    share = TILES // groups
    every = raws[0].shape[0]
    raw_copies, later = [], []
    if fetch:
        raw_copies = [pltpu.make_async_copy(raws[0].at[k:k + 256, :], kept[0].at[k:k + 256, :], raw_sem.at[k // 256]) for k in range(0, every, 256)]
        raws = kept
    for source, target in zip(sources, targets):
        step = 1 if len(source.shape) == 3 else every // 4
        for k in range(0, source.shape[0], step):
            later.append(pltpu.make_async_copy(source.at[k:k + step], target.at[k:k + step], ahead_sem.at[len(later)]))
    for copy in raw_copies + later:
        copy.start()
    for j, raw in enumerate(raws):
        for k in range(0, every, 256):
            if fetch:
                raw_copies[k // 256].wait()
            turned[j, :, k:k + 256] = raw[k:k + 256, half * HALF:(half + 1) * HALF].T
    for g in range(groups):
        for i in range(share):
            cols = slice(i * TILE, (i + 1) * TILE)
            value = nn_dot(turned[0], left[g * share + i])
            if mixed and i == share - 1:
                other = nn_dot(turned[1], left[g * share + i])
                lane = lax.broadcasted_iota(jnp.int32, other.shape, 1)
                value = jnp.where(lane < 3 * D // groups - i * TILE, value, other)
            out_buf[g, :, cols] = value.astype(bf)
        rel = g ^ me

        @pl.when((rel & 1) == 0)
        def _():
            pltpu.make_async_copy(out_buf.at[g], keep_o.at[rel >> 1], out_sem).start()

        @pl.when((rel & 1) == 1)
        def _():
            pltpu.make_async_copy(out_buf.at[g], send_o.at[rel >> 1], out_sem).start()
    pltpu.make_async_copy(out_buf, out_buf, out_sem).wait()
    for copy in later:
        copy.wait()


def weight_call(every, groups, half, mixed, waits, fetch, ahead, limit=12):
    V = pl.BlockSpec(memory_space=pltpu.VMEM)
    S = pl.BlockSpec(memory_space=pltpu.SMEM)
    A = pl.BlockSpec(memory_space=pl.ANY)
    raws = 1 + mixed
    return pl.pallas_call(
        functools.partial(weight_kernel, groups, half, mixed, waits, fetch, len(ahead)),
        in_specs=[S, V] + [A if fetch else V] * raws + [A] * (waits + len(ahead)),
        out_specs=[A] * 2 + [V] * (fetch + len(ahead)),
        out_shape=[pltpu.HBM((2, HALF, D), bf)] * 2 + [pltpu.VMEM((every, D), bf)] * fetch + [pltpu.VMEM(shape, bf) for shape in ahead],
        scratch_shapes=[pltpu.VMEM((raws, HALF, every), bf), pltpu.VMEM((groups, HALF, D), bf), pltpu.SemaphoreType.DMA,
                        pltpu.SemaphoreType.DMA((every // 256,)), pltpu.SemaphoreType.DMA((24,))],
        cost_estimate=pl.CostEstimate(flops=2 * every * HALF * 4 * D, bytes_accessed=every * 5 * D * 2, transcendentals=0),
        compiler_params=pltpu.CompilerParams(vmem_limit_bytes=limit * 2**20),
        name="weight_grad",
    )


MB_ROWS = 1024
MICRO = 2
ROWS = 256
DELTA = 2


def geometry(doc_ids):
    quarter = MB_ROWS // 4
    marks = doc_ids.reshape(-1, MB_ROWS)[:, ::quarter]
    pieces = 1 + jnp.sum((marks[:, 1:] != marks[:, :-1]).astype(jnp.int32), axis=1)
    length = MB_ROWS // pieces
    row = jnp.arange(MB_ROWS, dtype=jnp.int32)
    position = row[None, :] % length[:, None]
    angle = (0.5 * math.pi) * position.astype(f32) / length[:, None].astype(f32)
    angle = angle.reshape(-1, 1)
    starts = jnp.arange(0, MB_ROWS, ROWS, dtype=jnp.int32)
    first = (starts[None, :] % length[:, None]) == 0
    last = ((starts[None, :] + ROWS) % length[:, None]) == 0
    wide = (angle.shape[0], 128)
    return (jnp.broadcast_to(jnp.cos(angle), wide), jnp.broadcast_to(jnp.sin(angle), wide),
            first.reshape(-1).astype(jnp.int32), last.reshape(-1).astype(jnp.int32))


def exchange(block, axis, flip):
    route = [(i, i ^ flip) for i in range(lax.axis_size(axis))]
    return lax.ppermute(block, axis, route)


def add_kernel(*refs):
    total = sum(ref[...].reshape(refs[-1].shape).astype(f32) for ref in refs[:-1])
    refs[-1][...] = total.astype(refs[-1].dtype)


def add_call(slot, keep, got, *more, limit=12):
    rows, columns = keep.shape[1:]
    step = min(rows, 192)
    pick = pl.BlockSpec((1, step, columns), lambda i: (slot, i, 0))
    flat = pl.BlockSpec((step, columns), lambda i: (i, 0))
    return pl.pallas_call(
        add_kernel,
        grid=(rows // step,),
        in_specs=[pick, pick] + [flat] * len(more),
        out_specs=flat,
        out_shape=jax.ShapeDtypeStruct((rows, columns), keep.dtype),
        cost_estimate=pl.CostEstimate(flops=rows * columns * 2, bytes_accessed=rows * columns * 6, transcendentals=0),
        compiler_params=pltpu.CompilerParams(vmem_limit_bytes=limit * 2**20),
        name="add_parts",
    )(keep, got, *more)


def reduced(keep, send, before):
    got = exchange(send, "group", 1)
    away = add_call(1, keep, got)
    if before:
        before[0], away = lax.optimization_barrier((before[0], away))
    back = exchange(away, "group", 2)
    return [back, keep, got, away]


def spread(own, before):
    if lax.axis_size("dp") != 2:
        return lax.psum(own, "dp")
    if before:
        before[-1], own = lax.optimization_barrier((before[-1], own))
    return exchange(own, "dp", 1)


def finished(own, other):
    if lax.axis_size("dp") == 2:
        return own.astype(f32) + other.astype(f32)
    return other.astype(f32)


def local(tokens, doc_ids, cotangent, w_qkv, w_out, w_up, w_down,
          first_gain, first_bias, second_gain, second_bias):
    stages = lax.axis_size("pipe")
    groups = lax.axis_size("group")
    stage = lax.axis_index("pipe").astype(jnp.int32)
    me = lax.axis_index("group").astype(jnp.int32)
    n = tokens.shape[0] // ROWS
    ticks = n + DELTA * (stages - 1)
    cos, sin, first, last = geometry(doc_ids)
    meta = jnp.concatenate([stage[None], me[None], first, last])
    resident = far((tokens,)) + [cos, sin] + far((w_qkv[0], w_out[0], w_up[0], w_down[0]))
    gb = jnp.concatenate([first_gain, first_bias, second_gain, second_bias], axis=0)
    blank = jnp.zeros((ROWS, D), bf)
    arriving = [blank] * DELTA
    resident = resident + [gb]
    state, big = (), ()
    for t in range(ticks):
        made = forward_call(ROWS, n, DELTA, t == 0)(jnp.full((1,), t, jnp.int32), meta, arriving.pop(0), *resident, *state, *big)
        state, big, resident = made[1:2], made[2:16], made[16:]
        route = [(a, a + 1) for a in range(stages - 1) if 0 <= t - a * DELTA < n]
        arriving.append(lax.ppermute(made[0], "pipe", route) if route else made[0])
    block_out, x, att, hb, act, qn, kf, v, sg, n1, gp, n2, rs, sb = big
    arriving = [made[0]] * DELTA
    state, big = (), ()
    for t in range(ticks):
        made = backward_call(ROWS, n, DELTA, stages, groups, t == 0)(
            jnp.full((1,), t, jnp.int32), meta, arriving.pop(0), *resident, *state,
            *far((n2, rs, gp, n1, att, v, qn, kf, sg, sb)), *big, *far([act if t > 0 else cotangent]))
        state, big, resident = made[1:3], made[3:7], made[7:]
        route = [(a, a - 1) for a in range(1, stages) if 0 <= t - (stages - 1 - a) * DELTA < n]
        arriving.append(lax.ppermute(made[0], "pipe", route) if route else made[0])
    df, du, de, input_grad = big
    act = resident[8]
    pieces = [(act, df), (de, x, att), (du, hb)]
    waiting, owns, others, keeps = [], [], [], []
    for piece in range(3):
        left, *rights = pieces[piece]
        for half in range(2):
            fetch = not keeps
            ready = {2: 1, 4: 2, 5: 3}.get(len(keeps))
            waits = [] if ready is None else [waiting[ready][3]]
            call = weight_call(n * ROWS, groups, half, len(rights) == 2, len(waits), fetch, [])
            keep, send, *loads = call(meta, left, *(far(rights) if fetch else rights), *waits)
            rights = loads if fetch else rights
            keeps.append(keep)
            waiting.append(reduced(keep, send, waiting[-1] if waiting else None))
    for back, keep, got, _ in waiting:
        own = add_call(0, keep, got, back)
        other = spread(own, others)
        owns.append(own)
        others.append(other)
    parts = [finished(*pair) for pair in zip(owns, others)]
    vectors, me, _ = lax.optimization_barrier((state[1], me, owns[3]))
    vectors = vectors[:4].reshape(4, groups, D // groups).swapaxes(0, 1).reshape(groups, 1, D)
    ordered = [lax.dynamic_index_in_dim(vectors, me ^ rel, 0, keepdims=False) for rel in range(4)]
    small = reduced(jnp.stack(ordered[0::2]), jnp.stack(ordered[1::2]), None)
    own = add_call(0, *small[1:3], small[0])
    mine = finished(own, spread(own, [])).reshape(4, D // groups)
    g_down, g_mixed, g_up = (jnp.concatenate(parts[i:i + 2], axis=0) for i in (0, 2, 4))
    odd = (me & 1) == 1
    swap = lambda a, b: jnp.concatenate([g_mixed[:, a], g_mixed[:, b]], axis=1)
    low, one, two, high = slice(0, 512), slice(512, 576), slice(576, 640), slice(640, 768)
    g_qkv = jnp.where(odd, swap(one, low), swap(low, one))
    g_out = jnp.where(odd, swap(two, high), swap(high, two))
    return (block_out[None], input_grad[None], g_qkv[None], g_out[None], g_up[None], g_down.T[None],
            mine[0:1], mine[1:2], mine[2:3], mine[3:4])


def solution(mesh):
    rows = ("group", "dp")
    whole = P("pipe", None, None)
    vector = P("pipe", None)
    return jax.shard_map(
        local,
        mesh=mesh,
        in_specs=(P(rows, None), P(rows), P(rows, None)) + (whole,) * 4 + (vector,) * 4,
        out_specs=(P("pipe", rows, None), P("pipe", rows, None), P("pipe", None, "group"), P("pipe", None, "group"),
                   P("pipe", None, "group"), P("pipe", "group", None)) + (P("pipe", "group"),) * 4,
        check_vma=False,
    )
```

```python
import functools, math
import jax, jax.numpy as jnp
from jax import lax
from jax.experimental import pallas as pl
from jax.experimental.pallas import tpu as pltpu
from jax.sharding import PartitionSpec as P

bf = jnp.bfloat16
f32 = jnp.float32
EPS = 1e-05
D = 768
PAIRS = 6
TILE = 256
TILES = 4 * D // TILE
NT = (((1,), (1,)), ((), ()))
TN = (((0,), (0,)), ((), ()))


def nn_dot(a, b):
    return jnp.dot(a, b, preferred_element_type=f32)


def nt_dot(a, b):
    return lax.dot_general(a, b, NT, preferred_element_type=f32)


def tn_dot(a, b):
    return lax.dot_general(a, b, TN, preferred_element_type=f32)


def head_lanes(rows, lanes):
    lane = lax.broadcasted_iota(jnp.int32, (rows, lanes), 1)
    return (lane & 64) == 0


def block_diag(size):
    r = lax.broadcasted_iota(jnp.int32, (size, size), 0)
    c = lax.broadcasted_iota(jnp.int32, (size, size), 1)
    return ((r ^ c) & 64) == 0


def soft_pair(raw):
    e = jnp.exp(-jnp.abs(raw))
    one = 1.0 + e
    tail = jnp.where(e < 1e-3, e * (1.0 - e * (0.5 - e * (1.0 / 3.0))), jnp.log(one))
    soft = jnp.maximum(raw, 0.0) + tail
    sig = jnp.where(raw >= 0.0, 1.0, e) / one
    return soft, sig


def norm_rows(v):
    centre = jnp.mean(v, axis=-1, keepdims=True)
    centred = v - centre
    spread = jnp.mean(centred * centred, axis=-1, keepdims=True)
    rstd = lax.rsqrt(spread + EPS)
    return centred * rstd, rstd


class Sender:
    def __init__(self, sems):
        self.sems, self.copies = sems, []

    def put(self, src, dst):
        copy = pltpu.make_async_copy(src, dst, self.sems.at[len(self.copies)])
        copy.start()
        self.copies.append(copy)

    def finish(self):
        for copy in self.copies:
            copy.wait()


def forward_kernel(delta, n, rows,
                   t_ref, meta_ref, tok_ref, arr_ref, cos_ref, sin_ref,
                   wq_ref, wo_ref, wu_ref, wd_ref, gb_ref, s_in,
                   y_ref, s_out, all_o, x_o, att_o, hb_o, act_o, qn_o, kf_o, v_o, sg_o, n1_o, gp_o, n2_o, rs_o, sb_o,
                   x_ref, att_ref, hb_ref, act_ref, qn_ref, kf_ref, v_ref, sg_ref, n1_ref, gp_ref, n2_ref, rs_ref, sb_ref, sems, loads=()):
    stage = meta_ref[0]
    chunk = t_ref[0] - delta * stage
    valid = (chunk >= 0) & (chunk < n)

    def loaded(*which):
        for i in which:
            if loads:
                loads[i].wait()

    @pl.when(jnp.logical_not(valid))
    def _():
        loaded(*range(len(loads)))

    @pl.when(valid)
    def _():
        send = Sender(sems)
        base = pl.multiple_of(chunk * rows, rows)
        here = pl.ds(base, rows)
        first = meta_ref[2 + chunk] != 0
        loaded(0)

        @pl.when(stage == 0)
        def _():
            x_ref[...] = tok_ref[pl.ds(base, rows), :]

        @pl.when(stage != 0)
        def _():
            x_ref[...] = arr_ref[...]

        @pl.when(first)
        def _():
            s_out[...] = jnp.zeros_like(s_out)

        if s_in is not None:
            @pl.when(jnp.logical_not(first))
            def _():
                s_out[...] = s_in[...]

        send.put(x_ref, x_o.at[here, :])
        x = x_ref[...]
        cos = cos_ref[pl.ds(base, rows), :]
        sin = sin_ref[pl.ds(base, rows), :]
        loaded(1)
        q_raw = nn_dot(x, wq_ref[:, 0:D])
        k_raw = nn_dot(x, wq_ref[:, D:2 * D])
        v_ref[...] = nn_dot(x, wq_ref[:, 2 * D:]).astype(bf)
        send.put(v_ref, v_o.at[here, :])
        m_a = head_lanes(rows, 256)
        ri = lax.broadcasted_iota(jnp.int32, (rows, rows), 0)
        ci = lax.broadcasted_iota(jnp.int32, (rows, rows), 1)
        tril = ci <= ri
        diag = block_diag(256)
        ones = jnp.ones((rows, 128), bf)
        zero = jnp.zeros((), bf)
        for p in range(PAIRS):
            lanes = slice(128 * p, 128 * p + 128)
            wide = slice(256 * p, 256 * p + 256)
            q, sq = soft_pair(q_raw[:, lanes])
            k, sk = soft_pair(k_raw[:, lanes])
            qc, qs = q * cos, q * sin
            qf = jnp.concatenate([qc, qs], axis=1).astype(bf)
            kf = jnp.concatenate([k * cos, k * sin], axis=1).astype(bf)
            kf_ref[:, wide] = kf
            sg_ref[:, D + 128 * p:D + 128 * p + 128] = sk.astype(bf)
            ve = jnp.concatenate([v_ref[:, lanes], ones], axis=1)
            s_a = nt_dot(jnp.where(m_a, qf, zero), kf)
            s_b = nt_dot(jnp.where(m_a, zero, qf), kf)
            p_ab = jnp.concatenate([jnp.where(tril, s_a, 0.0), jnp.where(tril, s_b, 0.0)], axis=1).astype(bf)
            ve2 = jnp.concatenate([jnp.where(m_a, ve, zero), jnp.where(m_a, zero, ve)], axis=0)
            before = s_out[p].astype(bf)
            sb_ref[p] = before
            nd = nn_dot(p_ab, ve2) + nn_dot(qf, before)
            inv = 1.0 / nd[:, 128:]
            att_ref[:, lanes] = (nd[:, :128] * inv).astype(bf)
            qn_ref[:, wide] = jnp.concatenate([qc * inv, qs * inv], axis=1).astype(bf)
            sg_ref[:, lanes] = (sq * inv).astype(bf)
            s_out[p] = s_out[p] + jnp.where(diag, tn_dot(kf, ve), 0.0)
        send.put(kf_ref, kf_o.at[here, :])
        send.put(att_ref, att_o.at[here, :])
        send.put(qn_ref, qn_o.at[here, :])
        send.put(sg_ref, sg_o.at[here, :])
        send.put(sb_ref, sb_o.at[chunk])
        loaded(2)
        residual = x.astype(f32) + nn_dot(att_ref[...], wo_ref[...])
        n1, r1 = norm_rows(residual)
        n1_ref[...] = n1.astype(bf)
        hidden = n1 * gb_ref[0:1, :] + gb_ref[1:2, :]
        hb = hidden.astype(bf)
        hb_ref[...] = hb
        send.put(n1_ref, n1_o.at[here, :])
        send.put(hb_ref, hb_o.at[here, :])
        total = hidden
        loaded(3, 4)
        FB = 768
        for j in range(0, 4 * D, FB):
            cols = slice(j, j + FB)
            u = nn_dot(hb, wu_ref[:, cols])
            cdf = 0.5 + 0.5 * lax.erf(u * (1.0 / math.sqrt(2.0)))
            act = (u * cdf).astype(bf)
            act_ref[:, cols] = act
            gp_ref[:, cols] = (cdf + u * (jnp.exp(-0.5 * u * u) * (1.0 / math.sqrt(2.0 * math.pi)))).astype(bf)
            for i in range(j // TILE, (j + FB) // TILE):
                send.put(act_ref.at[:, i * TILE:(i + 1) * TILE], act_o.at[i, here, :])
            send.put(gp_ref.at[:, cols], gp_o.at[here, cols])
            total = total + nn_dot(act, wd_ref[cols, :])
        n2, r2 = norm_rows(total)
        n2_ref[...] = n2.astype(bf)
        lane = lax.broadcasted_iota(jnp.int32, (rows, 128), 1)
        rs_ref[...] = jnp.where(lane < 64, r1, r2)
        send.put(n2_ref, n2_o.at[here, :])
        send.put(rs_ref, rs_o.at[here, :])
        y_ref[...] = (n2 * gb_ref[2:3, :] + gb_ref[3:4, :]).astype(bf)
        send.put(y_ref, all_o.at[here, :])
        loaded(5)
        send.finish()


def far(items):
    return [pltpu.with_memory_space_constraint(item, pltpu.HBM) for item in items]


def near(items):
    return [pltpu.with_memory_space_constraint(item, pltpu.VMEM) for item in items]


def forward_opening(delta, n, rows, *refs):
    ins, refs = refs[:11], refs[11:]
    outs, kept, scratch, load_sems = refs[:16], refs[16:25], refs[25:-1], refs[-1]
    tok, cos, sin, *weights, gb = ins[3:]
    tok_v, _, _, *weights_v = kept[:7]
    head, tail = pl.ds(0, rows), pl.ds(rows, (n - 1) * rows)
    pairs = [(tok.at[head, :], tok_v.at[head, :])] + list(zip(weights, weights_v)) + [(tok.at[tail, :], tok_v.at[tail, :])]
    loads = [pltpu.make_async_copy(src, dst, load_sems.at[i]) for i, (src, dst) in enumerate(pairs)]
    for copy in loads:
        copy.start()
    forward_kernel(delta, n, rows, *ins[:2], tok_v, ins[2], cos, sin, *weights_v, gb, None, *outs, *scratch, loads=loads)


def forward_next(delta, n, rows, *refs):
    t, meta, arr, tok, cos, sin, wq, wo, wu, wd, gb, _, s_in = refs[:13]
    forward_kernel(delta, n, rows, t, meta, tok, arr, cos, sin, wq, wo, wu, wd, gb, s_in, *refs[27:43], *refs[52:])


def saved_items(rows):
    return [((rows, D), bf)] * 3 + [((rows, 4 * D), bf), ((rows, 2 * D), bf), ((rows, 2 * D), bf), ((rows, D), bf), ((rows, 2 * D), bf),
                                    ((rows, D), bf), ((rows, 4 * D), bf), ((rows, D), bf), ((rows, 128), f32), ((PAIRS, 256, 256), bf)]


def kept_items(every):
    return [((every, D), bf), ((every, 128), f32), ((every, 128), f32), ((D, 3 * D), bf), ((D, D), bf), ((D, 4 * D), bf), ((4 * D, D), bf),
            ((4, D), f32), ((TILES, every, TILE), bf)]


def forward_call(rows, n, delta, opening, limit=17):
    V = pl.BlockSpec(memory_space=pltpu.VMEM)
    S = pl.BlockSpec(memory_space=pltpu.SMEM)
    A = pl.BlockSpec(memory_space=pl.ANY)
    sd = jax.ShapeDtypeStruct
    every = n * rows
    big = [pltpu.HBM((every, D), bf)] + [pltpu.HBM(*item) for item in saved_items(every)]
    big[4] = pltpu.HBM((TILES, every, TILE), bf)
    big[13] = pltpu.HBM((n, PAIRS, 256, 256), bf)
    aliases = {4: 17, 5: 18, 10: 23}
    if not opening:
        aliases = {12: 1, **{13 + i: 2 + i for i in range(14)}, **{3 + i: 16 + i for i in range(9)}}
    return pl.pallas_call(
        functools.partial(forward_opening if opening else forward_next, delta, n, rows),
        in_specs=[S, S, V, A, V, V, A, A, A, A, V] if opening else [S, S] + [V] * 11 + [A] * 14,
        out_specs=[V, V] + [A] * 14 + [V] * 9,
        out_shape=[sd((rows, D), bf), sd((PAIRS, 256, 256), f32)] + big + [pltpu.VMEM(*item) for item in kept_items(every)],
        scratch_shapes=[pltpu.VMEM(*item) for item in saved_items(rows)] + [pltpu.SemaphoreType.DMA((30,))] + [pltpu.SemaphoreType.DMA((6,))] * opening,
        input_output_aliases=aliases,
        cost_estimate=pl.CostEstimate(flops=rows * 2 * 9 * 10**6, bytes_accessed=4 * 2**20, transcendentals=0),
        compiler_params=pltpu.CompilerParams(vmem_limit_bytes=limit * 2**20),
        name="layer_forward",
    )


def norm_back(grad, normed, rstd, gain):
    scaled = grad * gain
    mean_one = jnp.mean(scaled, axis=-1, keepdims=True)
    mean_two = jnp.mean(scaled * normed, axis=-1, keepdims=True)
    return rstd * (scaled - mean_one - normed * mean_two)


def backward_kernel(delta, n, rows, stages, groups,
                    t_ref, meta_ref, cot_ref, arr_ref, cos_ref, sin_ref,
                    wq_ref, wo_ref, wu_ref, wd_ref, gb_ref, t_in, ga_in,
                    n2_i, rs_i, gp_i, n1_i, att_i, v_i, qn_i, kf_i, sg_i, sb_i,
                    ds_ref, t_out, ga_out, df_o, du_o, de_o, all_o,
                    df_ref, du_ref, de_ref, dm_ref, da_ref, g_ref,
                    n2_ref, rs_ref, gp_ref, n1_ref, att_ref, v_ref, qn_ref, kf_ref, sg_ref, sb_ref, sems, fetch_sems, loads=()):
    stage = meta_ref[0]
    chunk = n - 1 - t_ref[0] + delta * (stages - 1 - stage)
    valid = (chunk >= 0) & (chunk < n)

    def loaded(*which):
        for i in which:
            if loads:
                loads[i].wait()

    quarters = [slice(j, j + D) for j in range(0, 4 * D, D)]

    def early(which):
        part = pl.ds(pl.multiple_of(which * rows, rows), rows)
        pairs = [(n2_i.at[part, :], n2_ref), (rs_i.at[part, :], rs_ref)] + [(gp_i.at[part, cols], gp_ref.at[:, cols]) for cols in quarters]
        return [pltpu.make_async_copy(src, dst, fetch_sems.at[i]) for i, (src, dst) in enumerate(pairs)]

    @pl.when(chunk == n)
    def _():
        for copy in early(n - 1):
            copy.start()
        for copy in early(n - 1):
            copy.wait()

    @pl.when(jnp.logical_not(valid))
    def _():
        loaded(*range(len(loads)))

    @pl.when(valid)
    def _():
        base = pl.multiple_of(chunk * rows, rows)
        here = pl.ds(base, rows)
        fetched = early(chunk) if loads else []
        for copy in fetched:
            copy.start()
        needed = []
        rest = [(src.at[here, :], dst) for src, dst in ((n1_i, n1_ref), (att_i, att_ref), (v_i, v_ref), (qn_i, qn_ref), (kf_i, kf_ref), (sg_i, sg_ref))]
        for src, dst in rest + [(sb_i.at[chunk], sb_ref)]:
            copy = pltpu.make_async_copy(src, dst, fetch_sems.at[6 + len(needed)])
            copy.start()
            needed.append(copy)
        send = Sender(sems)
        last = meta_ref[2 + n + chunk] != 0

        loaded(0)

        if cot_ref is None:
            g_ref[...] = arr_ref[...]
        else:
            @pl.when(stage == stages - 1)
            def _():
                g_ref[...] = cot_ref[pl.ds(base, rows), :]

            @pl.when(stage != stages - 1)
            def _():
                g_ref[...] = arr_ref[...]

        @pl.when(last)
        def _():
            t_out[...] = jnp.zeros_like(t_out)

        if t_in is not None:
            @pl.when(jnp.logical_not(last))
            def _():
                t_out[...] = t_in[...]

        @pl.when(chunk == n - 1)
        def _():
            ga_out[...] = jnp.zeros_like(ga_out)

        if ga_in is not None:
            @pl.when(chunk != n - 1)
            def _():
                ga_out[...] = ga_in[...]

        g = g_ref[...].astype(f32)
        for copy in fetched:
            copy.wait()
        n2 = n2_ref[...].astype(f32)
        r1 = rs_ref[:, 0:1]
        r2 = rs_ref[:, 64:65]
        ga_out[2:3, :] += jnp.sum(g * n2, axis=0, keepdims=True)
        ga_out[3:4, :] += jnp.sum(g, axis=0, keepdims=True)
        d_two = norm_back(g, n2, r2, gb_ref[2:3, :])
        df = d_two.astype(bf)
        df_ref[...] = df
        send.put(df_ref, df_o.at[here, :])
        total = d_two
        for cols in quarters:
            du = (nt_dot(df, wd_ref[cols, :]) * gp_ref[:, cols].astype(f32)).astype(bf)
            du_ref[:, cols] = du
            for i in range(cols.start // TILE, cols.stop // TILE):
                send.put(du_ref.at[:, i * TILE:(i + 1) * TILE], du_o.at[i, here, :])
            total = total + nt_dot(du, wu_ref[:, cols])
        needed[0].wait()
        n1 = n1_ref[...].astype(f32)
        ga_out[0:1, :] += jnp.sum(total * n1, axis=0, keepdims=True)
        ga_out[1:2, :] += jnp.sum(total, axis=0, keepdims=True)
        d_res = norm_back(total, n1, r1, gb_ref[0:1, :])
        dp = d_res.astype(bf)

        @pl.when(chunk > 0)
        def _():
            for copy in early(chunk - 1):
                copy.start()

        da_ref[...] = nt_dot(dp, wo_ref[...]).astype(bf)
        for copy in needed[1:]:
            copy.wait()
        cos = cos_ref[pl.ds(base, rows), :]
        sin = sin_ref[pl.ds(base, rows), :]
        m_a = head_lanes(rows, 256)
        lane = lax.broadcasted_iota(jnp.int32, (rows, 128), 1)
        ri = lax.broadcasted_iota(jnp.int32, (rows, rows), 0)
        ci = lax.broadcasted_iota(jnp.int32, (rows, rows), 1)
        tril = ci <= ri
        triu = ri <= ci
        diag = block_diag(256)
        ones = jnp.ones((rows, 128), bf)
        zero = jnp.zeros((), bf)
        for p in range(PAIRS):
            lanes = slice(128 * p, 128 * p + 128)
            wide = slice(256 * p, 256 * p + 256)
            d_o = da_ref[:, lanes]
            prod = d_o.astype(f32) * att_ref[:, lanes].astype(f32)
            in_a = jnp.sum(jnp.where(lane < 64, prod, 0.0), axis=1, keepdims=True)
            in_b = jnp.sum(jnp.where(lane < 64, 0.0, prod), axis=1, keepdims=True)
            inner = jnp.where(lane < 64, -in_a, -in_b)
            high = inner.astype(bf).astype(f32)
            ext = jnp.where((lane & 63) == 0, high, jnp.where((lane & 63) == 1, inner - high, 0.0)).astype(bf)
            left = jnp.concatenate([d_o, ext], axis=1)
            left_a, left_b = jnp.where(m_a, left, zero), jnp.where(m_a, zero, left)
            ve = jnp.concatenate([v_ref[:, lanes], ones], axis=1)
            qn = qn_ref[:, wide]
            kf = kf_ref[:, wide]
            qn_a, qn_b = jnp.where(m_a, qn, zero), jnp.where(m_a, zero, qn)
            kf_a, kf_b = jnp.where(m_a, kf, zero), jnp.where(m_a, zero, kf)
            pt = jnp.concatenate([jnp.where(triu, nt_dot(kf, qn_a), 0.0), jnp.where(triu, nt_dot(kf, qn_b), 0.0)], axis=1).astype(bf)
            gg = jnp.concatenate([jnp.where(tril, nt_dot(left_a, ve), 0.0), jnp.where(tril, nt_dot(left_b, ve), 0.0)], axis=1).astype(bf)
            gt = jnp.concatenate([jnp.where(triu, nt_dot(ve, left_a), 0.0), jnp.where(triu, nt_dot(ve, left_b), 0.0)], axis=1).astype(bf)
            after = t_out[p].astype(bf)
            dv = nn_dot(pt, jnp.concatenate([left_a[:, :128], left_b[:, :128]], axis=0)) + nn_dot(kf, after[:, :128])
            dq = nn_dot(gg, jnp.concatenate([kf_a, kf_b], axis=0)) + nt_dot(left, sb_ref[p])
            dk = nn_dot(gt, jnp.concatenate([qn_a, qn_b], axis=0)) + nt_dot(ve, after)
            t_out[p] = t_out[p] + jnp.where(diag, tn_dot(qn, left), 0.0)
            sq = sg_ref[:, lanes].astype(f32)
            sk = sg_ref[:, D + 128 * p:D + 128 * p + 128].astype(f32)
            dm_ref[:, lanes] = ((dq[:, :128] * cos + dq[:, 128:] * sin) * sq).astype(bf)
            dm_ref[:, D + 128 * p:D + 128 * p + 128] = ((dk[:, :128] * cos + dk[:, 128:] * sin) * sk).astype(bf)
            dm_ref[:, 2 * D + 128 * p:2 * D + 128 * p + 128] = dv.astype(bf)
        loaded(1)
        dm = dm_ref[...]
        for g in range(groups):
            odd = g & 1
            part, rest = 9 * g, 3 * g
            inner, outer = part + odd, rest + odd
            de_ref[:, g * D:g * D + 4 * 128] = dm[:, inner * 64:inner * 64 + 4 * 128]
            de_ref[:, g * D + 5 * 128:(g + 1) * D] = dp[:, outer * 64:outer * 64 + 128]
            one = dm[:, (part if odd else part + 8) // 2 * 128:][:, :128].astype(f32)
            two = dp[:, (rest if odd else rest + 2) // 2 * 128:][:, :128].astype(f32)
            if odd:
                one = pltpu.roll(one, 64, 1)
            else:
                two = pltpu.roll(two, 64, 1)
            de_ref[:, g * D + 4 * 128:g * D + 5 * 128] = jnp.where(lane < 64, one, two).astype(bf)
        for i in range(TILES):
            send.put(de_ref.at[:, i * TILE:(i + 1) * TILE], de_o.at[i, here, :])
        ds_ref[...] = (d_res + nt_dot(dm, wq_ref[...])).astype(bf)
        send.put(ds_ref, all_o.at[here, :])
        send.finish()

        @pl.when(chunk > 0)
        def _():
            for copy in early(chunk - 1):
                copy.wait()


def backward_opening(delta, n, rows, stages, groups, *refs):
    t, meta, arr = refs[:3]
    cot, cot_v, load_sems, refs = refs[22], refs[30], refs[-1], refs[:-1]
    head, tail = pl.ds((n - 1) * rows, rows), pl.ds(0, (n - 1) * rows)
    loads = [pltpu.make_async_copy(cot.at[part, :], cot_v.at[part, :], load_sems.at[i]) for i, part in enumerate((head, tail))]
    for copy in loads:
        copy.start()
    backward_kernel(delta, n, rows, stages, groups, t, meta, cot_v, arr, *refs[4:11], None, None, *refs[12:22], *refs[23:30],
                    *refs[42:48], *refs[39:42], *refs[48:], loads=loads)


def backward_next(delta, n, rows, stages, groups, *refs):
    t, meta, arr, cot = refs[:4]
    act, act_v, sem, refs = refs[31], refs[47], refs[-1], refs[:-1]
    fill = (t[0] >= 1) & (t[0] <= TILES)
    tile = jnp.clip(t[0] - 1, 0, TILES - 1)
    copy = pltpu.make_async_copy(act.at[tile], act_v.at[tile], sem)

    @pl.when(fill)
    def _():
        copy.start()

    backward_kernel(delta, n, rows, stages, groups, t, meta, cot, arr, *refs[4:11], *refs[15:27], *refs[32:39],
                    *refs[51:57], *refs[48:51], *refs[57:])

    @pl.when(fill)
    def _():
        copy.wait()


def backward_call(rows, n, delta, stages, groups, opening, limit=17):
    V = pl.BlockSpec(memory_space=pltpu.VMEM)
    S = pl.BlockSpec(memory_space=pltpu.SMEM)
    A = pl.BlockSpec(memory_space=pl.ANY)
    sd = jax.ShapeDtypeStruct
    every = n * rows
    made = [((rows, D), bf), ((rows, 4 * D), bf), ((rows, 4 * D), bf)]
    saved = [((rows, D), bf), ((rows, 128), f32), ((rows, 4 * D), bf), ((rows, D), bf), ((rows, D), bf), ((rows, D), bf),
             ((rows, 2 * D), bf), ((rows, 2 * D), bf), ((rows, 2 * D), bf), ((PAIRS, 256, 256), bf)]
    own = [((rows, 3 * D), bf), ((rows, D), bf), ((rows, D), bf)]
    early, saved = saved[:3], saved[3:]
    big = [pltpu.HBM((every, D), bf), pltpu.HBM((TILES, every, TILE), bf), pltpu.HBM((TILES, every, TILE), bf), pltpu.HBM((every, D), bf)]
    if opening:
        aliases = {3 + i: 7 + i for i in range(9)}
    else:
        aliases = {**{3 + i: 7 + i for i in range(12)}, 15: 1, 16: 2, **{27 + i: 3 + i for i in range(4)}}
    return pl.pallas_call(
        functools.partial(backward_opening if opening else backward_next, delta, n, rows, stages, groups),
        in_specs=[S, S] + [V] * 10 + [A] * 11 if opening else [S, S] + [V] * 15 + [A] * 15,
        out_specs=[V] * 3 + [A] * 4 + [V] * 12,
        out_shape=[sd((rows, D), bf), sd((PAIRS, 256, 256), f32), sd((8, D), f32)] + big
        + [pltpu.VMEM(*item) for item in kept_items(every) + early],
        scratch_shapes=[pltpu.VMEM(*item) for item in made + own + saved] + [pltpu.SemaphoreType.DMA((30,)), pltpu.SemaphoreType.DMA((13,))]
        + [pltpu.SemaphoreType.DMA((2,)) if opening else pltpu.SemaphoreType.DMA],
        input_output_aliases=aliases,
        cost_estimate=pl.CostEstimate(flops=rows * 2 * 10 * 10**6, bytes_accessed=4 * 2**20, transcendentals=0),
        compiler_params=pltpu.CompilerParams(vmem_limit_bytes=limit * 2**20),
        name="layer_backward",
    )


HALF = D // 2


def weight_kernel(groups, half, mixed, waits, fetch, ahead, meta_ref, left, *refs):
    raws, refs = refs[:1 + mixed], refs[1 + mixed + waits:]
    sources, refs = refs[:ahead], refs[ahead:]
    keep_o, send_o, refs = refs[0], refs[1], refs[2:]
    kept, refs = refs[:fetch], refs[fetch:]
    targets, refs = refs[:ahead], refs[ahead:]
    turned, out_buf, out_sem, raw_sem, ahead_sem = refs
    me = meta_ref[1]
    share = TILES // groups
    every = raws[0].shape[0]
    raw_copies, later = [], []
    if fetch:
        raw_copies = [pltpu.make_async_copy(raws[0].at[k:k + 256, :], kept[0].at[k:k + 256, :], raw_sem.at[k // 256]) for k in range(0, every, 256)]
        raws = kept
    for source, target in zip(sources, targets):
        step = 1 if len(source.shape) == 3 else every // 4
        for k in range(0, source.shape[0], step):
            later.append(pltpu.make_async_copy(source.at[k:k + step], target.at[k:k + step], ahead_sem.at[len(later)]))
    for copy in raw_copies + later:
        copy.start()
    for j, raw in enumerate(raws):
        for k in range(0, every, 256):
            if fetch:
                raw_copies[k // 256].wait()
            turned[j, :, k:k + 256] = raw[k:k + 256, half * HALF:(half + 1) * HALF].T
    for g in range(groups):
        for i in range(share):
            cols = slice(i * TILE, (i + 1) * TILE)
            value = nn_dot(turned[0], left[g * share + i])
            if mixed and i == share - 1:
                other = nn_dot(turned[1], left[g * share + i])
                lane = lax.broadcasted_iota(jnp.int32, other.shape, 1)
                value = jnp.where(lane < 3 * D // groups - i * TILE, value, other)
            out_buf[g, :, cols] = value.astype(bf)
        rel = g ^ me

        @pl.when((rel & 1) == 0)
        def _():
            pltpu.make_async_copy(out_buf.at[g], keep_o.at[rel >> 1], out_sem).start()

        @pl.when((rel & 1) == 1)
        def _():
            pltpu.make_async_copy(out_buf.at[g], send_o.at[rel >> 1], out_sem).start()
    pltpu.make_async_copy(out_buf, out_buf, out_sem).wait()
    for copy in later:
        copy.wait()


def weight_call(every, groups, half, mixed, waits, fetch, ahead, limit=12):
    V = pl.BlockSpec(memory_space=pltpu.VMEM)
    S = pl.BlockSpec(memory_space=pltpu.SMEM)
    A = pl.BlockSpec(memory_space=pl.ANY)
    raws = 1 + mixed
    return pl.pallas_call(
        functools.partial(weight_kernel, groups, half, mixed, waits, fetch, len(ahead)),
        in_specs=[S, V] + [A if fetch else V] * raws + [A] * (waits + len(ahead)),
        out_specs=[A] * 2 + [V] * (fetch + len(ahead)),
        out_shape=[pltpu.HBM((2, HALF, D), bf)] * 2 + [pltpu.VMEM((every, D), bf)] * fetch + [pltpu.VMEM(shape, bf) for shape in ahead],
        scratch_shapes=[pltpu.VMEM((raws, HALF, every), bf), pltpu.VMEM((groups, HALF, D), bf), pltpu.SemaphoreType.DMA,
                        pltpu.SemaphoreType.DMA((every // 256,)), pltpu.SemaphoreType.DMA((24,))],
        cost_estimate=pl.CostEstimate(flops=2 * every * HALF * 4 * D, bytes_accessed=every * 5 * D * 2, transcendentals=0),
        compiler_params=pltpu.CompilerParams(vmem_limit_bytes=limit * 2**20),
        name="weight_grad",
    )


READY = {2: 0, 3: 1, 4: 2, 5: 3}
MB_ROWS = 1024
MICRO = 2
ROWS = 256
DELTA = 2


def geometry(doc_ids):
    quarter = MB_ROWS // 4
    marks = doc_ids.reshape(-1, MB_ROWS)[:, ::quarter]
    pieces = 1 + jnp.sum((marks[:, 1:] != marks[:, :-1]).astype(jnp.int32), axis=1)
    length = MB_ROWS // pieces
    row = jnp.arange(MB_ROWS, dtype=jnp.int32)
    position = row[None, :] % length[:, None]
    angle = (0.5 * math.pi) * position.astype(f32) / length[:, None].astype(f32)
    angle = angle.reshape(-1, 1)
    starts = jnp.arange(0, MB_ROWS, ROWS, dtype=jnp.int32)
    first = (starts[None, :] % length[:, None]) == 0
    last = ((starts[None, :] + ROWS) % length[:, None]) == 0
    wide = (angle.shape[0], 128)
    return (jnp.broadcast_to(jnp.cos(angle), wide), jnp.broadcast_to(jnp.sin(angle), wide),
            first.reshape(-1).astype(jnp.int32), last.reshape(-1).astype(jnp.int32))


def exchange(block, axis, flip):
    route = [(i, i ^ flip) for i in range(lax.axis_size(axis))]
    return lax.ppermute(block, axis, route)


def add_kernel(*refs):
    total = sum(ref[...].reshape(refs[-1].shape).astype(f32) for ref in refs[:-1])
    refs[-1][...] = total.astype(refs[-1].dtype)


def add_call(slot, keep, got, *more, limit=12):
    rows, columns = keep.shape[1:]
    step = min(rows, 192)
    pick = pl.BlockSpec((1, step, columns), lambda i: (slot, i, 0))
    flat = pl.BlockSpec((step, columns), lambda i: (i, 0))
    return pl.pallas_call(
        add_kernel,
        grid=(rows // step,),
        in_specs=[pick, pick] + [flat] * len(more),
        out_specs=flat,
        out_shape=jax.ShapeDtypeStruct((rows, columns), keep.dtype),
        cost_estimate=pl.CostEstimate(flops=rows * columns * 2, bytes_accessed=rows * columns * 6, transcendentals=0),
        compiler_params=pltpu.CompilerParams(vmem_limit_bytes=limit * 2**20),
        name="add_parts",
    )(keep, got, *more)


def plain_add(*items, limit=12):
    V = pl.BlockSpec(memory_space=pltpu.VMEM)
    return pl.pallas_call(
        add_kernel, in_specs=[V] * len(items), out_specs=V, out_shape=jax.ShapeDtypeStruct(items[0].shape, items[0].dtype),
        cost_estimate=pl.CostEstimate(flops=items[0].size, bytes_accessed=items[0].size * 4, transcendentals=0),
        compiler_params=pltpu.CompilerParams(vmem_limit_bytes=limit * 2**20), name="add_vectors",
    )(*items)


def spread(own, before):
    if lax.axis_size("dp") != 2:
        return lax.psum(own, "dp")
    if before:
        before[-1], own = lax.optimization_barrier((before[-1], own))
    return exchange(own, "dp", 1)


def finished(own, other):
    if lax.axis_size("dp") == 2:
        return own.astype(f32) + other.astype(f32)
    return other.astype(f32)


def local(tokens, doc_ids, cotangent, w_qkv, w_out, w_up, w_down,
          first_gain, first_bias, second_gain, second_bias):
    stages = lax.axis_size("pipe")
    groups = lax.axis_size("group")
    stage = lax.axis_index("pipe").astype(jnp.int32)
    me = lax.axis_index("group").astype(jnp.int32)
    n = tokens.shape[0] // ROWS
    ticks = n + DELTA * (stages - 1)
    cos, sin, first, last = geometry(doc_ids)
    meta = jnp.concatenate([stage[None], me[None], first, last])
    resident = far((tokens,)) + [cos, sin] + far((w_qkv[0], w_out[0], w_up[0], w_down[0]))
    gb = jnp.concatenate([first_gain, first_bias, second_gain, second_bias], axis=0)
    blank = jnp.zeros((ROWS, D), bf)
    arriving = [blank] * DELTA
    resident = resident + [gb]
    state, big = (), ()
    for t in range(ticks):
        made = forward_call(ROWS, n, DELTA, t == 0)(jnp.full((1,), t, jnp.int32), meta, arriving.pop(0), *resident, *state, *big)
        state, big, resident = made[1:2], made[2:16], made[16:]
        route = [(a, a + 1) for a in range(stages - 1) if 0 <= t - a * DELTA < n]
        arriving.append(lax.ppermute(made[0], "pipe", route) if route else made[0])
    block_out, x, att, hb, act, qn, kf, v, sg, n1, gp, n2, rs, sb = big
    arriving = [made[0]] * DELTA
    state, big = (), ()
    for t in range(ticks):
        made = backward_call(ROWS, n, DELTA, stages, groups, t == 0)(
            jnp.full((1,), t, jnp.int32), meta, arriving.pop(0), *resident, *state,
            *far((n2, rs, gp, n1, att, v, qn, kf, sg, sb)), *big, *far([act if t > 0 else cotangent]))
        state, big, resident = made[1:3], made[3:7], made[7:]
        route = [(a, a - 1) for a in range(1, stages) if 0 <= t - (stages - 1 - a) * DELTA < n]
        arriving.append(lax.ppermute(made[0], "pipe", route) if route else made[0])
    df, du, de, input_grad = big
    act = resident[8]
    pieces = [(act, df), (de, x, att), (du, hb)]
    vectors = state[1]
    for flip in (1, 2):
        vectors = plain_add(vectors, exchange(vectors, "group", flip))
    aways, keeps, gots, backs, owns, others = [], [], [], [], [], []

    def turn(k):
        if backs:
            backs[-1], aways[k] = lax.optimization_barrier((backs[-1], aways[k]))
        backs.append(exchange(aways[k], "group", 2))

    for piece in range(3):
        left, *rights = pieces[piece]
        for half in range(2):
            k = len(keeps)
            fetch = k == 0
            ready = READY.get(k)
            waits = [] if ready is None else [aways[ready]]
            call = weight_call(n * ROWS, groups, half, len(rights) == 2, len(waits), fetch, [])
            keep, send, *loads = call(meta, left, *(far(rights) if fetch else rights), *waits)
            rights = loads if fetch else rights
            keeps.append(keep)
            gots.append(exchange(send, "group", 1))
            away = add_call(1, keep, gots[-1])
            if k == 1:
                vectors, away = lax.optimization_barrier((vectors, away))
            aways.append(away)
            turn(k)
    for keep, got, back in zip(keeps, gots, backs):
        own = add_call(0, keep, got, back)
        other = spread(own, others)
        owns.append(own)
        others.append(other)
    parts = [finished(*pair) for pair in zip(owns, others)]
    if lax.axis_size("dp") == 2:
        vectors = plain_add(vectors, exchange(vectors, "dp", 1))
    else:
        vectors = lax.psum(vectors, "dp")
    vectors, me, _ = lax.optimization_barrier((vectors, me, owns[3]))
    mine = lax.dynamic_slice_in_dim(vectors, me * (D // groups), D // groups, axis=1)
    g_down, g_mixed, g_up = (jnp.concatenate(parts[i:i + 2], axis=0) for i in (0, 2, 4))
    odd = (me & 1) == 1
    swap = lambda a, b: jnp.concatenate([g_mixed[:, a], g_mixed[:, b]], axis=1)
    low, one, two, high = slice(0, 512), slice(512, 576), slice(576, 640), slice(640, 768)
    g_qkv = jnp.where(odd, swap(one, low), swap(low, one))
    g_out = jnp.where(odd, swap(two, high), swap(high, two))
    return (block_out[None], input_grad[None], g_qkv[None], g_out[None], g_up[None], g_down.T[None],
            mine[0:1], mine[1:2], mine[2:3], mine[3:4])


def solution(mesh):
    rows = ("group", "dp")
    whole = P("pipe", None, None)
    vector = P("pipe", None)
    return jax.shard_map(
        local,
        mesh=mesh,
        in_specs=(P(rows, None), P(rows), P(rows, None)) + (whole,) * 4 + (vector,) * 4,
        out_specs=(P("pipe", rows, None), P("pipe", rows, None), P("pipe", None, "group"), P("pipe", None, "group"),
                   P("pipe", None, "group"), P("pipe", "group", None)) + (P("pipe", "group"),) * 4,
        check_vma=False,
    )
```

```python
import functools, math
import jax, jax.numpy as jnp
from jax import lax
from jax.experimental import pallas as pl
from jax.experimental.pallas import tpu as pltpu
from jax.sharding import PartitionSpec as P

bf = jnp.bfloat16
f32 = jnp.float32
EPS = 1e-05
D = 768
PAIRS = 6
TILE = 256
TILES = 4 * D // TILE
NT = (((1,), (1,)), ((), ()))
TN = (((0,), (0,)), ((), ()))


def nn_dot(a, b):
    return jnp.dot(a, b, preferred_element_type=f32)


def nt_dot(a, b):
    return lax.dot_general(a, b, NT, preferred_element_type=f32)


def tn_dot(a, b):
    return lax.dot_general(a, b, TN, preferred_element_type=f32)


def head_lanes(rows, lanes):
    lane = lax.broadcasted_iota(jnp.int32, (rows, lanes), 1)
    return (lane & 64) == 0


def block_diag(size):
    r = lax.broadcasted_iota(jnp.int32, (size, size), 0)
    c = lax.broadcasted_iota(jnp.int32, (size, size), 1)
    return ((r ^ c) & 64) == 0


def soft_pair(raw):
    e = jnp.exp(-jnp.abs(raw))
    one = 1.0 + e
    tail = jnp.where(e < 1e-3, e * (1.0 - e * (0.5 - e * (1.0 / 3.0))), jnp.log(one))
    soft = jnp.maximum(raw, 0.0) + tail
    sig = jnp.where(raw >= 0.0, 1.0, e) / one
    return soft, sig


def norm_rows(v):
    centre = jnp.mean(v, axis=-1, keepdims=True)
    centred = v - centre
    spread = jnp.mean(centred * centred, axis=-1, keepdims=True)
    rstd = lax.rsqrt(spread + EPS)
    return centred * rstd, rstd


class Sender:
    def __init__(self, sems):
        self.sems, self.copies = sems, []

    def put(self, src, dst):
        copy = pltpu.make_async_copy(src, dst, self.sems.at[len(self.copies)])
        copy.start()
        self.copies.append(copy)

    def finish(self):
        for copy in self.copies:
            copy.wait()


def forward_kernel(delta, n, rows,
                   t_ref, meta_ref, tok_ref, arr_ref, cos_ref, sin_ref,
                   wq_ref, wo_ref, wu_ref, wd_ref, gb_ref, s_in,
                   y_ref, s_out, all_o, x_o, att_o, hb_o, act_o, qn_o, kf_o, v_o, sg_o, n1_o, gp_o, n2_o, rs_o, sb_o,
                   x_ref, att_ref, hb_ref, act_ref, qn_ref, kf_ref, v_ref, sg_ref, n1_ref, gp_ref, n2_ref, rs_ref, sb_ref, sems, loads=()):
    stage = meta_ref[0]
    chunk = t_ref[0] - delta * stage
    valid = (chunk >= 0) & (chunk < n)

    def loaded(*which):
        for i in which:
            if loads:
                loads[i].wait()

    @pl.when(jnp.logical_not(valid))
    def _():
        loaded(*range(len(loads)))

    @pl.when(valid)
    def _():
        send = Sender(sems)
        base = pl.multiple_of(chunk * rows, rows)
        here = pl.ds(base, rows)
        first = meta_ref[2 + chunk] != 0
        loaded(0)

        @pl.when(stage == 0)
        def _():
            x_ref[...] = tok_ref[pl.ds(base, rows), :]

        @pl.when(stage != 0)
        def _():
            x_ref[...] = arr_ref[...]

        @pl.when(first)
        def _():
            s_out[...] = jnp.zeros_like(s_out)

        if s_in is not None:
            @pl.when(jnp.logical_not(first))
            def _():
                s_out[...] = s_in[...]

        send.put(x_ref, x_o.at[here, :])
        x = x_ref[...]
        cos = cos_ref[pl.ds(base, rows), :]
        sin = sin_ref[pl.ds(base, rows), :]
        loaded(1)
        q_raw = nn_dot(x, wq_ref[:, 0:D])
        k_raw = nn_dot(x, wq_ref[:, D:2 * D])
        v_ref[...] = nn_dot(x, wq_ref[:, 2 * D:]).astype(bf)
        send.put(v_ref, v_o.at[here, :])
        m_a = head_lanes(rows, 256)
        ri = lax.broadcasted_iota(jnp.int32, (rows, rows), 0)
        ci = lax.broadcasted_iota(jnp.int32, (rows, rows), 1)
        tril = ci <= ri
        diag = block_diag(256)
        ones = jnp.ones((rows, 128), bf)
        zero = jnp.zeros((), bf)
        for p in range(PAIRS):
            lanes = slice(128 * p, 128 * p + 128)
            wide = slice(256 * p, 256 * p + 256)
            q, sq = soft_pair(q_raw[:, lanes])
            k, sk = soft_pair(k_raw[:, lanes])
            qc, qs = q * cos, q * sin
            qf = jnp.concatenate([qc, qs], axis=1).astype(bf)
            kf = jnp.concatenate([k * cos, k * sin], axis=1).astype(bf)
            kf_ref[:, wide] = kf
            sg_ref[:, D + 128 * p:D + 128 * p + 128] = sk.astype(bf)
            ve = jnp.concatenate([v_ref[:, lanes], ones], axis=1)
            s_a = nt_dot(jnp.where(m_a, qf, zero), kf)
            s_b = nt_dot(jnp.where(m_a, zero, qf), kf)
            p_ab = jnp.concatenate([jnp.where(tril, s_a, 0.0), jnp.where(tril, s_b, 0.0)], axis=1).astype(bf)
            ve2 = jnp.concatenate([jnp.where(m_a, ve, zero), jnp.where(m_a, zero, ve)], axis=0)
            before = s_out[p].astype(bf)
            sb_ref[p] = before
            nd = nn_dot(p_ab, ve2) + nn_dot(qf, before)
            inv = 1.0 / nd[:, 128:]
            att_ref[:, lanes] = (nd[:, :128] * inv).astype(bf)
            qn_ref[:, wide] = jnp.concatenate([qc * inv, qs * inv], axis=1).astype(bf)
            sg_ref[:, lanes] = (sq * inv).astype(bf)
            s_out[p] = s_out[p] + jnp.where(diag, tn_dot(kf, ve), 0.0)
        send.put(kf_ref, kf_o.at[here, :])
        send.put(att_ref, att_o.at[here, :])
        send.put(qn_ref, qn_o.at[here, :])
        send.put(sg_ref, sg_o.at[here, :])
        send.put(sb_ref, sb_o.at[chunk])
        loaded(2)
        residual = x.astype(f32) + nn_dot(att_ref[...], wo_ref[...])
        n1, r1 = norm_rows(residual)
        n1_ref[...] = n1.astype(bf)
        hidden = n1 * gb_ref[0:1, :] + gb_ref[1:2, :]
        hb = hidden.astype(bf)
        hb_ref[...] = hb
        send.put(n1_ref, n1_o.at[here, :])
        send.put(hb_ref, hb_o.at[here, :])
        total = hidden
        loaded(3, 4)
        FB = 768
        for j in range(0, 4 * D, FB):
            cols = slice(j, j + FB)
            u = nn_dot(hb, wu_ref[:, cols])
            cdf = 0.5 + 0.5 * lax.erf(u * (1.0 / math.sqrt(2.0)))
            act = (u * cdf).astype(bf)
            act_ref[:, cols] = act
            gp_ref[:, cols] = (cdf + u * (jnp.exp(-0.5 * u * u) * (1.0 / math.sqrt(2.0 * math.pi)))).astype(bf)
            for i in range(j // TILE, (j + FB) // TILE):
                send.put(act_ref.at[:, i * TILE:(i + 1) * TILE], act_o.at[i, here, :])
            send.put(gp_ref.at[:, cols], gp_o.at[here, cols])
            total = total + nn_dot(act, wd_ref[cols, :])
        n2, r2 = norm_rows(total)
        n2_ref[...] = n2.astype(bf)
        lane = lax.broadcasted_iota(jnp.int32, (rows, 128), 1)
        rs_ref[...] = jnp.where(lane < 64, r1, r2)
        send.put(n2_ref, n2_o.at[here, :])
        send.put(rs_ref, rs_o.at[here, :])
        y_ref[...] = (n2 * gb_ref[2:3, :] + gb_ref[3:4, :]).astype(bf)
        send.put(y_ref, all_o.at[here, :])
        loaded(5)
        send.finish()


def far(items):
    return [pltpu.with_memory_space_constraint(item, pltpu.HBM) for item in items]


def near(items):
    return [pltpu.with_memory_space_constraint(item, pltpu.VMEM) for item in items]


def forward_opening(delta, n, rows, *refs):
    ins, refs = refs[:11], refs[11:]
    outs, kept, scratch, load_sems = refs[:16], refs[16:25], refs[25:-1], refs[-1]
    tok, cos, sin, *weights, gb = ins[3:]
    tok_v, _, _, *weights_v = kept[:7]
    head, tail = pl.ds(0, rows), pl.ds(rows, (n - 1) * rows)
    pairs = [(tok.at[head, :], tok_v.at[head, :])] + list(zip(weights, weights_v)) + [(tok.at[tail, :], tok_v.at[tail, :])]
    loads = [pltpu.make_async_copy(src, dst, load_sems.at[i]) for i, (src, dst) in enumerate(pairs)]
    for copy in loads:
        copy.start()
    forward_kernel(delta, n, rows, *ins[:2], tok_v, ins[2], cos, sin, *weights_v, gb, None, *outs, *scratch, loads=loads)


def forward_next(delta, n, rows, *refs):
    t, meta, arr, tok, cos, sin, wq, wo, wu, wd, gb, _, s_in = refs[:13]
    forward_kernel(delta, n, rows, t, meta, tok, arr, cos, sin, wq, wo, wu, wd, gb, s_in, *refs[27:43], *refs[52:])


def saved_items(rows):
    return [((rows, D), bf)] * 3 + [((rows, 4 * D), bf), ((rows, 2 * D), bf), ((rows, 2 * D), bf), ((rows, D), bf), ((rows, 2 * D), bf),
                                    ((rows, D), bf), ((rows, 4 * D), bf), ((rows, D), bf), ((rows, 128), f32), ((PAIRS, 256, 256), bf)]


def kept_items(every):
    return [((every, D), bf), ((every, 128), f32), ((every, 128), f32), ((D, 3 * D), bf), ((D, D), bf), ((D, 4 * D), bf), ((4 * D, D), bf),
            ((4, D), f32), ((TILES, every, TILE), bf)]


def forward_call(rows, n, delta, opening, limit=17):
    V = pl.BlockSpec(memory_space=pltpu.VMEM)
    S = pl.BlockSpec(memory_space=pltpu.SMEM)
    A = pl.BlockSpec(memory_space=pl.ANY)
    sd = jax.ShapeDtypeStruct
    every = n * rows
    big = [pltpu.HBM((every, D), bf)] + [pltpu.HBM(*item) for item in saved_items(every)]
    big[4] = pltpu.HBM((TILES, every, TILE), bf)
    big[13] = pltpu.HBM((n, PAIRS, 256, 256), bf)
    aliases = {4: 17, 5: 18, 10: 23}
    if not opening:
        aliases = {12: 1, **{13 + i: 2 + i for i in range(14)}, **{3 + i: 16 + i for i in range(9)}}
    return pl.pallas_call(
        functools.partial(forward_opening if opening else forward_next, delta, n, rows),
        in_specs=[S, S, V, A, V, V, A, A, A, A, V] if opening else [S, S] + [V] * 11 + [A] * 14,
        out_specs=[V, V] + [A] * 14 + [V] * 9,
        out_shape=[sd((rows, D), bf), sd((PAIRS, 256, 256), f32)] + big + [pltpu.VMEM(*item) for item in kept_items(every)],
        scratch_shapes=[pltpu.VMEM(*item) for item in saved_items(rows)] + [pltpu.SemaphoreType.DMA((30,))] + [pltpu.SemaphoreType.DMA((6,))] * opening,
        input_output_aliases=aliases,
        cost_estimate=pl.CostEstimate(flops=rows * 2 * 9 * 10**6, bytes_accessed=4 * 2**20, transcendentals=0),
        compiler_params=pltpu.CompilerParams(vmem_limit_bytes=limit * 2**20),
        name="layer_forward",
    )


def norm_back(grad, normed, rstd, gain):
    scaled = grad * gain
    mean_one = jnp.mean(scaled, axis=-1, keepdims=True)
    mean_two = jnp.mean(scaled * normed, axis=-1, keepdims=True)
    return rstd * (scaled - mean_one - normed * mean_two)


def backward_kernel(delta, n, rows, stages, groups,
                    t_ref, meta_ref, cot_ref, arr_ref, cos_ref, sin_ref,
                    wq_ref, wo_ref, wu_ref, wd_ref, gb_ref, t_in, ga_in,
                    n2_i, rs_i, gp_i, n1_i, att_i, v_i, qn_i, kf_i, sg_i, sb_i,
                    ds_ref, t_out, ga_out, df_o, du_o, de_o, all_o,
                    df_ref, du_ref, mix_ref, dm_ref, da_ref, g_ref, dp_ref,
                    n2_ref, rs_ref, gp_ref, n1_ref, att_ref, v_ref, qn_ref, kf_ref, sg_ref, sb_ref, sems, fetch_sems, loads=()):
    stage = meta_ref[0]
    chunk = n - 1 - t_ref[0] + delta * (stages - 1 - stage)
    valid = (chunk >= 0) & (chunk < n)

    def loaded(*which):
        for i in which:
            if loads:
                loads[i].wait()

    quarters = [slice(j, j + D) for j in range(0, 4 * D, D)]

    def early(which):
        part = pl.ds(pl.multiple_of(which * rows, rows), rows)
        pairs = [(n2_i.at[part, :], n2_ref), (rs_i.at[part, :], rs_ref)] + [(gp_i.at[part, cols], gp_ref.at[:, cols]) for cols in quarters]
        return [pltpu.make_async_copy(src, dst, fetch_sems.at[i]) for i, (src, dst) in enumerate(pairs)]

    @pl.when(chunk == n)
    def _():
        for copy in early(n - 1):
            copy.start()
        for copy in early(n - 1):
            copy.wait()

    @pl.when(jnp.logical_not(valid))
    def _():
        loaded(*range(len(loads)))

    @pl.when(valid)
    def _():
        base = pl.multiple_of(chunk * rows, rows)
        here = pl.ds(base, rows)
        fetched = early(chunk) if loads else []
        for copy in fetched:
            copy.start()
        needed = []
        rest = [(src.at[here, :], dst) for src, dst in ((n1_i, n1_ref), (att_i, att_ref), (v_i, v_ref), (qn_i, qn_ref), (kf_i, kf_ref), (sg_i, sg_ref))]
        for src, dst in rest + [(sb_i.at[chunk], sb_ref)]:
            copy = pltpu.make_async_copy(src, dst, fetch_sems.at[6 + len(needed)])
            copy.start()
            needed.append(copy)
        send = Sender(sems)

        def place(part, g, spot):
            send.put(part, de_o.at[3 * g + spot // 2, here, spot % 2 * 128:spot % 2 * 128 + 128])

        last = meta_ref[2 + n + chunk] != 0

        loaded(0)

        if cot_ref is None:
            g_ref[...] = arr_ref[...]
        else:
            @pl.when(stage == stages - 1)
            def _():
                g_ref[...] = cot_ref[pl.ds(base, rows), :]

            @pl.when(stage != stages - 1)
            def _():
                g_ref[...] = arr_ref[...]

        @pl.when(last)
        def _():
            t_out[...] = jnp.zeros_like(t_out)

        if t_in is not None:
            @pl.when(jnp.logical_not(last))
            def _():
                t_out[...] = t_in[...]

        @pl.when(chunk == n - 1)
        def _():
            ga_out[...] = jnp.zeros_like(ga_out)

        if ga_in is not None:
            @pl.when(chunk != n - 1)
            def _():
                ga_out[...] = ga_in[...]

        g = g_ref[...].astype(f32)
        for copy in fetched:
            copy.wait()
        n2 = n2_ref[...].astype(f32)
        r1 = rs_ref[:, 0:1]
        r2 = rs_ref[:, 64:65]
        ga_out[2:3, :] += jnp.sum(g * n2, axis=0, keepdims=True)
        ga_out[3:4, :] += jnp.sum(g, axis=0, keepdims=True)
        d_two = norm_back(g, n2, r2, gb_ref[2:3, :])
        df = d_two.astype(bf)
        df_ref[...] = df
        send.put(df_ref, df_o.at[here, :])
        total = d_two
        for cols in quarters:
            du = (nt_dot(df, wd_ref[cols, :]) * gp_ref[:, cols].astype(f32)).astype(bf)
            du_ref[:, cols] = du
            for i in range(cols.start // TILE, cols.stop // TILE):
                send.put(du_ref.at[:, i * TILE:(i + 1) * TILE], du_o.at[i, here, :])
            total = total + nt_dot(du, wu_ref[:, cols])
        needed[0].wait()
        n1 = n1_ref[...].astype(f32)
        ga_out[0:1, :] += jnp.sum(total * n1, axis=0, keepdims=True)
        ga_out[1:2, :] += jnp.sum(total, axis=0, keepdims=True)
        d_res = norm_back(total, n1, r1, gb_ref[0:1, :])
        dp = d_res.astype(bf)
        dp_ref[...] = dp
        for g, j in enumerate((0, 2, 3, 5)):
            place(dp_ref.at[:, 128 * j:128 * j + 128], g, 5)

        @pl.when(chunk > 0)
        def _():
            for copy in early(chunk - 1):
                copy.start()

        for copy in needed[1:]:
            copy.wait()
        da_ref[...] = nt_dot(dp, wo_ref[...]).astype(bf)
        cos = cos_ref[pl.ds(base, rows), :]
        sin = sin_ref[pl.ds(base, rows), :]
        m_a = head_lanes(rows, 256)
        lane = lax.broadcasted_iota(jnp.int32, (rows, 128), 1)
        ri = lax.broadcasted_iota(jnp.int32, (rows, rows), 0)
        ci = lax.broadcasted_iota(jnp.int32, (rows, rows), 1)
        tril = ci <= ri
        triu = ri <= ci
        diag = block_diag(256)
        ones = jnp.ones((rows, 128), bf)
        zero = jnp.zeros((), bf)
        d_state = d_res
        for p in range(PAIRS):
            lanes = slice(128 * p, 128 * p + 128)
            wide = slice(256 * p, 256 * p + 256)
            d_o = da_ref[:, lanes]
            prod = d_o.astype(f32) * att_ref[:, lanes].astype(f32)
            in_a = jnp.sum(jnp.where(lane < 64, prod, 0.0), axis=1, keepdims=True)
            in_b = jnp.sum(jnp.where(lane < 64, 0.0, prod), axis=1, keepdims=True)
            inner = jnp.where(lane < 64, -in_a, -in_b)
            high = inner.astype(bf).astype(f32)
            ext = jnp.where((lane & 63) == 0, high, jnp.where((lane & 63) == 1, inner - high, 0.0)).astype(bf)
            left = jnp.concatenate([d_o, ext], axis=1)
            left_a, left_b = jnp.where(m_a, left, zero), jnp.where(m_a, zero, left)
            ve = jnp.concatenate([v_ref[:, lanes], ones], axis=1)
            qn = qn_ref[:, wide]
            kf = kf_ref[:, wide]
            qn_a, qn_b = jnp.where(m_a, qn, zero), jnp.where(m_a, zero, qn)
            kf_a, kf_b = jnp.where(m_a, kf, zero), jnp.where(m_a, zero, kf)
            pt = jnp.concatenate([jnp.where(triu, nt_dot(kf, qn_a), 0.0), jnp.where(triu, nt_dot(kf, qn_b), 0.0)], axis=1).astype(bf)
            gg = jnp.concatenate([jnp.where(tril, nt_dot(left_a, ve), 0.0), jnp.where(tril, nt_dot(left_b, ve), 0.0)], axis=1).astype(bf)
            gt = jnp.concatenate([jnp.where(triu, nt_dot(ve, left_a), 0.0), jnp.where(triu, nt_dot(ve, left_b), 0.0)], axis=1).astype(bf)
            after = t_out[p].astype(bf)
            dv = nn_dot(pt, jnp.concatenate([left_a[:, :128], left_b[:, :128]], axis=0)) + nn_dot(kf, after[:, :128])
            dq = nn_dot(gg, jnp.concatenate([kf_a, kf_b], axis=0)) + nt_dot(left, sb_ref[p])
            dk = nn_dot(gt, jnp.concatenate([qn_a, qn_b], axis=0)) + nt_dot(ve, after)
            t_out[p] = t_out[p] + jnp.where(diag, tn_dot(qn, left), 0.0)
            sq = sg_ref[:, lanes].astype(f32)
            sk = sg_ref[:, D + 128 * p:D + 128 * p + 128].astype(f32)
            dm_ref[:, lanes] = ((dq[:, :128] * cos + dq[:, 128:] * sin) * sq).astype(bf)
            dm_ref[:, D + 128 * p:D + 128 * p + 128] = ((dk[:, :128] * cos + dk[:, 128:] * sin) * sk).astype(bf)
            dm_ref[:, 2 * D + 128 * p:2 * D + 128 * p + 128] = dv.astype(bf)
            for j in (p, 6 + p, 12 + p):
                column = slice(128 * j, 128 * j + 128)
                if j in (4, 13):
                    below = (dp_ref[:, 128:256] if j == 4 else dp_ref[:, 512:640]).astype(f32)
                    above = dm_ref[:, column].astype(f32)
                    for g in ((0, 1) if j == 4 else (2, 3)):
                        one, two = (pltpu.roll(above, 64, 1), below) if g & 1 else (above, pltpu.roll(below, 64, 1))
                        mix_ref[g] = jnp.where(lane < 64, one, two).astype(bf)
                        place(mix_ref.at[g], g, 4)
                else:
                    g = sum(j >= first for first in (5, 9, 14))
                    place(dm_ref.at[:, column], g, j - (0, 5, 9, 14)[g])
            if p % 2 == 1:
                for j in (0, D, 2 * D):
                    both = slice(j + 128 * (p - 1), j + 128 * (p + 1))
                    d_state = d_state + nt_dot(dm_ref[:, both], wq_ref[:, both])
        loaded(1)
        ds_ref[...] = d_state.astype(bf)
        send.put(ds_ref, all_o.at[here, :])
        send.finish()

        @pl.when(chunk > 0)
        def _():
            for copy in early(chunk - 1):
                copy.wait()


def backward_opening(delta, n, rows, stages, groups, *refs):
    t, meta, arr = refs[:3]
    cot, cot_v, load_sems, refs = refs[22], refs[30], refs[-1], refs[:-1]
    head, tail = pl.ds((n - 1) * rows, rows), pl.ds(0, (n - 1) * rows)
    loads = [pltpu.make_async_copy(cot.at[part, :], cot_v.at[part, :], load_sems.at[i]) for i, part in enumerate((head, tail))]
    for copy in loads:
        copy.start()
    backward_kernel(delta, n, rows, stages, groups, t, meta, cot_v, arr, *refs[4:11], None, None, *refs[12:22], *refs[23:30],
                    *refs[42:49], *refs[39:42], *refs[49:], loads=loads)


def backward_next(delta, n, rows, stages, groups, *refs):
    t, meta, arr, cot = refs[:4]
    act, act_v, sem, refs = refs[31], refs[47], refs[-1], refs[:-1]
    fill = (t[0] >= 1) & (t[0] <= TILES)
    tile = jnp.clip(t[0] - 1, 0, TILES - 1)
    copy = pltpu.make_async_copy(act.at[tile], act_v.at[tile], sem)

    @pl.when(fill)
    def _():
        copy.start()

    backward_kernel(delta, n, rows, stages, groups, t, meta, cot, arr, *refs[4:11], *refs[15:27], *refs[32:39],
                    *refs[51:58], *refs[48:51], *refs[58:])

    @pl.when(fill)
    def _():
        copy.wait()


def backward_call(rows, n, delta, stages, groups, opening, limit=17):
    V = pl.BlockSpec(memory_space=pltpu.VMEM)
    S = pl.BlockSpec(memory_space=pltpu.SMEM)
    A = pl.BlockSpec(memory_space=pl.ANY)
    sd = jax.ShapeDtypeStruct
    every = n * rows
    made = [((rows, D), bf), ((rows, 4 * D), bf), ((4, rows, 128), bf)]
    saved = [((rows, D), bf), ((rows, 128), f32), ((rows, 4 * D), bf), ((rows, D), bf), ((rows, D), bf), ((rows, D), bf),
             ((rows, 2 * D), bf), ((rows, 2 * D), bf), ((rows, 2 * D), bf), ((PAIRS, 256, 256), bf)]
    own = [((rows, 3 * D), bf), ((rows, D), bf), ((rows, D), bf), ((rows, D), bf)]
    early, saved = saved[:3], saved[3:]
    big = [pltpu.HBM((every, D), bf), pltpu.HBM((TILES, every, TILE), bf), pltpu.HBM((TILES, every, TILE), bf), pltpu.HBM((every, D), bf)]
    if opening:
        aliases = {3 + i: 7 + i for i in range(9)}
    else:
        aliases = {**{3 + i: 7 + i for i in range(12)}, 15: 1, 16: 2, **{27 + i: 3 + i for i in range(4)}}
    return pl.pallas_call(
        functools.partial(backward_opening if opening else backward_next, delta, n, rows, stages, groups),
        in_specs=[S, S] + [V] * 10 + [A] * 11 if opening else [S, S] + [V] * 15 + [A] * 15,
        out_specs=[V] * 3 + [A] * 4 + [V] * 12,
        out_shape=[sd((rows, D), bf), sd((PAIRS, 256, 256), f32), sd((8, D), f32)] + big
        + [pltpu.VMEM(*item) for item in kept_items(every) + early],
        scratch_shapes=[pltpu.VMEM(*item) for item in made + own + saved] + [pltpu.SemaphoreType.DMA((40,)), pltpu.SemaphoreType.DMA((13,))]
        + [pltpu.SemaphoreType.DMA((2,)) if opening else pltpu.SemaphoreType.DMA],
        input_output_aliases=aliases,
        cost_estimate=pl.CostEstimate(flops=rows * 2 * 10 * 10**6, bytes_accessed=4 * 2**20, transcendentals=0),
        compiler_params=pltpu.CompilerParams(vmem_limit_bytes=limit * 2**20),
        name="layer_backward",
    )


HALF = D // 2


def weight_kernel(groups, half, mixed, waits, fetch, ahead, meta_ref, left, *refs):
    raws, refs = refs[:1 + mixed], refs[1 + mixed + waits:]
    sources, refs = refs[:ahead], refs[ahead:]
    keep_o, send_o, refs = refs[0], refs[1], refs[2:]
    kept, refs = refs[:fetch], refs[fetch:]
    targets, refs = refs[:ahead], refs[ahead:]
    turned, out_buf, out_sem, raw_sem, ahead_sem = refs
    me = meta_ref[1]
    share = TILES // groups
    every = raws[0].shape[0]
    raw_copies, later = [], []
    if fetch:
        raw_copies = [pltpu.make_async_copy(raws[0].at[k:k + 256, :], kept[0].at[k:k + 256, :], raw_sem.at[k // 256]) for k in range(0, every, 256)]
        raws = kept
    for source, target in zip(sources, targets):
        step = 1 if len(source.shape) == 3 else every // 4
        for k in range(0, source.shape[0], step):
            later.append(pltpu.make_async_copy(source.at[k:k + step], target.at[k:k + step], ahead_sem.at[len(later)]))
    for copy in raw_copies + later:
        copy.start()
    for j, raw in enumerate(raws):
        for k in range(0, every, 256):
            if fetch:
                raw_copies[k // 256].wait()
            turned[j, :, k:k + 256] = raw[k:k + 256, half * HALF:(half + 1) * HALF].T
    for g in range(groups):
        for i in range(share):
            cols = slice(i * TILE, (i + 1) * TILE)
            value = nn_dot(turned[0], left[g * share + i])
            if mixed and i == share - 1:
                other = nn_dot(turned[1], left[g * share + i])
                lane = lax.broadcasted_iota(jnp.int32, other.shape, 1)
                value = jnp.where(lane < 3 * D // groups - i * TILE, value, other)
            out_buf[g, :, cols] = value.astype(bf)
        rel = g ^ me

        @pl.when((rel & 1) == 0)
        def _():
            pltpu.make_async_copy(out_buf.at[g], keep_o.at[rel >> 1], out_sem).start()

        @pl.when((rel & 1) == 1)
        def _():
            pltpu.make_async_copy(out_buf.at[g], send_o.at[rel >> 1], out_sem).start()
    pltpu.make_async_copy(out_buf, out_buf, out_sem).wait()
    for copy in later:
        copy.wait()


def weight_call(every, groups, half, mixed, waits, fetch, ahead, limit=12):
    V = pl.BlockSpec(memory_space=pltpu.VMEM)
    S = pl.BlockSpec(memory_space=pltpu.SMEM)
    A = pl.BlockSpec(memory_space=pl.ANY)
    raws = 1 + mixed
    return pl.pallas_call(
        functools.partial(weight_kernel, groups, half, mixed, waits, fetch, len(ahead)),
        in_specs=[S, V] + [A if fetch else V] * raws + [A] * (waits + len(ahead)),
        out_specs=[A] * 2 + [V] * (fetch + len(ahead)),
        out_shape=[pltpu.HBM((2, HALF, D), bf)] * 2 + [pltpu.VMEM((every, D), bf)] * fetch + [pltpu.VMEM(shape, bf) for shape in ahead],
        scratch_shapes=[pltpu.VMEM((raws, HALF, every), bf), pltpu.VMEM((groups, HALF, D), bf), pltpu.SemaphoreType.DMA,
                        pltpu.SemaphoreType.DMA((every // 256,)), pltpu.SemaphoreType.DMA((24,))],
        cost_estimate=pl.CostEstimate(flops=2 * every * HALF * 4 * D, bytes_accessed=every * 5 * D * 2, transcendentals=0),
        compiler_params=pltpu.CompilerParams(vmem_limit_bytes=limit * 2**20),
        name="weight_grad",
    )


READY = {2: 0, 3: 1, 4: 2, 5: 3}
MB_ROWS = 1024
MICRO = 2
ROWS = 256
DELTA = 2


def geometry(doc_ids):
    quarter = MB_ROWS // 4
    marks = doc_ids.reshape(-1, MB_ROWS)[:, ::quarter]
    pieces = 1 + jnp.sum((marks[:, 1:] != marks[:, :-1]).astype(jnp.int32), axis=1)
    length = MB_ROWS // pieces
    row = jnp.arange(MB_ROWS, dtype=jnp.int32)
    position = row[None, :] % length[:, None]
    angle = (0.5 * math.pi) * position.astype(f32) / length[:, None].astype(f32)
    angle = angle.reshape(-1, 1)
    starts = jnp.arange(0, MB_ROWS, ROWS, dtype=jnp.int32)
    first = (starts[None, :] % length[:, None]) == 0
    last = ((starts[None, :] + ROWS) % length[:, None]) == 0
    wide = (angle.shape[0], 128)
    return (jnp.broadcast_to(jnp.cos(angle), wide), jnp.broadcast_to(jnp.sin(angle), wide),
            first.reshape(-1).astype(jnp.int32), last.reshape(-1).astype(jnp.int32))


def exchange(block, axis, flip):
    route = [(i, i ^ flip) for i in range(lax.axis_size(axis))]
    return lax.ppermute(block, axis, route)


def add_kernel(*refs):
    total = sum(ref[...].reshape(refs[-1].shape).astype(f32) for ref in refs[:-1])
    refs[-1][...] = total.astype(refs[-1].dtype)


def add_call(slot, keep, got, *more, limit=12):
    rows, columns = keep.shape[1:]
    step = min(rows, 192)
    pick = pl.BlockSpec((1, step, columns), lambda i: (slot, i, 0))
    flat = pl.BlockSpec((step, columns), lambda i: (i, 0))
    return pl.pallas_call(
        add_kernel,
        grid=(rows // step,),
        in_specs=[pick, pick] + [flat] * len(more),
        out_specs=flat,
        out_shape=jax.ShapeDtypeStruct((rows, columns), keep.dtype),
        cost_estimate=pl.CostEstimate(flops=rows * columns * 2, bytes_accessed=rows * columns * 6, transcendentals=0),
        compiler_params=pltpu.CompilerParams(vmem_limit_bytes=limit * 2**20),
        name="add_parts",
    )(keep, got, *more)


def plain_add(*items, limit=12):
    V = pl.BlockSpec(memory_space=pltpu.VMEM)
    return pl.pallas_call(
        add_kernel, in_specs=[V] * len(items), out_specs=V, out_shape=jax.ShapeDtypeStruct(items[0].shape, items[0].dtype),
        cost_estimate=pl.CostEstimate(flops=items[0].size, bytes_accessed=items[0].size * 4, transcendentals=0),
        compiler_params=pltpu.CompilerParams(vmem_limit_bytes=limit * 2**20), name="add_vectors",
    )(*items)


def spread(own, before):
    if lax.axis_size("dp") != 2:
        return lax.psum(own, "dp")
    if before:
        before[-1], own = lax.optimization_barrier((before[-1], own))
    return exchange(own, "dp", 1)


def finished(own, other):
    if lax.axis_size("dp") == 2:
        return own.astype(f32) + other.astype(f32)
    return other.astype(f32)


def local(tokens, doc_ids, cotangent, w_qkv, w_out, w_up, w_down,
          first_gain, first_bias, second_gain, second_bias):
    stages = lax.axis_size("pipe")
    groups = lax.axis_size("group")
    stage = lax.axis_index("pipe").astype(jnp.int32)
    me = lax.axis_index("group").astype(jnp.int32)
    n = tokens.shape[0] // ROWS
    ticks = n + DELTA * (stages - 1)
    cos, sin, first, last = geometry(doc_ids)
    meta = jnp.concatenate([stage[None], me[None], first, last])
    resident = far((tokens,)) + [cos, sin] + far((w_qkv[0], w_out[0], w_up[0], w_down[0]))
    gb = jnp.concatenate([first_gain, first_bias, second_gain, second_bias], axis=0)
    blank = jnp.zeros((ROWS, D), bf)
    arriving = [blank] * DELTA
    resident = resident + [gb]
    state, big = (), ()
    for t in range(ticks):
        made = forward_call(ROWS, n, DELTA, t == 0)(jnp.full((1,), t, jnp.int32), meta, arriving.pop(0), *resident, *state, *big)
        state, big, resident = made[1:2], made[2:16], made[16:]
        route = [(a, a + 1) for a in range(stages - 1) if 0 <= t - a * DELTA < n]
        arriving.append(lax.ppermute(made[0], "pipe", route) if route else made[0])
    block_out, x, att, hb, act, qn, kf, v, sg, n1, gp, n2, rs, sb = big
    arriving = [made[0]] * DELTA
    state, big = (), ()
    for t in range(ticks):
        made = backward_call(ROWS, n, DELTA, stages, groups, t == 0)(
            jnp.full((1,), t, jnp.int32), meta, arriving.pop(0), *resident, *state,
            *far((n2, rs, gp, n1, att, v, qn, kf, sg, sb)), *big, *far([act if t > 0 else cotangent]))
        state, big, resident = made[1:3], made[3:7], made[7:]
        route = [(a, a - 1) for a in range(1, stages) if 0 <= t - (stages - 1 - a) * DELTA < n]
        arriving.append(lax.ppermute(made[0], "pipe", route) if route else made[0])
    df, du, de, input_grad = big
    act = resident[8]
    pieces = [(act, df), (de, x, att), (du, hb)]
    vectors = state[1]
    for flip in (1, 2):
        vectors = plain_add(vectors, exchange(vectors, "group", flip))
    aways, keeps, gots, backs, owns, others = [], [], [], [], [], []

    def turn(k):
        if backs:
            backs[-1], aways[k] = lax.optimization_barrier((backs[-1], aways[k]))
        backs.append(exchange(aways[k], "group", 2))

    for piece in range(3):
        left, *rights = pieces[piece]
        for half in range(2):
            k = len(keeps)
            fetch = k == 0
            ready = READY.get(k)
            waits = [] if ready is None else [aways[ready]]
            call = weight_call(n * ROWS, groups, half, len(rights) == 2, len(waits), fetch, [])
            keep, send, *loads = call(meta, left, *(far(rights) if fetch else rights), *waits)
            rights = loads if fetch else rights
            keeps.append(keep)
            gots.append(exchange(send, "group", 1))
            away = add_call(1, keep, gots[-1])
            if k == 1:
                vectors, away = lax.optimization_barrier((vectors, away))
            aways.append(away)
            turn(k)
    for keep, got, back in zip(keeps, gots, backs):
        own = add_call(0, keep, got, back)
        other = spread(own, others)
        owns.append(own)
        others.append(other)
    parts = [finished(*pair) for pair in zip(owns, others)]
    if lax.axis_size("dp") == 2:
        vectors = plain_add(vectors, exchange(vectors, "dp", 1))
    else:
        vectors = lax.psum(vectors, "dp")
    vectors, me, _ = lax.optimization_barrier((vectors, me, owns[3]))
    mine = lax.dynamic_slice_in_dim(vectors, me * (D // groups), D // groups, axis=1)
    g_down, g_mixed, g_up = (jnp.concatenate(parts[i:i + 2], axis=0) for i in (0, 2, 4))
    odd = (me & 1) == 1
    swap = lambda a, b: jnp.concatenate([g_mixed[:, a], g_mixed[:, b]], axis=1)
    low, one, two, high = slice(0, 512), slice(512, 576), slice(576, 640), slice(640, 768)
    g_qkv = jnp.where(odd, swap(one, low), swap(low, one))
    g_out = jnp.where(odd, swap(two, high), swap(high, two))
    return (block_out[None], input_grad[None], g_qkv[None], g_out[None], g_up[None], g_down.T[None],
            mine[0:1], mine[1:2], mine[2:3], mine[3:4])


def solution(mesh):
    rows = ("group", "dp")
    whole = P("pipe", None, None)
    vector = P("pipe", None)
    return jax.shard_map(
        local,
        mesh=mesh,
        in_specs=(P(rows, None), P(rows), P(rows, None)) + (whole,) * 4 + (vector,) * 4,
        out_specs=(P("pipe", rows, None), P("pipe", rows, None), P("pipe", None, "group"), P("pipe", None, "group"),
                   P("pipe", None, "group"), P("pipe", "group", None)) + (P("pipe", "group"),) * 4,
        check_vma=False,
    )
```

```python
import functools, math
import jax, jax.numpy as jnp
from jax import lax
from jax.experimental import pallas as pl
from jax.experimental.pallas import tpu as pltpu
from jax.sharding import PartitionSpec as P

bf = jnp.bfloat16
f32 = jnp.float32
EPS = 1e-05
D = 768
PAIRS = 6
TILE = 256
TILES = 4 * D // TILE
NT = (((1,), (1,)), ((), ()))
TN = (((0,), (0,)), ((), ()))


def nn_dot(a, b):
    return jnp.dot(a, b, preferred_element_type=f32)


def nt_dot(a, b):
    return lax.dot_general(a, b, NT, preferred_element_type=f32)


def tn_dot(a, b):
    return lax.dot_general(a, b, TN, preferred_element_type=f32)


def head_lanes(rows, lanes):
    lane = lax.broadcasted_iota(jnp.int32, (rows, lanes), 1)
    return (lane & 64) == 0


def block_diag(size):
    r = lax.broadcasted_iota(jnp.int32, (size, size), 0)
    c = lax.broadcasted_iota(jnp.int32, (size, size), 1)
    return ((r ^ c) & 64) == 0


def soft_pair(raw):
    e = jnp.exp(-jnp.abs(raw))
    one = 1.0 + e
    tail = jnp.where(e < 1e-3, e * (1.0 - e * (0.5 - e * (1.0 / 3.0))), jnp.log(one))
    soft = jnp.maximum(raw, 0.0) + tail
    sig = jnp.where(raw >= 0.0, 1.0, e) / one
    return soft, sig


def norm_rows(v):
    centre = jnp.mean(v, axis=-1, keepdims=True)
    centred = v - centre
    spread = jnp.mean(centred * centred, axis=-1, keepdims=True)
    rstd = lax.rsqrt(spread + EPS)
    return centred * rstd, rstd


class Sender:
    def __init__(self, sems):
        self.sems, self.copies = sems, []

    def put(self, src, dst):
        copy = pltpu.make_async_copy(src, dst, self.sems.at[len(self.copies)])
        copy.start()
        self.copies.append(copy)

    def finish(self):
        for copy in self.copies:
            copy.wait()


def forward_kernel(delta, n, rows,
                   t_ref, meta_ref, tok_ref, arr_ref, cos_ref, sin_ref,
                   wq_ref, wo_ref, wu_ref, wd_ref, gb_ref, s_in,
                   y_ref, s_out, all_o, x_o, att_o, hb_o, act_o, qn_o, kf_o, v_o, sg_o, n1_o, gp_o, n2_o, rs_o, sb_o,
                   x_ref, att_ref, hb_ref, act_ref, qn_ref, kf_ref, v_ref, sg_ref, n1_ref, gp_ref, n2_ref, rs_ref, sb_ref, sems, loads=(), final=False):
    stage = meta_ref[0]
    chunk = t_ref[0] - delta * stage
    valid = (chunk >= 0) & (chunk < n)

    def loaded(*which):
        for i in which:
            if loads:
                loads[i].wait()

    @pl.when(jnp.logical_not(valid))
    def _():
        loaded(*range(len(loads)))

    @pl.when(valid)
    def _():
        send = Sender(sems)
        base = pl.multiple_of(chunk * rows, rows)
        here = pl.ds(base, rows)
        first = meta_ref[2 + chunk] != 0
        loaded(0)

        @pl.when(stage == 0)
        def _():
            x_ref[...] = tok_ref[pl.ds(base, rows), :]

        @pl.when(stage != 0)
        def _():
            x_ref[...] = arr_ref[...]

        @pl.when(first)
        def _():
            s_out[...] = jnp.zeros_like(s_out)

        if s_in is not None:
            @pl.when(jnp.logical_not(first))
            def _():
                s_out[...] = s_in[...]

        send.put(x_ref, x_o.at[here, :])
        x = x_ref[...]
        cos = cos_ref[pl.ds(base, rows), :]
        sin = sin_ref[pl.ds(base, rows), :]
        loaded(1)
        q_raw = nn_dot(x, wq_ref[:, 0:D])
        k_raw = nn_dot(x, wq_ref[:, D:2 * D])
        v_ref[...] = nn_dot(x, wq_ref[:, 2 * D:]).astype(bf)
        send.put(v_ref, v_o.at[here, :])
        m_a = head_lanes(rows, 256)
        ri = lax.broadcasted_iota(jnp.int32, (rows, rows), 0)
        ci = lax.broadcasted_iota(jnp.int32, (rows, rows), 1)
        tril = ci <= ri
        diag = block_diag(256)
        ones = jnp.ones((rows, 128), bf)
        zero = jnp.zeros((), bf)
        for p in range(PAIRS):
            lanes = slice(128 * p, 128 * p + 128)
            wide = slice(256 * p, 256 * p + 256)
            q, sq = soft_pair(q_raw[:, lanes])
            k, sk = soft_pair(k_raw[:, lanes])
            qc, qs = q * cos, q * sin
            qf = jnp.concatenate([qc, qs], axis=1).astype(bf)
            kf = jnp.concatenate([k * cos, k * sin], axis=1).astype(bf)
            kf_ref[:, wide] = kf
            sg_ref[:, D + 128 * p:D + 128 * p + 128] = sk.astype(bf)
            ve = jnp.concatenate([v_ref[:, lanes], ones], axis=1)
            s_a = nt_dot(jnp.where(m_a, qf, zero), kf)
            s_b = nt_dot(jnp.where(m_a, zero, qf), kf)
            p_ab = jnp.concatenate([jnp.where(tril, s_a, 0.0), jnp.where(tril, s_b, 0.0)], axis=1).astype(bf)
            ve2 = jnp.concatenate([jnp.where(m_a, ve, zero), jnp.where(m_a, zero, ve)], axis=0)
            before = s_out[p].astype(bf)
            sb_ref[p] = before
            nd = nn_dot(p_ab, ve2) + nn_dot(qf, before)
            inv = 1.0 / nd[:, 128:]
            att_ref[:, lanes] = (nd[:, :128] * inv).astype(bf)
            qn_ref[:, wide] = jnp.concatenate([qc * inv, qs * inv], axis=1).astype(bf)
            sg_ref[:, lanes] = (sq * inv).astype(bf)
            s_out[p] = s_out[p] + jnp.where(diag, tn_dot(kf, ve), 0.0)
        send.put(kf_ref, kf_o.at[here, :])
        send.put(att_ref, att_o.at[here, :])
        send.put(qn_ref, qn_o.at[here, :])
        send.put(sg_ref, sg_o.at[here, :])
        send.put(sb_ref, sb_o.at[chunk])
        loaded(2)
        residual = x.astype(f32) + nn_dot(att_ref[...], wo_ref[...])
        n1, r1 = norm_rows(residual)
        n1_ref[...] = n1.astype(bf)
        hidden = n1 * gb_ref[0:1, :] + gb_ref[1:2, :]
        hb = hidden.astype(bf)
        hb_ref[...] = hb
        send.put(n1_ref, n1_o.at[here, :])
        send.put(hb_ref, hb_o.at[here, :])
        total = hidden
        loaded(3, 4)
        FB = 768
        for j in range(0, 4 * D, FB):
            cols = slice(j, j + FB)
            u = nn_dot(hb, wu_ref[:, cols])
            cdf = 0.5 + 0.5 * lax.erf(u * (1.0 / math.sqrt(2.0)))
            act = (u * cdf).astype(bf)
            act_ref[:, cols] = act
            gp_ref[:, cols] = (cdf + u * (jnp.exp(-0.5 * u * u) * (1.0 / math.sqrt(2.0 * math.pi)))).astype(bf)
            for i in range(j // TILE, (j + FB) // TILE):
                send.put(act_ref.at[:, i * TILE:(i + 1) * TILE], act_o.at[i, here, :])
            send.put(gp_ref.at[:, cols], gp_o.at[here, cols])
            total = total + nn_dot(act, wd_ref[cols, :])
        n2, r2 = norm_rows(total)
        n2_ref[...] = n2.astype(bf)
        lane = lax.broadcasted_iota(jnp.int32, (rows, 128), 1)
        rs_ref[...] = jnp.where(lane < 64, r1, r2)
        y_ref[...] = (n2 * gb_ref[2:3, :] + gb_ref[3:4, :]).astype(bf)
        if final:
            send.put(n2_ref, n2_o.at[here, :])
            send.put(rs_ref, rs_o.at[here, :])
            send.put(y_ref, all_o.at[here, :])
        loaded(5)
        send.finish()


def far(items):
    return [pltpu.with_memory_space_constraint(item, pltpu.HBM) for item in items]


def near(items):
    return [pltpu.with_memory_space_constraint(item, pltpu.VMEM) for item in items]


def forward_opening(delta, n, rows, *refs):
    ins, outs, big, kept, scratch, sems, load_sems = refs[:11], refs[11:15], refs[15:29], refs[29:38], refs[38:49], refs[49], refs[50]
    tok, cos, sin, *weights, gb = ins[3:]
    tok_v, _, _, *weights_v = kept[:7]
    head, tail = pl.ds(0, rows), pl.ds(rows, (n - 1) * rows)
    pairs = [(tok.at[head, :], tok_v.at[head, :])] + list(zip(weights, weights_v)) + [(tok.at[tail, :], tok_v.at[tail, :])]
    loads = [pltpu.make_async_copy(src, dst, load_sems.at[i]) for i, (src, dst) in enumerate(pairs)]
    for copy in loads:
        copy.start()
    forward_kernel(delta, n, rows, *ins[:2], tok_v, ins[2], cos, sin, *weights_v, gb, None, *outs[:2], *big,
                   *scratch[:10], *outs[2:], scratch[10], sems, loads=loads)


def forward_next(delta, n, rows, final, *refs):
    t, meta, arr, tok = refs[:4]
    outs, big, scratch, sems, before_sems = refs[30:34], refs[34:48], refs[57:68], refs[68], refs[69]
    before = t[0] - 1 - delta * meta[0]
    there = pl.ds(pl.multiple_of(jnp.clip(before, 0, n - 1) * rows, rows), rows)
    copies = [pltpu.make_async_copy(src, big[i].at[there, :], before_sems.at[j]) for j, (src, i) in enumerate(zip(refs[13:16], (0, 11, 12)))]
    pending = (before >= 0) & (before < n)

    @pl.when(pending)
    def _():
        for copy in copies:
            copy.start()

    forward_kernel(delta, n, rows, t, meta, tok, arr, *refs[4:11], refs[12], *outs[:2], *big,
                   *scratch[:10], *outs[2:], scratch[10], sems, final=final)

    @pl.when(pending)
    def _():
        for copy in copies:
            copy.wait()


def saved_items(rows):
    return [((rows, D), bf)] * 3 + [((rows, 4 * D), bf), ((rows, 2 * D), bf), ((rows, 2 * D), bf), ((rows, D), bf), ((rows, 2 * D), bf),
                                    ((rows, D), bf), ((rows, 4 * D), bf), ((rows, D), bf), ((rows, 128), f32), ((PAIRS, 256, 256), bf)]


def kept_items(every):
    return [((every, D), bf), ((every, 128), f32), ((every, 128), f32), ((D, 3 * D), bf), ((D, D), bf), ((D, 4 * D), bf), ((4 * D, D), bf),
            ((4, D), f32), ((TILES, every, TILE), bf)]


def forward_call(rows, n, delta, opening, final, limit=17):
    V = pl.BlockSpec(memory_space=pltpu.VMEM)
    S = pl.BlockSpec(memory_space=pltpu.SMEM)
    A = pl.BlockSpec(memory_space=pl.ANY)
    sd = jax.ShapeDtypeStruct
    every = n * rows
    big = [pltpu.HBM((every, D), bf)] + [pltpu.HBM(*item) for item in saved_items(every)]
    big[4] = pltpu.HBM((TILES, every, TILE), bf)
    big[13] = pltpu.HBM((n, PAIRS, 256, 256), bf)
    own = saved_items(rows)
    handed = [sd((rows, D), bf), sd((PAIRS, 256, 256), f32), sd(*own[10]), sd(*own[11])]
    aliases = {4: 19, 5: 20, 10: 25}
    if not opening:
        aliases = {12: 1, **{16 + i: 4 + i for i in range(14)}, **{3 + i: 18 + i for i in range(9)}}
    return pl.pallas_call(
        functools.partial(forward_opening, delta, n, rows) if opening else functools.partial(forward_next, delta, n, rows, final),
        in_specs=[S, S, V, A, V, V, A, A, A, A, V] if opening else [S, S] + [V] * 14 + [A] * 14,
        out_specs=[V] * 4 + [A] * 14 + [V] * 9,
        out_shape=handed + big + [pltpu.VMEM(*item) for item in kept_items(every)],
        scratch_shapes=[pltpu.VMEM(*item) for item in own[:10] + own[12:]]
        + [pltpu.SemaphoreType.DMA((30,)), pltpu.SemaphoreType.DMA((6 if opening else 3,))],
        input_output_aliases=aliases,
        cost_estimate=pl.CostEstimate(flops=rows * 2 * 9 * 10**6, bytes_accessed=4 * 2**20, transcendentals=0),
        compiler_params=pltpu.CompilerParams(vmem_limit_bytes=limit * 2**20),
        name="layer_forward",
    )


def norm_back(grad, normed, rstd, gain):
    scaled = grad * gain
    mean_one = jnp.mean(scaled, axis=-1, keepdims=True)
    mean_two = jnp.mean(scaled * normed, axis=-1, keepdims=True)
    return rstd * (scaled - mean_one - normed * mean_two)


def backward_kernel(delta, n, rows, stages, groups,
                    t_ref, meta_ref, cot_ref, arr_ref, cos_ref, sin_ref,
                    wq_ref, wo_ref, wu_ref, wd_ref, gb_ref, t_in, ga_in,
                    n2_i, rs_i, gp_i, n1_i, att_i, v_i, qn_i, kf_i, sg_i, sb_i,
                    ds_ref, t_out, ga_out, df_o, du_o, de_o, all_o,
                    df_ref, du_ref, mix_ref, dm_ref, da_ref, g_ref, dp_ref,
                    n2_ref, rs_ref, gp_ref, n1_ref, att_ref, v_ref, qn_ref, kf_ref, sg_ref, sb_ref, sems, fetch_sems, loads=()):
    stage = meta_ref[0]
    chunk = n - 1 - t_ref[0] + delta * (stages - 1 - stage)
    valid = (chunk >= 0) & (chunk < n)

    def loaded(*which):
        for i in which:
            if loads:
                loads[i].wait()

    quarters = [slice(j, j + D) for j in range(0, 4 * D, D)]

    def early(which):
        part = pl.ds(pl.multiple_of(which * rows, rows), rows)
        pairs = [(n2_i.at[part, :], n2_ref), (rs_i.at[part, :], rs_ref)] + [(gp_i.at[part, cols], gp_ref.at[:, cols]) for cols in quarters]
        return [pltpu.make_async_copy(src, dst, fetch_sems.at[i]) for i, (src, dst) in enumerate(pairs)]

    @pl.when(chunk == n)
    def _():
        for copy in early(n - 1):
            copy.start()
        for copy in early(n - 1):
            copy.wait()

    @pl.when(jnp.logical_not(valid))
    def _():
        loaded(*range(len(loads)))

    @pl.when(valid)
    def _():
        base = pl.multiple_of(chunk * rows, rows)
        here = pl.ds(base, rows)
        fetched = early(chunk) if loads else []
        for copy in fetched:
            copy.start()
        needed = []
        rest = [(src.at[here, :], dst) for src, dst in ((n1_i, n1_ref), (att_i, att_ref), (v_i, v_ref), (qn_i, qn_ref), (kf_i, kf_ref), (sg_i, sg_ref))]
        for src, dst in rest + [(sb_i.at[chunk], sb_ref)]:
            copy = pltpu.make_async_copy(src, dst, fetch_sems.at[6 + len(needed)])
            copy.start()
            needed.append(copy)
        send = Sender(sems)

        def place(part, g, spot):
            send.put(part, de_o.at[3 * g + spot // 2, here, spot % 2 * 128:spot % 2 * 128 + 128])

        last = meta_ref[2 + n + chunk] != 0

        loaded(0)

        if cot_ref is None:
            g_ref[...] = arr_ref[...]
        else:
            @pl.when(stage == stages - 1)
            def _():
                g_ref[...] = cot_ref[pl.ds(base, rows), :]

            @pl.when(stage != stages - 1)
            def _():
                g_ref[...] = arr_ref[...]

        @pl.when(last)
        def _():
            t_out[...] = jnp.zeros_like(t_out)

        if t_in is not None:
            @pl.when(jnp.logical_not(last))
            def _():
                t_out[...] = t_in[...]

        @pl.when(chunk == n - 1)
        def _():
            ga_out[...] = jnp.zeros_like(ga_out)

        if ga_in is not None:
            @pl.when(chunk != n - 1)
            def _():
                ga_out[...] = ga_in[...]

        g = g_ref[...].astype(f32)
        for copy in fetched:
            copy.wait()
        n2 = n2_ref[...].astype(f32)
        r1 = rs_ref[:, 0:1]
        r2 = rs_ref[:, 64:65]
        ga_out[2:3, :] += jnp.sum(g * n2, axis=0, keepdims=True)
        ga_out[3:4, :] += jnp.sum(g, axis=0, keepdims=True)
        d_two = norm_back(g, n2, r2, gb_ref[2:3, :])
        df = d_two.astype(bf)
        df_ref[...] = df
        send.put(df_ref, df_o.at[here, :])
        total = d_two
        for cols in quarters:
            du = (nt_dot(df, wd_ref[cols, :]) * gp_ref[:, cols].astype(f32)).astype(bf)
            du_ref[:, cols] = du
            for i in range(cols.start // TILE, cols.stop // TILE):
                send.put(du_ref.at[:, i * TILE:(i + 1) * TILE], du_o.at[i, here, :])
            total = total + nt_dot(du, wu_ref[:, cols])
        needed[0].wait()
        n1 = n1_ref[...].astype(f32)
        ga_out[0:1, :] += jnp.sum(total * n1, axis=0, keepdims=True)
        ga_out[1:2, :] += jnp.sum(total, axis=0, keepdims=True)
        d_res = norm_back(total, n1, r1, gb_ref[0:1, :])
        dp = d_res.astype(bf)
        dp_ref[...] = dp
        for g, j in enumerate((0, 2, 3, 5)):
            place(dp_ref.at[:, 128 * j:128 * j + 128], g, 5)

        @pl.when(chunk > 0)
        def _():
            for copy in early(chunk - 1):
                copy.start()

        for copy in needed[1:]:
            copy.wait()
        da_ref[...] = nt_dot(dp, wo_ref[...]).astype(bf)
        cos = cos_ref[pl.ds(base, rows), :]
        sin = sin_ref[pl.ds(base, rows), :]
        m_a = head_lanes(rows, 256)
        lane = lax.broadcasted_iota(jnp.int32, (rows, 128), 1)
        ri = lax.broadcasted_iota(jnp.int32, (rows, rows), 0)
        ci = lax.broadcasted_iota(jnp.int32, (rows, rows), 1)
        tril = ci <= ri
        triu = ri <= ci
        diag = block_diag(256)
        ones = jnp.ones((rows, 128), bf)
        zero = jnp.zeros((), bf)
        d_state = d_res
        for p in range(PAIRS):
            lanes = slice(128 * p, 128 * p + 128)
            wide = slice(256 * p, 256 * p + 256)
            d_o = da_ref[:, lanes]
            prod = d_o.astype(f32) * att_ref[:, lanes].astype(f32)
            in_a = jnp.sum(jnp.where(lane < 64, prod, 0.0), axis=1, keepdims=True)
            in_b = jnp.sum(jnp.where(lane < 64, 0.0, prod), axis=1, keepdims=True)
            inner = jnp.where(lane < 64, -in_a, -in_b)
            high = inner.astype(bf).astype(f32)
            ext = jnp.where((lane & 63) == 0, high, jnp.where((lane & 63) == 1, inner - high, 0.0)).astype(bf)
            left = jnp.concatenate([d_o, ext], axis=1)
            left_a, left_b = jnp.where(m_a, left, zero), jnp.where(m_a, zero, left)
            ve = jnp.concatenate([v_ref[:, lanes], ones], axis=1)
            qn = qn_ref[:, wide]
            kf = kf_ref[:, wide]
            qn_a, qn_b = jnp.where(m_a, qn, zero), jnp.where(m_a, zero, qn)
            kf_a, kf_b = jnp.where(m_a, kf, zero), jnp.where(m_a, zero, kf)
            pt = jnp.concatenate([jnp.where(triu, nt_dot(kf, qn_a), 0.0), jnp.where(triu, nt_dot(kf, qn_b), 0.0)], axis=1).astype(bf)
            gg = jnp.concatenate([jnp.where(tril, nt_dot(left_a, ve), 0.0), jnp.where(tril, nt_dot(left_b, ve), 0.0)], axis=1).astype(bf)
            gt = jnp.concatenate([jnp.where(triu, nt_dot(ve, left_a), 0.0), jnp.where(triu, nt_dot(ve, left_b), 0.0)], axis=1).astype(bf)
            after = t_out[p].astype(bf)
            dv = nn_dot(pt, jnp.concatenate([left_a[:, :128], left_b[:, :128]], axis=0)) + nn_dot(kf, after[:, :128])
            dq = nn_dot(gg, jnp.concatenate([kf_a, kf_b], axis=0)) + nt_dot(left, sb_ref[p])
            dk = nn_dot(gt, jnp.concatenate([qn_a, qn_b], axis=0)) + nt_dot(ve, after)
            t_out[p] = t_out[p] + jnp.where(diag, tn_dot(qn, left), 0.0)
            sq = sg_ref[:, lanes].astype(f32)
            sk = sg_ref[:, D + 128 * p:D + 128 * p + 128].astype(f32)
            dm_ref[:, lanes] = ((dq[:, :128] * cos + dq[:, 128:] * sin) * sq).astype(bf)
            dm_ref[:, D + 128 * p:D + 128 * p + 128] = ((dk[:, :128] * cos + dk[:, 128:] * sin) * sk).astype(bf)
            dm_ref[:, 2 * D + 128 * p:2 * D + 128 * p + 128] = dv.astype(bf)
            for j in (p, 6 + p, 12 + p):
                column = slice(128 * j, 128 * j + 128)
                if j in (4, 13):
                    below = (dp_ref[:, 128:256] if j == 4 else dp_ref[:, 512:640]).astype(f32)
                    above = dm_ref[:, column].astype(f32)
                    for g in ((0, 1) if j == 4 else (2, 3)):
                        one, two = (pltpu.roll(above, 64, 1), below) if g & 1 else (above, pltpu.roll(below, 64, 1))
                        mix_ref[g] = jnp.where(lane < 64, one, two).astype(bf)
                        place(mix_ref.at[g], g, 4)
                else:
                    g = sum(j >= first for first in (5, 9, 14))
                    place(dm_ref.at[:, column], g, j - (0, 5, 9, 14)[g])
            if p % 2 == 1:
                for j in (0, D, 2 * D):
                    both = slice(j + 128 * (p - 1), j + 128 * (p + 1))
                    d_state = d_state + nt_dot(dm_ref[:, both], wq_ref[:, both])
        loaded(1)
        ds_ref[...] = d_state.astype(bf)
        send.put(ds_ref, all_o.at[here, :])
        send.finish()

        @pl.when(chunk > 0)
        def _():
            for copy in early(chunk - 1):
                copy.wait()


def backward_opening(delta, n, rows, stages, groups, *refs):
    t, meta, arr = refs[:3]
    cot, cot_v, load_sems, refs = refs[22], refs[30], refs[-1], refs[:-1]
    head, tail = pl.ds((n - 1) * rows, rows), pl.ds(0, (n - 1) * rows)
    loads = [pltpu.make_async_copy(cot.at[part, :], cot_v.at[part, :], load_sems.at[i]) for i, part in enumerate((head, tail))]
    for copy in loads:
        copy.start()
    backward_kernel(delta, n, rows, stages, groups, t, meta, cot_v, arr, *refs[4:11], None, None, *refs[12:22], *refs[23:30],
                    *refs[42:49], *refs[39:42], *refs[49:], loads=loads)


def backward_next(delta, n, rows, stages, groups, *refs):
    t, meta, arr, cot = refs[:4]
    act, act_v, sem, refs = refs[31], refs[47], refs[-1], refs[:-1]
    fill = (t[0] >= 1) & (t[0] <= TILES)
    tile = jnp.clip(t[0] - 1, 0, TILES - 1)
    copy = pltpu.make_async_copy(act.at[tile], act_v.at[tile], sem)

    @pl.when(fill)
    def _():
        copy.start()

    backward_kernel(delta, n, rows, stages, groups, t, meta, cot, arr, *refs[4:11], *refs[15:27], *refs[32:39],
                    *refs[51:58], *refs[48:51], *refs[58:])

    @pl.when(fill)
    def _():
        copy.wait()


def backward_call(rows, n, delta, stages, groups, opening, limit=17):
    V = pl.BlockSpec(memory_space=pltpu.VMEM)
    S = pl.BlockSpec(memory_space=pltpu.SMEM)
    A = pl.BlockSpec(memory_space=pl.ANY)
    sd = jax.ShapeDtypeStruct
    every = n * rows
    made = [((rows, D), bf), ((rows, 4 * D), bf), ((4, rows, 128), bf)]
    saved = [((rows, D), bf), ((rows, 128), f32), ((rows, 4 * D), bf), ((rows, D), bf), ((rows, D), bf), ((rows, D), bf),
             ((rows, 2 * D), bf), ((rows, 2 * D), bf), ((rows, 2 * D), bf), ((PAIRS, 256, 256), bf)]
    own = [((rows, 3 * D), bf), ((rows, D), bf), ((rows, D), bf), ((rows, D), bf)]
    early, saved = saved[:3], saved[3:]
    big = [pltpu.HBM((every, D), bf), pltpu.HBM((TILES, every, TILE), bf), pltpu.HBM((TILES, every, TILE), bf), pltpu.HBM((every, D), bf)]
    if opening:
        aliases = {3 + i: 7 + i for i in range(9)}
    else:
        aliases = {**{3 + i: 7 + i for i in range(12)}, 15: 1, 16: 2, **{27 + i: 3 + i for i in range(4)}}
    return pl.pallas_call(
        functools.partial(backward_opening if opening else backward_next, delta, n, rows, stages, groups),
        in_specs=[S, S] + [V] * 10 + [A] * 11 if opening else [S, S] + [V] * 15 + [A] * 15,
        out_specs=[V] * 3 + [A] * 4 + [V] * 12,
        out_shape=[sd((rows, D), bf), sd((PAIRS, 256, 256), f32), sd((8, D), f32)] + big
        + [pltpu.VMEM(*item) for item in kept_items(every) + early],
        scratch_shapes=[pltpu.VMEM(*item) for item in made + own + saved] + [pltpu.SemaphoreType.DMA((40,)), pltpu.SemaphoreType.DMA((13,))]
        + [pltpu.SemaphoreType.DMA((2,)) if opening else pltpu.SemaphoreType.DMA],
        input_output_aliases=aliases,
        cost_estimate=pl.CostEstimate(flops=rows * 2 * 10 * 10**6, bytes_accessed=4 * 2**20, transcendentals=0),
        compiler_params=pltpu.CompilerParams(vmem_limit_bytes=limit * 2**20),
        name="layer_backward",
    )


HALF = D // 2


def weight_kernel(groups, half, mixed, waits, fetch, ahead, meta_ref, left, *refs):
    raws, refs = refs[:1 + mixed], refs[1 + mixed + waits:]
    sources, refs = refs[:ahead], refs[ahead:]
    keep_o, send_o, refs = refs[0], refs[1], refs[2:]
    kept, refs = refs[:fetch], refs[fetch:]
    targets, refs = refs[:ahead], refs[ahead:]
    turned, out_buf, out_sem, raw_sem, ahead_sem = refs
    me = meta_ref[1]
    share = TILES // groups
    every = raws[0].shape[0]
    raw_copies, later = [], []
    if fetch:
        raw_copies = [pltpu.make_async_copy(raws[0].at[k:k + 256, :], kept[0].at[k:k + 256, :], raw_sem.at[k // 256]) for k in range(0, every, 256)]
        raws = kept
    for source, target in zip(sources, targets):
        step = 1 if len(source.shape) == 3 else every // 4
        for k in range(0, source.shape[0], step):
            later.append(pltpu.make_async_copy(source.at[k:k + step], target.at[k:k + step], ahead_sem.at[len(later)]))
    for copy in raw_copies + later:
        copy.start()
    for j, raw in enumerate(raws):
        for k in range(0, every, 256):
            if fetch:
                raw_copies[k // 256].wait()
            turned[j, :, k:k + 256] = raw[k:k + 256, half * HALF:(half + 1) * HALF].T
    for g in range(groups):
        for i in range(share):
            cols = slice(i * TILE, (i + 1) * TILE)
            value = nn_dot(turned[0], left[g * share + i])
            if mixed and i == share - 1:
                other = nn_dot(turned[1], left[g * share + i])
                lane = lax.broadcasted_iota(jnp.int32, other.shape, 1)
                value = jnp.where(lane < 3 * D // groups - i * TILE, value, other)
            out_buf[g, :, cols] = value.astype(bf)
        rel = g ^ me

        @pl.when((rel & 1) == 0)
        def _():
            pltpu.make_async_copy(out_buf.at[g], keep_o.at[rel >> 1], out_sem).start()

        @pl.when((rel & 1) == 1)
        def _():
            pltpu.make_async_copy(out_buf.at[g], send_o.at[rel >> 1], out_sem).start()
    pltpu.make_async_copy(out_buf, out_buf, out_sem).wait()
    for copy in later:
        copy.wait()


def weight_call(every, groups, half, mixed, waits, fetch, ahead, limit=12):
    V = pl.BlockSpec(memory_space=pltpu.VMEM)
    S = pl.BlockSpec(memory_space=pltpu.SMEM)
    A = pl.BlockSpec(memory_space=pl.ANY)
    raws = 1 + mixed
    return pl.pallas_call(
        functools.partial(weight_kernel, groups, half, mixed, waits, fetch, len(ahead)),
        in_specs=[S, V] + [A if fetch else V] * raws + [A] * (waits + len(ahead)),
        out_specs=[A] * 2 + [V] * (fetch + len(ahead)),
        out_shape=[pltpu.HBM((2, HALF, D), bf)] * 2 + [pltpu.VMEM((every, D), bf)] * fetch + [pltpu.VMEM(shape, bf) for shape in ahead],
        scratch_shapes=[pltpu.VMEM((raws, HALF, every), bf), pltpu.VMEM((groups, HALF, D), bf), pltpu.SemaphoreType.DMA,
                        pltpu.SemaphoreType.DMA((every // 256,)), pltpu.SemaphoreType.DMA((24,))],
        cost_estimate=pl.CostEstimate(flops=2 * every * HALF * 4 * D, bytes_accessed=every * 5 * D * 2, transcendentals=0),
        compiler_params=pltpu.CompilerParams(vmem_limit_bytes=limit * 2**20),
        name="weight_grad",
    )


READY = {2: 0, 3: 1, 4: 2, 5: 3}
MB_ROWS = 1024
MICRO = 2
ROWS = 256
DELTA = 2


def geometry(doc_ids):
    quarter = MB_ROWS // 4
    marks = doc_ids.reshape(-1, MB_ROWS)[:, ::quarter]
    pieces = 1 + jnp.sum((marks[:, 1:] != marks[:, :-1]).astype(jnp.int32), axis=1)
    length = MB_ROWS // pieces
    row = jnp.arange(MB_ROWS, dtype=jnp.int32)
    position = row[None, :] % length[:, None]
    angle = (0.5 * math.pi) * position.astype(f32) / length[:, None].astype(f32)
    angle = angle.reshape(-1, 1)
    starts = jnp.arange(0, MB_ROWS, ROWS, dtype=jnp.int32)
    first = (starts[None, :] % length[:, None]) == 0
    last = ((starts[None, :] + ROWS) % length[:, None]) == 0
    wide = (angle.shape[0], 128)
    return (jnp.broadcast_to(jnp.cos(angle), wide), jnp.broadcast_to(jnp.sin(angle), wide),
            first.reshape(-1).astype(jnp.int32), last.reshape(-1).astype(jnp.int32))


def exchange(block, axis, flip):
    route = [(i, i ^ flip) for i in range(lax.axis_size(axis))]
    return lax.ppermute(block, axis, route)


def add_kernel(*refs):
    total = sum(ref[...].reshape(refs[-1].shape).astype(f32) for ref in refs[:-1])
    refs[-1][...] = total.astype(refs[-1].dtype)


def add_call(slot, keep, got, *more, limit=12):
    rows, columns = keep.shape[1:]
    step = min(rows, 192)
    pick = pl.BlockSpec((1, step, columns), lambda i: (slot, i, 0))
    flat = pl.BlockSpec((step, columns), lambda i: (i, 0))
    return pl.pallas_call(
        add_kernel,
        grid=(rows // step,),
        in_specs=[pick, pick] + [flat] * len(more),
        out_specs=flat,
        out_shape=jax.ShapeDtypeStruct((rows, columns), keep.dtype),
        cost_estimate=pl.CostEstimate(flops=rows * columns * 2, bytes_accessed=rows * columns * 6, transcendentals=0),
        compiler_params=pltpu.CompilerParams(vmem_limit_bytes=limit * 2**20),
        name="add_parts",
    )(keep, got, *more)


def plain_add(*items, limit=12):
    V = pl.BlockSpec(memory_space=pltpu.VMEM)
    return pl.pallas_call(
        add_kernel, in_specs=[V] * len(items), out_specs=V, out_shape=jax.ShapeDtypeStruct(items[0].shape, items[0].dtype),
        cost_estimate=pl.CostEstimate(flops=items[0].size, bytes_accessed=items[0].size * 4, transcendentals=0),
        compiler_params=pltpu.CompilerParams(vmem_limit_bytes=limit * 2**20), name="add_vectors",
    )(*items)


def spread(own, before):
    if lax.axis_size("dp") != 2:
        return lax.psum(own, "dp")
    if before:
        before[-1], own = lax.optimization_barrier((before[-1], own))
    return exchange(own, "dp", 1)


def finished(own, other):
    if lax.axis_size("dp") == 2:
        return own.astype(f32) + other.astype(f32)
    return other.astype(f32)


def local(tokens, doc_ids, cotangent, w_qkv, w_out, w_up, w_down,
          first_gain, first_bias, second_gain, second_bias):
    stages = lax.axis_size("pipe")
    groups = lax.axis_size("group")
    stage = lax.axis_index("pipe").astype(jnp.int32)
    me = lax.axis_index("group").astype(jnp.int32)
    n = tokens.shape[0] // ROWS
    ticks = n + DELTA * (stages - 1)
    cos, sin, first, last = geometry(doc_ids)
    meta = jnp.concatenate([stage[None], me[None], first, last])
    resident = far((tokens,)) + [cos, sin] + far((w_qkv[0], w_out[0], w_up[0], w_down[0]))
    gb = jnp.concatenate([first_gain, first_bias, second_gain, second_bias], axis=0)
    blank = jnp.zeros((ROWS, D), bf)
    arriving = [blank] * DELTA
    resident = resident + [gb]
    state, big = (), ()
    for t in range(ticks):
        made = forward_call(ROWS, n, DELTA, t == 0, t == ticks - 1)(jnp.full((1,), t, jnp.int32), meta, arriving.pop(0), *resident, *state, *big)
        state, big, resident = [made[1], made[0], made[2], made[3]], made[4:18], made[18:]
        route = [(a, a + 1) for a in range(stages - 1) if 0 <= t - a * DELTA < n]
        arriving.append(lax.ppermute(made[0], "pipe", route) if route else made[0])
    block_out, x, att, hb, act, qn, kf, v, sg, n1, gp, n2, rs, sb = big
    arriving = [made[0]] * DELTA
    state, big = (), ()
    for t in range(ticks):
        made = backward_call(ROWS, n, DELTA, stages, groups, t == 0)(
            jnp.full((1,), t, jnp.int32), meta, arriving.pop(0), *resident, *state,
            *far((n2, rs, gp, n1, att, v, qn, kf, sg, sb)), *big, *far([act if t > 0 else cotangent]))
        state, big, resident = made[1:3], made[3:7], made[7:]
        route = [(a, a - 1) for a in range(1, stages) if 0 <= t - (stages - 1 - a) * DELTA < n]
        arriving.append(lax.ppermute(made[0], "pipe", route) if route else made[0])
    df, du, de, input_grad = big
    act = resident[8]
    pieces = [(act, df), (de, x, att), (du, hb)]
    vectors = state[1]
    for flip in (1, 2):
        vectors = plain_add(vectors, exchange(vectors, "group", flip))
    aways, keeps, gots, backs, owns, others = [], [], [], [], [], []

    def turn(k):
        if backs:
            backs[-1], aways[k] = lax.optimization_barrier((backs[-1], aways[k]))
        backs.append(exchange(aways[k], "group", 2))

    for piece in range(3):
        left, *rights = pieces[piece]
        for half in range(2):
            k = len(keeps)
            fetch = k == 0
            ready = READY.get(k)
            waits = [] if ready is None else [aways[ready]]
            call = weight_call(n * ROWS, groups, half, len(rights) == 2, len(waits), fetch, [])
            keep, send, *loads = call(meta, left, *(far(rights) if fetch else rights), *waits)
            rights = loads if fetch else rights
            keeps.append(keep)
            gots.append(exchange(send, "group", 1))
            away = add_call(1, keep, gots[-1])
            if k == 1:
                vectors, away = lax.optimization_barrier((vectors, away))
            aways.append(away)
            turn(k)
    for keep, got, back in zip(keeps, gots, backs):
        own = add_call(0, keep, got, back)
        other = spread(own, others)
        owns.append(own)
        others.append(other)
    parts = [finished(*pair) for pair in zip(owns, others)]
    if lax.axis_size("dp") == 2:
        vectors = plain_add(vectors, exchange(vectors, "dp", 1))
    else:
        vectors = lax.psum(vectors, "dp")
    vectors, me, _ = lax.optimization_barrier((vectors, me, owns[3]))
    mine = lax.dynamic_slice_in_dim(vectors, me * (D // groups), D // groups, axis=1)
    g_down, g_mixed, g_up = (jnp.concatenate(parts[i:i + 2], axis=0) for i in (0, 2, 4))
    odd = (me & 1) == 1
    swap = lambda a, b: jnp.concatenate([g_mixed[:, a], g_mixed[:, b]], axis=1)
    low, one, two, high = slice(0, 512), slice(512, 576), slice(576, 640), slice(640, 768)
    g_qkv = jnp.where(odd, swap(one, low), swap(low, one))
    g_out = jnp.where(odd, swap(two, high), swap(high, two))
    return (block_out[None], input_grad[None], g_qkv[None], g_out[None], g_up[None], g_down.T[None],
            mine[0:1], mine[1:2], mine[2:3], mine[3:4])


def solution(mesh):
    rows = ("group", "dp")
    whole = P("pipe", None, None)
    vector = P("pipe", None)
    return jax.shard_map(
        local,
        mesh=mesh,
        in_specs=(P(rows, None), P(rows), P(rows, None)) + (whole,) * 4 + (vector,) * 4,
        out_specs=(P("pipe", rows, None), P("pipe", rows, None), P("pipe", None, "group"), P("pipe", None, "group"),
                   P("pipe", None, "group"), P("pipe", "group", None)) + (P("pipe", "group"),) * 4,
        check_vma=False,
    )
```

```python
import functools, math
import jax, jax.numpy as jnp
from jax import lax
from jax.experimental import pallas as pl
from jax.experimental.pallas import tpu as pltpu
from jax.sharding import PartitionSpec as P

bf = jnp.bfloat16
f32 = jnp.float32
EPS = 1e-05
D = 768
PAIRS = 6
TILE = 256
TILES = 4 * D // TILE
NT = (((1,), (1,)), ((), ()))
TN = (((0,), (0,)), ((), ()))


def nn_dot(a, b):
    return jnp.dot(a, b, preferred_element_type=f32)


def nt_dot(a, b):
    return lax.dot_general(a, b, NT, preferred_element_type=f32)


def tn_dot(a, b):
    return lax.dot_general(a, b, TN, preferred_element_type=f32)


def head_lanes(rows, lanes):
    lane = lax.broadcasted_iota(jnp.int32, (rows, lanes), 1)
    return (lane & 64) == 0


def block_diag(size):
    r = lax.broadcasted_iota(jnp.int32, (size, size), 0)
    c = lax.broadcasted_iota(jnp.int32, (size, size), 1)
    return ((r ^ c) & 64) == 0


def soft_pair(raw):
    e = jnp.exp(-jnp.abs(raw))
    one = 1.0 + e
    tail = jnp.where(e < 1e-3, e * (1.0 - e * (0.5 - e * (1.0 / 3.0))), jnp.log(one))
    soft = jnp.maximum(raw, 0.0) + tail
    sig = jnp.where(raw >= 0.0, 1.0, e) / one
    return soft, sig


def norm_rows(v):
    centre = jnp.mean(v, axis=-1, keepdims=True)
    centred = v - centre
    spread = jnp.mean(centred * centred, axis=-1, keepdims=True)
    rstd = lax.rsqrt(spread + EPS)
    return centred * rstd, rstd


class Sender:
    def __init__(self, sems):
        self.sems, self.copies = sems, []

    def put(self, src, dst):
        copy = pltpu.make_async_copy(src, dst, self.sems.at[len(self.copies)])
        copy.start()
        self.copies.append(copy)

    def finish(self):
        for copy in self.copies:
            copy.wait()


def forward_kernel(delta, n, rows,
                   t_ref, meta_ref, tok_ref, arr_ref, cos_ref, sin_ref,
                   wq_ref, wo_ref, wu_ref, wd_ref, gb_ref, s_in,
                   y_ref, s_out, all_o, x_o, att_o, hb_o, act_o, qn_o, kf_o, v_o, sg_o, n1_o, gp_o, n2_o, rs_o, sb_o,
                   x_ref, att_ref, hb_ref, act_ref, qn_ref, kf_ref, v_ref, sg_ref, n1_ref, gp_ref, n2_ref, rs_ref, sb_ref, sems, loads=(), final=False):
    stage = meta_ref[0]
    chunk = t_ref[0] - delta * stage
    valid = (chunk >= 0) & (chunk < n)

    def loaded(*which):
        for i in which:
            if loads:
                loads[i].wait()

    @pl.when(jnp.logical_not(valid))
    def _():
        loaded(*range(len(loads)))

    @pl.when(valid)
    def _():
        send = Sender(sems)
        base = pl.multiple_of(chunk * rows, rows)
        here = pl.ds(base, rows)
        first = meta_ref[2 + chunk] != 0
        loaded(0)

        @pl.when(stage == 0)
        def _():
            x_ref[...] = tok_ref[pl.ds(base, rows), :]

        @pl.when(stage != 0)
        def _():
            x_ref[...] = arr_ref[...]

        @pl.when(first)
        def _():
            s_out[...] = jnp.zeros_like(s_out)

        if s_in is not None:
            @pl.when(jnp.logical_not(first))
            def _():
                s_out[...] = s_in[...]

        send.put(x_ref, x_o.at[here, :])
        x = x_ref[...]
        cos = cos_ref[pl.ds(base, rows), :]
        sin = sin_ref[pl.ds(base, rows), :]
        loaded(1)
        q_raw = nn_dot(x, wq_ref[:, 0:D])
        k_raw = nn_dot(x, wq_ref[:, D:2 * D])
        v_ref[...] = nn_dot(x, wq_ref[:, 2 * D:]).astype(bf)
        send.put(v_ref, v_o.at[here, :])
        m_a = head_lanes(rows, 256)
        ri = lax.broadcasted_iota(jnp.int32, (rows, rows), 0)
        ci = lax.broadcasted_iota(jnp.int32, (rows, rows), 1)
        tril = ci <= ri
        diag = block_diag(256)
        ones = jnp.ones((rows, 128), bf)
        zero = jnp.zeros((), bf)
        for p in range(PAIRS):
            lanes = slice(128 * p, 128 * p + 128)
            wide = slice(256 * p, 256 * p + 256)
            q, sq = soft_pair(q_raw[:, lanes])
            k, sk = soft_pair(k_raw[:, lanes])
            qc, qs = q * cos, q * sin
            qf = jnp.concatenate([qc, qs], axis=1).astype(bf)
            kf = jnp.concatenate([k * cos, k * sin], axis=1).astype(bf)
            kf_ref[:, wide] = kf
            sg_ref[:, D + 128 * p:D + 128 * p + 128] = sk.astype(bf)
            ve = jnp.concatenate([v_ref[:, lanes], ones], axis=1)
            s_a = nt_dot(jnp.where(m_a, qf, zero), kf)
            s_b = nt_dot(jnp.where(m_a, zero, qf), kf)
            p_ab = jnp.concatenate([jnp.where(tril, s_a, 0.0), jnp.where(tril, s_b, 0.0)], axis=1).astype(bf)
            ve2 = jnp.concatenate([jnp.where(m_a, ve, zero), jnp.where(m_a, zero, ve)], axis=0)
            before = s_out[p].astype(bf)
            sb_ref[p] = before
            nd = nn_dot(p_ab, ve2) + nn_dot(qf, before)
            inv = 1.0 / nd[:, 128:]
            att_ref[:, lanes] = (nd[:, :128] * inv).astype(bf)
            qn_ref[:, wide] = jnp.concatenate([qc * inv, qs * inv], axis=1).astype(bf)
            sg_ref[:, lanes] = (sq * inv).astype(bf)
            s_out[p] = s_out[p] + jnp.where(diag, tn_dot(kf, ve), 0.0)
        send.put(kf_ref, kf_o.at[here, :])
        send.put(att_ref, att_o.at[here, :])
        send.put(qn_ref, qn_o.at[here, :])
        send.put(sg_ref, sg_o.at[here, :])
        send.put(sb_ref, sb_o.at[chunk])
        loaded(2)
        residual = x.astype(f32) + nn_dot(att_ref[...], wo_ref[...])
        n1, r1 = norm_rows(residual)
        n1_ref[...] = n1.astype(bf)
        hidden = n1 * gb_ref[0:1, :] + gb_ref[1:2, :]
        hb = hidden.astype(bf)
        hb_ref[...] = hb
        send.put(n1_ref, n1_o.at[here, :])
        send.put(hb_ref, hb_o.at[here, :])
        total = hidden
        loaded(3, 4)
        FB = 768
        for j in range(0, 4 * D, FB):
            cols = slice(j, j + FB)
            u = nn_dot(hb, wu_ref[:, cols])
            cdf = 0.5 + 0.5 * lax.erf(u * (1.0 / math.sqrt(2.0)))
            act = (u * cdf).astype(bf)
            act_ref[:, cols] = act
            gp_ref[:, cols] = (cdf + u * (jnp.exp(-0.5 * u * u) * (1.0 / math.sqrt(2.0 * math.pi)))).astype(bf)
            for i in range(j // TILE, (j + FB) // TILE):
                send.put(act_ref.at[:, i * TILE:(i + 1) * TILE], act_o.at[i, here, :])
            send.put(gp_ref.at[:, cols], gp_o.at[here, cols])
            total = total + nn_dot(act, wd_ref[cols, :])
        n2, r2 = norm_rows(total)
        n2_ref[...] = n2.astype(bf)
        lane = lax.broadcasted_iota(jnp.int32, (rows, 128), 1)
        rs_ref[...] = jnp.where(lane < 64, r1, r2)
        y_ref[...] = (n2 * gb_ref[2:3, :] + gb_ref[3:4, :]).astype(bf)
        if final:
            send.put(n2_ref, n2_o.at[here, :])
            send.put(rs_ref, rs_o.at[here, :])
            send.put(y_ref, all_o.at[here, :])
        loaded(5)
        send.finish()


def far(items):
    return [pltpu.with_memory_space_constraint(item, pltpu.HBM) for item in items]


def near(items):
    return [pltpu.with_memory_space_constraint(item, pltpu.VMEM) for item in items]


def forward_opening(delta, n, rows, *refs):
    ins, outs, big, kept, scratch, sems, load_sems = refs[:11], refs[11:15], refs[15:29], refs[29:38], refs[38:49], refs[49], refs[50]
    tok, cos, sin, *weights, gb = ins[3:]
    tok_v, _, _, *weights_v = kept[:7]
    head, tail = pl.ds(0, rows), pl.ds(rows, (n - 1) * rows)
    pairs = [(tok.at[head, :], tok_v.at[head, :])] + list(zip(weights, weights_v)) + [(tok.at[tail, :], tok_v.at[tail, :])]
    loads = [pltpu.make_async_copy(src, dst, load_sems.at[i]) for i, (src, dst) in enumerate(pairs)]
    for copy in loads:
        copy.start()
    forward_kernel(delta, n, rows, *ins[:2], tok_v, ins[2], cos, sin, *weights_v, gb, None, *outs[:2], *big,
                   *scratch[:10], *outs[2:], scratch[10], sems, loads=loads)


def forward_next(delta, n, rows, final, *refs):
    t, meta, arr, tok = refs[:4]
    outs, big, scratch, sems, before_sems = refs[30:34], refs[34:48], refs[57:68], refs[68], refs[69]
    before = t[0] - 1 - delta * meta[0]
    there = pl.ds(pl.multiple_of(jnp.clip(before, 0, n - 1) * rows, rows), rows)
    copies = [pltpu.make_async_copy(src, big[i].at[there, :], before_sems.at[j]) for j, (src, i) in enumerate(zip(refs[13:16], (0, 11, 12)))]
    pending = (before >= 0) & (before < n)

    @pl.when(pending)
    def _():
        for copy in copies:
            copy.start()

    forward_kernel(delta, n, rows, t, meta, tok, arr, *refs[4:11], refs[12], *outs[:2], *big,
                   *scratch[:10], *outs[2:], scratch[10], sems, final=final)

    @pl.when(pending)
    def _():
        for copy in copies:
            copy.wait()


def saved_items(rows):
    return [((rows, D), bf)] * 3 + [((rows, 4 * D), bf), ((rows, 2 * D), bf), ((rows, 2 * D), bf), ((rows, D), bf), ((rows, 2 * D), bf),
                                    ((rows, D), bf), ((rows, 4 * D), bf), ((rows, D), bf), ((rows, 128), f32), ((PAIRS, 256, 256), bf)]


def kept_items(every):
    return [((every, D), bf), ((every, 128), f32), ((every, 128), f32), ((D, 3 * D), bf), ((D, D), bf), ((D, 4 * D), bf), ((4 * D, D), bf),
            ((4, D), f32), ((TILES, every, TILE), bf)]


def forward_call(rows, n, delta, opening, final, limit=17):
    V = pl.BlockSpec(memory_space=pltpu.VMEM)
    S = pl.BlockSpec(memory_space=pltpu.SMEM)
    A = pl.BlockSpec(memory_space=pl.ANY)
    sd = jax.ShapeDtypeStruct
    every = n * rows
    big = [pltpu.HBM((every, D), bf)] + [pltpu.HBM(*item) for item in saved_items(every)]
    big[4] = pltpu.HBM((TILES, every, TILE), bf)
    big[13] = pltpu.HBM((n, PAIRS, 256, 256), bf)
    own = saved_items(rows)
    handed = [sd((rows, D), bf), sd((PAIRS, 256, 256), f32), sd(*own[10]), sd(*own[11])]
    aliases = {4: 19, 5: 20, 10: 25}
    if not opening:
        aliases = {12: 1, **{16 + i: 4 + i for i in range(14)}, **{3 + i: 18 + i for i in range(9)}}
    return pl.pallas_call(
        functools.partial(forward_opening, delta, n, rows) if opening else functools.partial(forward_next, delta, n, rows, final),
        in_specs=[S, S, V, A, V, V, A, A, A, A, V] if opening else [S, S] + [V] * 14 + [A] * 14,
        out_specs=[V] * 4 + [A] * 14 + [V] * 9,
        out_shape=handed + big + [pltpu.VMEM(*item) for item in kept_items(every)],
        scratch_shapes=[pltpu.VMEM(*item) for item in own[:10] + own[12:]]
        + [pltpu.SemaphoreType.DMA((30,)), pltpu.SemaphoreType.DMA((6 if opening else 3,))],
        input_output_aliases=aliases,
        cost_estimate=pl.CostEstimate(flops=rows * 2 * 9 * 10**6, bytes_accessed=4 * 2**20, transcendentals=0),
        compiler_params=pltpu.CompilerParams(vmem_limit_bytes=limit * 2**20),
        name="layer_forward",
    )


def norm_back(grad, normed, rstd, gain):
    scaled = grad * gain
    mean_one = jnp.mean(scaled, axis=-1, keepdims=True)
    mean_two = jnp.mean(scaled * normed, axis=-1, keepdims=True)
    return rstd * (scaled - mean_one - normed * mean_two)


def backward_kernel(delta, n, rows, stages, groups,
                    t_ref, meta_ref, cot_ref, arr_ref, cos_ref, sin_ref,
                    wq_ref, wo_ref, wu_ref, wd_ref, gb_ref, t_in, ga_in,
                    n2_i, rs_i, gp_i, n1_i, att_i, v_i, qn_i, kf_i, sg_i, sb_i,
                    ds_ref, t_out, ga_out, df_o, du_o, de_o, all_o,
                    df_ref, du_ref, mix_ref, dm_ref, da_ref, g_ref, dp_ref,
                    n2_ref, rs_ref, gp_ref, n1_ref, att_ref, v_ref, qn_ref, kf_ref, sg_ref, sb_ref, sems, fetch_sems, loads=()):
    stage = meta_ref[0]
    chunk = n - 1 - t_ref[0] + delta * (stages - 1 - stage)
    valid = (chunk >= 0) & (chunk < n)

    def loaded(*which):
        for i in which:
            if loads:
                loads[i].wait()

    quarters = [slice(j, j + D) for j in range(0, 4 * D, D)]

    def early(which):
        part = pl.ds(pl.multiple_of(which * rows, rows), rows)
        pairs = [(n2_i.at[part, :], n2_ref), (rs_i.at[part, :], rs_ref)] + [(gp_i.at[part, cols], gp_ref.at[:, cols]) for cols in quarters]
        return [pltpu.make_async_copy(src, dst, fetch_sems.at[i]) for i, (src, dst) in enumerate(pairs)]

    @pl.when(chunk == n)
    def _():
        for copy in early(n - 1):
            copy.start()
        for copy in early(n - 1):
            copy.wait()

    @pl.when(jnp.logical_not(valid))
    def _():
        loaded(*range(len(loads)))

    @pl.when(valid)
    def _():
        base = pl.multiple_of(chunk * rows, rows)
        here = pl.ds(base, rows)
        fetched = early(chunk) if loads else []
        for copy in fetched:
            copy.start()
        needed = []
        rest = [(src.at[here, :], dst) for src, dst in ((n1_i, n1_ref), (att_i, att_ref), (v_i, v_ref), (qn_i, qn_ref), (kf_i, kf_ref), (sg_i, sg_ref))]
        for src, dst in rest + [(sb_i.at[chunk], sb_ref)]:
            copy = pltpu.make_async_copy(src, dst, fetch_sems.at[6 + len(needed)])
            copy.start()
            needed.append(copy)
        send = Sender(sems)

        def place(part, g, spot):
            send.put(part, de_o.at[3 * g + spot // 2, here, spot % 2 * 128:spot % 2 * 128 + 128])

        last = meta_ref[2 + n + chunk] != 0

        loaded(0)

        if cot_ref is None:
            g_ref[...] = arr_ref[...]
        else:
            @pl.when(stage == stages - 1)
            def _():
                g_ref[...] = cot_ref[pl.ds(base, rows), :]

            @pl.when(stage != stages - 1)
            def _():
                g_ref[...] = arr_ref[...]

        @pl.when(last)
        def _():
            t_out[...] = jnp.zeros_like(t_out)

        if t_in is not None:
            @pl.when(jnp.logical_not(last))
            def _():
                t_out[...] = t_in[...]

        @pl.when(chunk == n - 1)
        def _():
            ga_out[...] = jnp.zeros_like(ga_out)

        if ga_in is not None:
            @pl.when(chunk != n - 1)
            def _():
                ga_out[...] = ga_in[...]

        g = g_ref[...].astype(f32)
        for copy in fetched:
            copy.wait()
        n2 = n2_ref[...].astype(f32)
        r1 = rs_ref[:, 0:1]
        r2 = rs_ref[:, 64:65]
        ga_out[2:3, :] += jnp.sum(g * n2, axis=0, keepdims=True)
        ga_out[3:4, :] += jnp.sum(g, axis=0, keepdims=True)
        d_two = norm_back(g, n2, r2, gb_ref[2:3, :])
        df = d_two.astype(bf)
        df_ref[...] = df
        send.put(df_ref, df_o.at[here, :])
        total = d_two
        for cols in quarters:
            du = (nt_dot(df, wd_ref[cols, :]) * gp_ref[:, cols].astype(f32)).astype(bf)
            du_ref[:, cols] = du
            for i in range(cols.start // TILE, cols.stop // TILE):
                send.put(du_ref.at[:, i * TILE:(i + 1) * TILE], du_o.at[i, here, :])
            total = total + nt_dot(du, wu_ref[:, cols])
        needed[0].wait()
        n1 = n1_ref[...].astype(f32)
        ga_out[0:1, :] += jnp.sum(total * n1, axis=0, keepdims=True)
        ga_out[1:2, :] += jnp.sum(total, axis=0, keepdims=True)
        d_res = norm_back(total, n1, r1, gb_ref[0:1, :])
        dp = d_res.astype(bf)
        dp_ref[...] = dp
        for g, j in enumerate((0, 2, 3, 5)):
            place(dp_ref.at[:, 128 * j:128 * j + 128], g, 5)

        @pl.when(chunk > 0)
        def _():
            for copy in early(chunk - 1):
                copy.start()

        for copy in needed[1:]:
            copy.wait()
        da_ref[...] = nt_dot(dp, wo_ref[...]).astype(bf)
        cos = cos_ref[pl.ds(base, rows), :]
        sin = sin_ref[pl.ds(base, rows), :]
        m_a = head_lanes(rows, 256)
        lane = lax.broadcasted_iota(jnp.int32, (rows, 128), 1)
        ri = lax.broadcasted_iota(jnp.int32, (rows, rows), 0)
        ci = lax.broadcasted_iota(jnp.int32, (rows, rows), 1)
        tril = ci <= ri
        triu = ri <= ci
        diag = block_diag(256)
        ones = jnp.ones((rows, 128), bf)
        zero = jnp.zeros((), bf)
        d_state = d_res
        for p in range(PAIRS):
            lanes = slice(128 * p, 128 * p + 128)
            wide = slice(256 * p, 256 * p + 256)
            d_o = da_ref[:, lanes]
            prod = d_o.astype(f32) * att_ref[:, lanes].astype(f32)
            in_a = jnp.sum(jnp.where(lane < 64, prod, 0.0), axis=1, keepdims=True)
            in_b = jnp.sum(jnp.where(lane < 64, 0.0, prod), axis=1, keepdims=True)
            inner = jnp.where(lane < 64, -in_a, -in_b)
            high = inner.astype(bf).astype(f32)
            ext = jnp.where((lane & 63) == 0, high, jnp.where((lane & 63) == 1, inner - high, 0.0)).astype(bf)
            left = jnp.concatenate([d_o, ext], axis=1)
            left_a, left_b = jnp.where(m_a, left, zero), jnp.where(m_a, zero, left)
            ve = jnp.concatenate([v_ref[:, lanes], ones], axis=1)
            qn = qn_ref[:, wide]
            kf = kf_ref[:, wide]
            qn_a, qn_b = jnp.where(m_a, qn, zero), jnp.where(m_a, zero, qn)
            kf_a, kf_b = jnp.where(m_a, kf, zero), jnp.where(m_a, zero, kf)
            pt = jnp.concatenate([jnp.where(triu, nt_dot(kf, qn_a), 0.0), jnp.where(triu, nt_dot(kf, qn_b), 0.0)], axis=1).astype(bf)
            gg = jnp.concatenate([jnp.where(tril, nt_dot(left_a, ve), 0.0), jnp.where(tril, nt_dot(left_b, ve), 0.0)], axis=1).astype(bf)
            gt = jnp.concatenate([jnp.where(triu, nt_dot(ve, left_a), 0.0), jnp.where(triu, nt_dot(ve, left_b), 0.0)], axis=1).astype(bf)
            after = t_out[p].astype(bf)
            dv = nn_dot(pt, jnp.concatenate([left_a[:, :128], left_b[:, :128]], axis=0)) + nn_dot(kf, after[:, :128])
            dq = nn_dot(gg, jnp.concatenate([kf_a, kf_b], axis=0)) + nt_dot(left, sb_ref[p])
            dk = nn_dot(gt, jnp.concatenate([qn_a, qn_b], axis=0)) + nt_dot(ve, after)
            t_out[p] = t_out[p] + jnp.where(diag, tn_dot(qn, left), 0.0)
            sq = sg_ref[:, lanes].astype(f32)
            sk = sg_ref[:, D + 128 * p:D + 128 * p + 128].astype(f32)
            dm_ref[:, lanes] = ((dq[:, :128] * cos + dq[:, 128:] * sin) * sq).astype(bf)
            dm_ref[:, D + 128 * p:D + 128 * p + 128] = ((dk[:, :128] * cos + dk[:, 128:] * sin) * sk).astype(bf)
            dm_ref[:, 2 * D + 128 * p:2 * D + 128 * p + 128] = dv.astype(bf)
            for j in (p, 6 + p, 12 + p):
                column = slice(128 * j, 128 * j + 128)
                if j in (4, 13):
                    below = (dp_ref[:, 128:256] if j == 4 else dp_ref[:, 512:640]).astype(f32)
                    above = dm_ref[:, column].astype(f32)
                    for g in ((0, 1) if j == 4 else (2, 3)):
                        one, two = (pltpu.roll(above, 64, 1), below) if g & 1 else (above, pltpu.roll(below, 64, 1))
                        mix_ref[g] = jnp.where(lane < 64, one, two).astype(bf)
                        place(mix_ref.at[g], g, 4)
                else:
                    g = sum(j >= first for first in (5, 9, 14))
                    place(dm_ref.at[:, column], g, j - (0, 5, 9, 14)[g])
            if p % 2 == 1:
                for j in (0, D, 2 * D):
                    both = slice(j + 128 * (p - 1), j + 128 * (p + 1))
                    d_state = d_state + nt_dot(dm_ref[:, both], wq_ref[:, both])
        loaded(1)
        ds_ref[...] = d_state.astype(bf)
        send.put(ds_ref, all_o.at[here, :])
        send.finish()

        @pl.when(chunk > 0)
        def _():
            for copy in early(chunk - 1):
                copy.wait()


def backward_opening(delta, n, rows, stages, groups, *refs):
    t, meta, arr = refs[:3]
    cot, cot_v, load_sems, refs = refs[22], refs[30], refs[-1], refs[:-1]
    head, tail = pl.ds((n - 1) * rows, rows), pl.ds(0, (n - 1) * rows)
    loads = [pltpu.make_async_copy(cot.at[part, :], cot_v.at[part, :], load_sems.at[i]) for i, part in enumerate((head, tail))]
    for copy in loads:
        copy.start()
    backward_kernel(delta, n, rows, stages, groups, t, meta, cot_v, arr, *refs[4:11], None, None, *refs[12:22], *refs[23:30],
                    *refs[42:49], *refs[39:42], *refs[49:], loads=loads)


def backward_next(delta, n, rows, stages, groups, *refs):
    t, meta, arr, cot = refs[:4]
    act, act_v, sem, refs = refs[31], refs[47], refs[-1], refs[:-1]
    fill = (t[0] >= 1) & (t[0] <= TILES)
    tile = jnp.clip(t[0] - 1, 0, TILES - 1)
    copy = pltpu.make_async_copy(act.at[tile], act_v.at[tile], sem)

    @pl.when(fill)
    def _():
        copy.start()

    backward_kernel(delta, n, rows, stages, groups, t, meta, cot, arr, *refs[4:11], *refs[15:27], *refs[32:39],
                    *refs[51:58], *refs[48:51], *refs[58:])

    @pl.when(fill)
    def _():
        copy.wait()


def backward_call(rows, n, delta, stages, groups, opening, limit=17):
    V = pl.BlockSpec(memory_space=pltpu.VMEM)
    S = pl.BlockSpec(memory_space=pltpu.SMEM)
    A = pl.BlockSpec(memory_space=pl.ANY)
    sd = jax.ShapeDtypeStruct
    every = n * rows
    made = [((rows, D), bf), ((rows, 4 * D), bf), ((4, rows, 128), bf)]
    saved = [((rows, D), bf), ((rows, 128), f32), ((rows, 4 * D), bf), ((rows, D), bf), ((rows, D), bf), ((rows, D), bf),
             ((rows, 2 * D), bf), ((rows, 2 * D), bf), ((rows, 2 * D), bf), ((PAIRS, 256, 256), bf)]
    own = [((rows, 3 * D), bf), ((rows, D), bf), ((rows, D), bf), ((rows, D), bf)]
    early, saved = saved[:3], saved[3:]
    big = [pltpu.HBM((every, D), bf), pltpu.HBM((TILES, every, TILE), bf), pltpu.HBM((TILES, every, TILE), bf), pltpu.HBM((every, D), bf)]
    if opening:
        aliases = {3 + i: 7 + i for i in range(9)}
    else:
        aliases = {**{3 + i: 7 + i for i in range(12)}, 15: 1, 16: 2, **{27 + i: 3 + i for i in range(4)}}
    return pl.pallas_call(
        functools.partial(backward_opening if opening else backward_next, delta, n, rows, stages, groups),
        in_specs=[S, S] + [V] * 10 + [A] * 11 if opening else [S, S] + [V] * 15 + [A] * 15,
        out_specs=[V] * 3 + [A] * 4 + [V] * 12,
        out_shape=[sd((rows, D), bf), sd((PAIRS, 256, 256), f32), sd((8, D), f32)] + big
        + [pltpu.VMEM(*item) for item in kept_items(every) + early],
        scratch_shapes=[pltpu.VMEM(*item) for item in made + own + saved] + [pltpu.SemaphoreType.DMA((40,)), pltpu.SemaphoreType.DMA((13,))]
        + [pltpu.SemaphoreType.DMA((2,)) if opening else pltpu.SemaphoreType.DMA],
        input_output_aliases=aliases,
        cost_estimate=pl.CostEstimate(flops=rows * 2 * 10 * 10**6, bytes_accessed=4 * 2**20, transcendentals=0),
        compiler_params=pltpu.CompilerParams(vmem_limit_bytes=limit * 2**20),
        name="layer_backward",
    )


HALF = D // 2


def weight_kernel(groups, half, mixed, waits, fetch, ahead, meta_ref, left, *refs):
    raws, refs = refs[:1 + mixed], refs[1 + mixed + waits:]
    sources, refs = refs[:ahead], refs[ahead:]
    keep_o, send_o, refs = refs[0], refs[1], refs[2:]
    kept, refs = refs[:fetch], refs[fetch:]
    targets, refs = refs[:ahead], refs[ahead:]
    turned, out_buf, out_sem, raw_sem, ahead_sem = refs
    me = meta_ref[1]
    share = TILES // groups
    every = raws[0].shape[0]
    raw_copies, later = [], []
    if fetch:
        raw_copies = [pltpu.make_async_copy(raws[0].at[k:k + 256, :], kept[0].at[k:k + 256, :], raw_sem.at[k // 256]) for k in range(0, every, 256)]
        raws = kept
    for source, target in zip(sources, targets):
        step = 1 if len(source.shape) == 3 else every // 4
        for k in range(0, source.shape[0], step):
            later.append(pltpu.make_async_copy(source.at[k:k + step], target.at[k:k + step], ahead_sem.at[len(later)]))
    for copy in raw_copies + later:
        copy.start()
    for j, raw in enumerate(raws):
        for k in range(0, every, 256):
            if fetch:
                raw_copies[k // 256].wait()
            turned[j, :, k:k + 256] = raw[k:k + 256, half * HALF:(half + 1) * HALF].T
    for g in range(groups):
        for i in range(share):
            cols = slice(i * TILE, (i + 1) * TILE)
            value = nn_dot(turned[0], left[g * share + i])
            if mixed and i == share - 1:
                other = nn_dot(turned[1], left[g * share + i])
                lane = lax.broadcasted_iota(jnp.int32, other.shape, 1)
                value = jnp.where(lane < 3 * D // groups - i * TILE, value, other)
            out_buf[g, :, cols] = value.astype(bf)
        rel = g ^ me

        @pl.when((rel & 1) == 0)
        def _():
            pltpu.make_async_copy(out_buf.at[g], keep_o.at[rel >> 1], out_sem).start()

        @pl.when((rel & 1) == 1)
        def _():
            pltpu.make_async_copy(out_buf.at[g], send_o.at[rel >> 1], out_sem).start()
    pltpu.make_async_copy(out_buf, out_buf, out_sem).wait()
    for copy in later:
        copy.wait()


def weight_call(every, groups, half, mixed, waits, fetch, ahead, limit=12):
    V = pl.BlockSpec(memory_space=pltpu.VMEM)
    S = pl.BlockSpec(memory_space=pltpu.SMEM)
    A = pl.BlockSpec(memory_space=pl.ANY)
    raws = 1 + mixed
    return pl.pallas_call(
        functools.partial(weight_kernel, groups, half, mixed, waits, fetch, len(ahead)),
        in_specs=[S, V] + [A if fetch else V] * raws + [A] * (waits + len(ahead)),
        out_specs=[A] * 2 + [V] * (fetch + len(ahead)),
        out_shape=[pltpu.HBM((2, HALF, D), bf)] * 2 + [pltpu.VMEM((every, D), bf)] * fetch + [pltpu.VMEM(shape, bf) for shape in ahead],
        scratch_shapes=[pltpu.VMEM((raws, HALF, every), bf), pltpu.VMEM((groups, HALF, D), bf), pltpu.SemaphoreType.DMA,
                        pltpu.SemaphoreType.DMA((every // 256,)), pltpu.SemaphoreType.DMA((24,))],
        cost_estimate=pl.CostEstimate(flops=2 * every * HALF * 4 * D, bytes_accessed=every * 5 * D * 2, transcendentals=0),
        compiler_params=pltpu.CompilerParams(vmem_limit_bytes=limit * 2**20),
        name="weight_grad",
    )


READY = {2: 0, 3: 1, 4: 2, 5: 3}
MB_ROWS = 1024
MICRO = 2
ROWS = 256
DELTA = 2


def geometry(doc_ids):
    quarter = MB_ROWS // 4
    marks = doc_ids.reshape(-1, MB_ROWS)[:, ::quarter]
    pieces = 1 + jnp.sum((marks[:, 1:] != marks[:, :-1]).astype(jnp.int32), axis=1)
    length = MB_ROWS // pieces
    row = jnp.arange(MB_ROWS, dtype=jnp.int32)
    position = row[None, :] % length[:, None]
    angle = (0.5 * math.pi) * position.astype(f32) / length[:, None].astype(f32)
    angle = angle.reshape(-1, 1)
    starts = jnp.arange(0, MB_ROWS, ROWS, dtype=jnp.int32)
    first = (starts[None, :] % length[:, None]) == 0
    last = ((starts[None, :] + ROWS) % length[:, None]) == 0
    wide = (angle.shape[0], 128)
    return (jnp.broadcast_to(jnp.cos(angle), wide), jnp.broadcast_to(jnp.sin(angle), wide),
            first.reshape(-1).astype(jnp.int32), last.reshape(-1).astype(jnp.int32))


def exchange(block, axis, flip):
    route = [(i, i ^ flip) for i in range(lax.axis_size(axis))]
    return lax.ppermute(block, axis, route)


def add_kernel(*refs):
    total = sum(ref[...].reshape(refs[-1].shape).astype(f32) for ref in refs[:-1])
    refs[-1][...] = total.astype(refs[-1].dtype)


def add_call(slot, keep, got, *more, limit=12):
    rows, columns = keep.shape[1:]
    step = min(rows, 192)
    pick = pl.BlockSpec((1, step, columns), lambda i: (slot, i, 0))
    flat = pl.BlockSpec((step, columns), lambda i: (i, 0))
    return pl.pallas_call(
        add_kernel,
        grid=(rows // step,),
        in_specs=[pick, pick] + [flat] * len(more),
        out_specs=flat,
        out_shape=jax.ShapeDtypeStruct((rows, columns), keep.dtype),
        cost_estimate=pl.CostEstimate(flops=rows * columns * 2, bytes_accessed=rows * columns * 6, transcendentals=0),
        compiler_params=pltpu.CompilerParams(vmem_limit_bytes=limit * 2**20),
        name="add_parts",
    )(keep, got, *more)


def plain_add(*items, limit=12):
    V = pl.BlockSpec(memory_space=pltpu.VMEM)
    return pl.pallas_call(
        add_kernel, in_specs=[V] * len(items), out_specs=V, out_shape=jax.ShapeDtypeStruct(items[0].shape, items[0].dtype),
        cost_estimate=pl.CostEstimate(flops=items[0].size, bytes_accessed=items[0].size * 4, transcendentals=0),
        compiler_params=pltpu.CompilerParams(vmem_limit_bytes=limit * 2**20), name="add_vectors",
    )(*items)


def spread(own, before):
    if lax.axis_size("dp") != 2:
        return lax.psum(own, "dp")
    if before:
        before[-1], own = lax.optimization_barrier((before[-1], own))
    return exchange(own, "dp", 1)


def finished(own, other):
    if lax.axis_size("dp") == 2:
        return own.astype(f32) + other.astype(f32)
    return other.astype(f32)


def local(tokens, doc_ids, cotangent, w_qkv, w_out, w_up, w_down,
          first_gain, first_bias, second_gain, second_bias):
    stages = lax.axis_size("pipe")
    groups = lax.axis_size("group")
    stage = lax.axis_index("pipe").astype(jnp.int32)
    me = lax.axis_index("group").astype(jnp.int32)
    n = tokens.shape[0] // ROWS
    ticks = n + DELTA * (stages - 1)
    cos, sin, first, last = geometry(doc_ids)
    meta = jnp.concatenate([stage[None], me[None], first, last])
    resident = far((tokens,)) + [cos, sin] + far((w_qkv[0], w_out[0], w_up[0], w_down[0]))
    gb = jnp.concatenate([first_gain, first_bias, second_gain, second_bias], axis=0)
    blank = jnp.zeros((ROWS, D), bf)
    arriving = [blank] * DELTA
    resident = resident + [gb]
    state, big = (), ()
    for t in range(ticks):
        made = forward_call(ROWS, n, DELTA, t == 0, t == ticks - 1)(jnp.full((1,), t, jnp.int32), meta, arriving.pop(0), *resident, *state, *big)
        state, big, resident = [made[1], made[0], made[2], made[3]], made[4:18], made[18:]
        route = [(a, a + 1) for a in range(stages - 1) if 0 <= t - a * DELTA < n]
        arriving.append(lax.ppermute(made[0], "pipe", route) if route else made[0])
    block_out, x, att, hb, act, qn, kf, v, sg, n1, gp, n2, rs, sb = big
    arriving = [made[0]] * DELTA
    state, big = (), ()
    for t in range(ticks):
        made = backward_call(ROWS, n, DELTA, stages, groups, t == 0)(
            jnp.full((1,), t, jnp.int32), meta, arriving.pop(0), *resident, *state,
            *far((n2, rs, gp, n1, att, v, qn, kf, sg, sb)), *big, *far([act if t > 0 else cotangent]))
        state, big, resident = made[1:3], made[3:7], made[7:]
        route = [(a, a - 1) for a in range(1, stages) if 0 <= t - (stages - 1 - a) * DELTA < n]
        arriving.append(lax.ppermute(made[0], "pipe", route) if route else made[0])
    df, du, de, input_grad = big
    act = resident[8]
    pieces = [(act, df), (de, x, att), (du, hb)]
    vectors = state[1]
    for flip in (1, 2):
        vectors = plain_add(vectors, exchange(vectors, "group", flip))
    aways, keeps, gots, backs, owns, others = [], [], [], [], [], []

    def turn(k):
        if backs:
            backs[-1], aways[k] = lax.optimization_barrier((backs[-1], aways[k]))
        backs.append(exchange(aways[k], "group", 2))

    for piece in range(3):
        left, *rights = pieces[piece]
        for half in range(2):
            k = len(keeps)
            fetch = k == 0
            ready = READY.get(k)
            waits = [] if ready is None else [aways[ready]]
            call = weight_call(n * ROWS, groups, half, len(rights) == 2, len(waits), fetch, [])
            keep, send, *loads = call(meta, left, *(far(rights) if fetch else rights), *waits)
            rights = loads if fetch else rights
            keeps.append(keep)
            gots.append(exchange(send, "group", 1))
            away = add_call(1, keep, gots[-1])
            if k in (1, 5):
                vectors, away = lax.optimization_barrier((vectors, away))
            aways.append(away)
            turn(k)
    for keep, got, back in zip(keeps, gots, backs):
        own = add_call(0, keep, got, back)
        other = spread(own, others)
        owns.append(own)
        others.append(other)
    parts = [finished(*pair) for pair in zip(owns, others)]
    if lax.axis_size("dp") == 2:
        vectors = plain_add(vectors, exchange(vectors, "dp", 1))
    else:
        vectors = lax.psum(vectors, "dp")
    vectors, me, _ = lax.optimization_barrier((vectors, me, owns[3]))
    mine = lax.dynamic_slice_in_dim(vectors, me * (D // groups), D // groups, axis=1)
    g_down, g_mixed, g_up = (jnp.concatenate(parts[i:i + 2], axis=0) for i in (0, 2, 4))
    odd = (me & 1) == 1
    swap = lambda a, b: jnp.concatenate([g_mixed[:, a], g_mixed[:, b]], axis=1)
    low, one, two, high = slice(0, 512), slice(512, 576), slice(576, 640), slice(640, 768)
    g_qkv = jnp.where(odd, swap(one, low), swap(low, one))
    g_out = jnp.where(odd, swap(two, high), swap(high, two))
    return (block_out[None], input_grad[None], g_qkv[None], g_out[None], g_up[None], g_down.T[None],
            mine[0:1], mine[1:2], mine[2:3], mine[3:4])


def solution(mesh):
    rows = ("group", "dp")
    whole = P("pipe", None, None)
    vector = P("pipe", None)
    return jax.shard_map(
        local,
        mesh=mesh,
        in_specs=(P(rows, None), P(rows), P(rows, None)) + (whole,) * 4 + (vector,) * 4,
        out_specs=(P("pipe", rows, None), P("pipe", rows, None), P("pipe", None, "group"), P("pipe", None, "group"),
                   P("pipe", None, "group"), P("pipe", "group", None)) + (P("pipe", "group"),) * 4,
        check_vma=False,
    )
```

```python
import functools, math
import jax, jax.numpy as jnp
from jax import lax
from jax.experimental import pallas as pl
from jax.experimental.pallas import tpu as pltpu
from jax.sharding import PartitionSpec as P

bf = jnp.bfloat16
f32 = jnp.float32
EPS = 1e-05
D = 768
PAIRS = 6
TILE = 256
TILES = 4 * D // TILE
NT = (((1,), (1,)), ((), ()))
TN = (((0,), (0,)), ((), ()))


def nn_dot(a, b):
    return jnp.dot(a, b, preferred_element_type=f32)


def nt_dot(a, b):
    return lax.dot_general(a, b, NT, preferred_element_type=f32)


def tn_dot(a, b):
    return lax.dot_general(a, b, TN, preferred_element_type=f32)


def head_lanes(rows, lanes):
    lane = lax.broadcasted_iota(jnp.int32, (rows, lanes), 1)
    return (lane & 64) == 0


def block_diag(size):
    r = lax.broadcasted_iota(jnp.int32, (size, size), 0)
    c = lax.broadcasted_iota(jnp.int32, (size, size), 1)
    return ((r ^ c) & 64) == 0


def soft_pair(raw):
    e = jnp.exp(-jnp.abs(raw))
    one = 1.0 + e
    tail = jnp.where(e < 1e-3, e * (1.0 - e * (0.5 - e * (1.0 / 3.0))), jnp.log(one))
    soft = jnp.maximum(raw, 0.0) + tail
    sig = jnp.where(raw >= 0.0, 1.0, e) / one
    return soft, sig


def norm_rows(v):
    centre = jnp.mean(v, axis=-1, keepdims=True)
    centred = v - centre
    spread = jnp.mean(centred * centred, axis=-1, keepdims=True)
    rstd = lax.rsqrt(spread + EPS)
    return centred * rstd, rstd


class Sender:
    def __init__(self, sems):
        self.sems, self.copies = sems, []

    def put(self, src, dst):
        copy = pltpu.make_async_copy(src, dst, self.sems.at[len(self.copies)])
        copy.start()
        self.copies.append(copy)

    def finish(self):
        for copy in self.copies:
            copy.wait()


def forward_kernel(delta, n, rows,
                   t_ref, meta_ref, tok_ref, arr_ref, cos_ref, sin_ref,
                   wq_ref, wo_ref, wu_ref, wd_ref, gb_ref, s_in,
                   y_ref, s_out, all_o, x_o, att_o, hb_o, act_o, qn_o, kf_o, v_o, sg_o, n1_o, gp_o, n2_o, rs_o, sb_o,
                   x_ref, att_ref, hb_ref, act_ref, qn_ref, kf_ref, v_ref, sg_ref, n1_ref, gp_ref, n2_ref, rs_ref, sb_ref, sems, loads=(), final=False):
    stage = meta_ref[0]
    chunk = t_ref[0] - delta * stage
    valid = (chunk >= 0) & (chunk < n)

    def loaded(*which):
        for i in which:
            if loads:
                loads[i].wait()

    @pl.when(jnp.logical_not(valid))
    def _():
        loaded(*range(len(loads)))

    @pl.when(valid)
    def _():
        send = Sender(sems)
        base = pl.multiple_of(chunk * rows, rows)
        here = pl.ds(base, rows)
        first = meta_ref[2 + chunk] != 0
        loaded(0)

        @pl.when(stage == 0)
        def _():
            x_ref[...] = tok_ref[pl.ds(base, rows), :]

        @pl.when(stage != 0)
        def _():
            x_ref[...] = arr_ref[...]

        @pl.when(first)
        def _():
            s_out[...] = jnp.zeros_like(s_out)

        if s_in is not None:
            @pl.when(jnp.logical_not(first))
            def _():
                s_out[...] = s_in[...]

        send.put(x_ref, x_o.at[here, :])
        x = x_ref[...]
        cos = cos_ref[pl.ds(base, rows), :]
        sin = sin_ref[pl.ds(base, rows), :]
        loaded(1)
        q_raw = nn_dot(x, wq_ref[:, 0:D])
        k_raw = nn_dot(x, wq_ref[:, D:2 * D])
        v_ref[...] = nn_dot(x, wq_ref[:, 2 * D:]).astype(bf)
        send.put(v_ref, v_o.at[here, :])
        m_a = head_lanes(rows, 256)
        ri = lax.broadcasted_iota(jnp.int32, (rows, rows), 0)
        ci = lax.broadcasted_iota(jnp.int32, (rows, rows), 1)
        tril = ci <= ri
        diag = block_diag(256)
        ones = jnp.ones((rows, 128), bf)
        zero = jnp.zeros((), bf)
        for p in range(PAIRS):
            lanes = slice(128 * p, 128 * p + 128)
            wide = slice(256 * p, 256 * p + 256)
            q, sq = soft_pair(q_raw[:, lanes])
            k, sk = soft_pair(k_raw[:, lanes])
            qc, qs = q * cos, q * sin
            qf = jnp.concatenate([qc, qs], axis=1).astype(bf)
            kf = jnp.concatenate([k * cos, k * sin], axis=1).astype(bf)
            kf_ref[:, wide] = kf
            sg_ref[:, D + 128 * p:D + 128 * p + 128] = sk.astype(bf)
            ve = jnp.concatenate([v_ref[:, lanes], ones], axis=1)
            s_a = nt_dot(jnp.where(m_a, qf, zero), kf)
            s_b = nt_dot(jnp.where(m_a, zero, qf), kf)
            p_ab = jnp.concatenate([jnp.where(tril, s_a, 0.0), jnp.where(tril, s_b, 0.0)], axis=1).astype(bf)
            ve2 = jnp.concatenate([jnp.where(m_a, ve, zero), jnp.where(m_a, zero, ve)], axis=0)
            before = s_out[p].astype(bf)
            sb_ref[p] = before
            nd = nn_dot(p_ab, ve2) + nn_dot(qf, before)
            inv = 1.0 / nd[:, 128:]
            att_ref[:, lanes] = (nd[:, :128] * inv).astype(bf)
            qn_ref[:, wide] = jnp.concatenate([qc * inv, qs * inv], axis=1).astype(bf)
            sg_ref[:, lanes] = (sq * inv).astype(bf)
            s_out[p] = s_out[p] + jnp.where(diag, tn_dot(kf, ve), 0.0)
        send.put(kf_ref, kf_o.at[here, :])
        send.put(att_ref, att_o.at[here, :])
        send.put(qn_ref, qn_o.at[here, :])
        send.put(sg_ref, sg_o.at[here, :])
        send.put(sb_ref, sb_o.at[chunk])
        loaded(2)
        residual = x.astype(f32) + nn_dot(att_ref[...], wo_ref[...])
        n1, r1 = norm_rows(residual)
        n1_ref[...] = n1.astype(bf)
        hidden = n1 * gb_ref[0:1, :] + gb_ref[1:2, :]
        hb = hidden.astype(bf)
        hb_ref[...] = hb
        send.put(n1_ref, n1_o.at[here, :])
        send.put(hb_ref, hb_o.at[here, :])
        total = hidden
        loaded(3, 4)
        FB = 768
        for j in range(0, 4 * D, FB):
            cols = slice(j, j + FB)
            u = nn_dot(hb, wu_ref[:, cols])
            cdf = 0.5 + 0.5 * lax.erf(u * (1.0 / math.sqrt(2.0)))
            act = (u * cdf).astype(bf)
            act_ref[:, cols] = act
            gp_ref[:, cols] = (cdf + u * (jnp.exp(-0.5 * u * u) * (1.0 / math.sqrt(2.0 * math.pi)))).astype(bf)
            for i in range(j // TILE, (j + FB) // TILE):
                send.put(act_ref.at[:, i * TILE:(i + 1) * TILE], act_o.at[i, here, :])
            send.put(gp_ref.at[:, cols], gp_o.at[here, cols])
            total = total + nn_dot(act, wd_ref[cols, :])
        n2, r2 = norm_rows(total)
        n2_ref[...] = n2.astype(bf)
        lane = lax.broadcasted_iota(jnp.int32, (rows, 128), 1)
        rs_ref[...] = jnp.where(lane < 64, r1, r2)
        y_ref[...] = (n2 * gb_ref[2:3, :] + gb_ref[3:4, :]).astype(bf)
        if final:
            send.put(n2_ref, n2_o.at[here, :])
            send.put(rs_ref, rs_o.at[here, :])
            send.put(y_ref, all_o.at[here, :])
        loaded(5)
        send.finish()


def far(items):
    return [pltpu.with_memory_space_constraint(item, pltpu.HBM) for item in items]


def near(items):
    return [pltpu.with_memory_space_constraint(item, pltpu.VMEM) for item in items]


def forward_opening(delta, n, rows, *refs):
    ins, outs, big, kept, scratch, sems, load_sems = refs[:11], refs[11:15], refs[15:29], refs[29:38], refs[38:49], refs[49], refs[50]
    tok, cos, sin, *weights, gb = ins[3:]
    tok_v, _, _, *weights_v = kept[:7]
    head, tail = pl.ds(0, rows), pl.ds(rows, (n - 1) * rows)
    pairs = [(tok.at[head, :], tok_v.at[head, :])] + list(zip(weights, weights_v)) + [(tok.at[tail, :], tok_v.at[tail, :])]
    loads = [pltpu.make_async_copy(src, dst, load_sems.at[i]) for i, (src, dst) in enumerate(pairs)]
    for copy in loads:
        copy.start()
    forward_kernel(delta, n, rows, *ins[:2], tok_v, ins[2], cos, sin, *weights_v, gb, None, *outs[:2], *big,
                   *scratch[:10], *outs[2:], scratch[10], sems, loads=loads)


def forward_next(delta, n, rows, final, *refs):
    t, meta, arr, tok = refs[:4]
    outs, big, scratch, sems, before_sems = refs[30:34], refs[34:48], refs[57:68], refs[68], refs[69]
    before = t[0] - 1 - delta * meta[0]
    there = pl.ds(pl.multiple_of(jnp.clip(before, 0, n - 1) * rows, rows), rows)
    copies = [pltpu.make_async_copy(src, big[i].at[there, :], before_sems.at[j]) for j, (src, i) in enumerate(zip(refs[13:16], (0, 11, 12)))]
    pending = (before >= 0) & (before < n)

    @pl.when(pending)
    def _():
        for copy in copies:
            copy.start()

    forward_kernel(delta, n, rows, t, meta, tok, arr, *refs[4:11], refs[12], *outs[:2], *big,
                   *scratch[:10], *outs[2:], scratch[10], sems, final=final)

    @pl.when(pending)
    def _():
        for copy in copies:
            copy.wait()


def saved_items(rows):
    return [((rows, D), bf)] * 3 + [((rows, 4 * D), bf), ((rows, 2 * D), bf), ((rows, 2 * D), bf), ((rows, D), bf), ((rows, 2 * D), bf),
                                    ((rows, D), bf), ((rows, 4 * D), bf), ((rows, D), bf), ((rows, 128), f32), ((PAIRS, 256, 256), bf)]


def kept_items(every):
    return [((every, D), bf), ((every, 128), f32), ((every, 128), f32), ((D, 3 * D), bf), ((D, D), bf), ((D, 4 * D), bf), ((4 * D, D), bf),
            ((4, D), f32), ((TILES, every, TILE), bf)]


def forward_call(rows, n, delta, opening, final, limit=17):
    V = pl.BlockSpec(memory_space=pltpu.VMEM)
    S = pl.BlockSpec(memory_space=pltpu.SMEM)
    A = pl.BlockSpec(memory_space=pl.ANY)
    sd = jax.ShapeDtypeStruct
    every = n * rows
    big = [pltpu.HBM((every, D), bf)] + [pltpu.HBM(*item) for item in saved_items(every)]
    big[4] = pltpu.HBM((TILES, every, TILE), bf)
    big[13] = pltpu.HBM((n, PAIRS, 256, 256), bf)
    own = saved_items(rows)
    handed = [sd((rows, D), bf), sd((PAIRS, 256, 256), f32), sd(*own[10]), sd(*own[11])]
    aliases = {4: 19, 5: 20, 10: 25}
    if not opening:
        aliases = {12: 1, **{16 + i: 4 + i for i in range(14)}, **{3 + i: 18 + i for i in range(9)}}
    return pl.pallas_call(
        functools.partial(forward_opening, delta, n, rows) if opening else functools.partial(forward_next, delta, n, rows, final),
        in_specs=[S, S, V, A, V, V, A, A, A, A, V] if opening else [S, S] + [V] * 14 + [A] * 14,
        out_specs=[V] * 4 + [A] * 14 + [V] * 9,
        out_shape=handed + big + [pltpu.VMEM(*item) for item in kept_items(every)],
        scratch_shapes=[pltpu.VMEM(*item) for item in own[:10] + own[12:]]
        + [pltpu.SemaphoreType.DMA((30,)), pltpu.SemaphoreType.DMA((6 if opening else 3,))],
        input_output_aliases=aliases,
        cost_estimate=pl.CostEstimate(flops=rows * 2 * 9 * 10**6, bytes_accessed=4 * 2**20, transcendentals=0),
        compiler_params=pltpu.CompilerParams(vmem_limit_bytes=limit * 2**20),
        name="layer_forward",
    )


def norm_back(grad, normed, rstd, gain):
    scaled = grad * gain
    mean_one = jnp.mean(scaled, axis=-1, keepdims=True)
    mean_two = jnp.mean(scaled * normed, axis=-1, keepdims=True)
    return rstd * (scaled - mean_one - normed * mean_two)


def backward_kernel(delta, n, rows, stages, groups,
                    t_ref, meta_ref, cot_ref, arr_ref, cos_ref, sin_ref,
                    wq_ref, wo_ref, wu_ref, wd_ref, gb_ref, t_in, ga_in,
                    n2_i, rs_i, gp_i, n1_i, att_i, v_i, qn_i, kf_i, sg_i, sb_i,
                    ds_ref, t_out, ga_out, df_o, du_o, de_o, all_o,
                    df_ref, du_ref, mix_ref, dm_ref, da_ref, g_ref, dp_ref,
                    n2_ref, rs_ref, gp_ref, n1_ref, att_ref, v_ref, qn_ref, kf_ref, sg_ref, sb_ref, sems, fetch_sems, loads=()):
    stage = meta_ref[0]
    chunk = n - 1 - t_ref[0] + delta * (stages - 1 - stage)
    valid = (chunk >= 0) & (chunk < n)

    def loaded(*which):
        for i in which:
            if loads:
                loads[i].wait()

    quarters = [slice(j, j + D) for j in range(0, 4 * D, D)]

    def early(which):
        part = pl.ds(pl.multiple_of(which * rows, rows), rows)
        pairs = [(n2_i.at[part, :], n2_ref), (rs_i.at[part, :], rs_ref)] + [(gp_i.at[part, cols], gp_ref.at[:, cols]) for cols in quarters]
        return [pltpu.make_async_copy(src, dst, fetch_sems.at[i]) for i, (src, dst) in enumerate(pairs)]

    @pl.when(chunk == n)
    def _():
        for copy in early(n - 1):
            copy.start()
        for copy in early(n - 1):
            copy.wait()

    @pl.when(jnp.logical_not(valid))
    def _():
        loaded(*range(len(loads)))

    @pl.when(valid)
    def _():
        base = pl.multiple_of(chunk * rows, rows)
        here = pl.ds(base, rows)
        fetched = early(chunk) if loads else []
        for copy in fetched:
            copy.start()
        needed = []
        rest = [(src.at[here, :], dst) for src, dst in ((n1_i, n1_ref), (att_i, att_ref), (v_i, v_ref), (qn_i, qn_ref), (kf_i, kf_ref), (sg_i, sg_ref))]
        for src, dst in rest + [(sb_i.at[chunk], sb_ref)]:
            copy = pltpu.make_async_copy(src, dst, fetch_sems.at[6 + len(needed)])
            copy.start()
            needed.append(copy)
        send = Sender(sems)

        def place(part, g, spot):
            send.put(part, de_o.at[3 * g + spot // 2, here, spot % 2 * 128:spot % 2 * 128 + 128])

        last = meta_ref[2 + n + chunk] != 0

        loaded(0)

        if cot_ref is None:
            g_ref[...] = arr_ref[...]
        else:
            @pl.when(stage == stages - 1)
            def _():
                g_ref[...] = cot_ref[pl.ds(base, rows), :]

            @pl.when(stage != stages - 1)
            def _():
                g_ref[...] = arr_ref[...]

        @pl.when(last)
        def _():
            t_out[...] = jnp.zeros_like(t_out)

        if t_in is not None:
            @pl.when(jnp.logical_not(last))
            def _():
                t_out[...] = t_in[...]

        @pl.when(chunk == n - 1)
        def _():
            ga_out[...] = jnp.zeros_like(ga_out)

        if ga_in is not None:
            @pl.when(chunk != n - 1)
            def _():
                ga_out[...] = ga_in[...]

        g = g_ref[...].astype(f32)
        for copy in fetched:
            copy.wait()
        n2 = n2_ref[...].astype(f32)
        r1 = rs_ref[:, 0:1]
        r2 = rs_ref[:, 64:65]
        ga_out[2:3, :] += jnp.sum(g * n2, axis=0, keepdims=True)
        ga_out[3:4, :] += jnp.sum(g, axis=0, keepdims=True)
        d_two = norm_back(g, n2, r2, gb_ref[2:3, :])
        df = d_two.astype(bf)
        df_ref[...] = df
        send.put(df_ref, df_o.at[here, :])
        total = d_two
        for cols in quarters:
            du = (nt_dot(df, wd_ref[cols, :]) * gp_ref[:, cols].astype(f32)).astype(bf)
            du_ref[:, cols] = du
            for i in range(cols.start // TILE, cols.stop // TILE):
                send.put(du_ref.at[:, i * TILE:(i + 1) * TILE], du_o.at[i, here, :])
            total = total + nt_dot(du, wu_ref[:, cols])
        needed[0].wait()
        n1 = n1_ref[...].astype(f32)
        ga_out[0:1, :] += jnp.sum(total * n1, axis=0, keepdims=True)
        ga_out[1:2, :] += jnp.sum(total, axis=0, keepdims=True)
        d_res = norm_back(total, n1, r1, gb_ref[0:1, :])
        dp = d_res.astype(bf)
        dp_ref[...] = dp
        for g, j in enumerate((0, 2, 3, 5)):
            place(dp_ref.at[:, 128 * j:128 * j + 128], g, 5)

        @pl.when(chunk > 0)
        def _():
            for copy in early(chunk - 1):
                copy.start()

        for copy in needed[1:]:
            copy.wait()
        da_ref[...] = nt_dot(dp, wo_ref[...]).astype(bf)
        cos = cos_ref[pl.ds(base, rows), :]
        sin = sin_ref[pl.ds(base, rows), :]
        m_a = head_lanes(rows, 256)
        lane = lax.broadcasted_iota(jnp.int32, (rows, 128), 1)
        ri = lax.broadcasted_iota(jnp.int32, (rows, rows), 0)
        ci = lax.broadcasted_iota(jnp.int32, (rows, rows), 1)
        tril = ci <= ri
        triu = ri <= ci
        diag = block_diag(256)
        ones = jnp.ones((rows, 128), bf)
        zero = jnp.zeros((), bf)
        d_state = d_res
        for p in range(PAIRS):
            lanes = slice(128 * p, 128 * p + 128)
            wide = slice(256 * p, 256 * p + 256)
            d_o = da_ref[:, lanes]
            prod = d_o.astype(f32) * att_ref[:, lanes].astype(f32)
            in_a = jnp.sum(jnp.where(lane < 64, prod, 0.0), axis=1, keepdims=True)
            in_b = jnp.sum(jnp.where(lane < 64, 0.0, prod), axis=1, keepdims=True)
            inner = jnp.where(lane < 64, -in_a, -in_b)
            high = inner.astype(bf).astype(f32)
            ext = jnp.where((lane & 63) == 0, high, jnp.where((lane & 63) == 1, inner - high, 0.0)).astype(bf)
            left = jnp.concatenate([d_o, ext], axis=1)
            left_a, left_b = jnp.where(m_a, left, zero), jnp.where(m_a, zero, left)
            ve = jnp.concatenate([v_ref[:, lanes], ones], axis=1)
            qn = qn_ref[:, wide]
            kf = kf_ref[:, wide]
            qn_a, qn_b = jnp.where(m_a, qn, zero), jnp.where(m_a, zero, qn)
            kf_a, kf_b = jnp.where(m_a, kf, zero), jnp.where(m_a, zero, kf)
            pt = jnp.concatenate([jnp.where(triu, nt_dot(kf, qn_a), 0.0), jnp.where(triu, nt_dot(kf, qn_b), 0.0)], axis=1).astype(bf)
            gg = jnp.concatenate([jnp.where(tril, nt_dot(left_a, ve), 0.0), jnp.where(tril, nt_dot(left_b, ve), 0.0)], axis=1).astype(bf)
            gt = jnp.concatenate([jnp.where(triu, nt_dot(ve, left_a), 0.0), jnp.where(triu, nt_dot(ve, left_b), 0.0)], axis=1).astype(bf)
            after = t_out[p].astype(bf)
            dv = nn_dot(pt, jnp.concatenate([left_a[:, :128], left_b[:, :128]], axis=0)) + nn_dot(kf, after[:, :128])
            dq = nn_dot(gg, jnp.concatenate([kf_a, kf_b], axis=0)) + nt_dot(left, sb_ref[p])
            dk = nn_dot(gt, jnp.concatenate([qn_a, qn_b], axis=0)) + nt_dot(ve, after)
            t_out[p] = t_out[p] + jnp.where(diag, tn_dot(qn, left), 0.0)
            sq = sg_ref[:, lanes].astype(f32)
            sk = sg_ref[:, D + 128 * p:D + 128 * p + 128].astype(f32)
            dm_ref[:, lanes] = ((dq[:, :128] * cos + dq[:, 128:] * sin) * sq).astype(bf)
            dm_ref[:, D + 128 * p:D + 128 * p + 128] = ((dk[:, :128] * cos + dk[:, 128:] * sin) * sk).astype(bf)
            dm_ref[:, 2 * D + 128 * p:2 * D + 128 * p + 128] = dv.astype(bf)
            for j in (p, 6 + p, 12 + p):
                column = slice(128 * j, 128 * j + 128)
                if j in (4, 13):
                    below = (dp_ref[:, 128:256] if j == 4 else dp_ref[:, 512:640]).astype(f32)
                    above = dm_ref[:, column].astype(f32)
                    for g in ((0, 1) if j == 4 else (2, 3)):
                        one, two = (pltpu.roll(above, 64, 1), below) if g & 1 else (above, pltpu.roll(below, 64, 1))
                        mix_ref[g] = jnp.where(lane < 64, one, two).astype(bf)
                        place(mix_ref.at[g], g, 4)
                else:
                    g = sum(j >= first for first in (5, 9, 14))
                    place(dm_ref.at[:, column], g, j - (0, 5, 9, 14)[g])
            if p % 2 == 1:
                for j in (0, D, 2 * D):
                    both = slice(j + 128 * (p - 1), j + 128 * (p + 1))
                    d_state = d_state + nt_dot(dm_ref[:, both], wq_ref[:, both])
        loaded(1)
        ds_ref[...] = d_state.astype(bf)
        send.put(ds_ref, all_o.at[here, :])
        send.finish()

        @pl.when(chunk > 0)
        def _():
            for copy in early(chunk - 1):
                copy.wait()


def backward_opening(delta, n, rows, stages, groups, *refs):
    t, meta, arr = refs[:3]
    cot, cot_v, load_sems, refs = refs[22], refs[30], refs[-1], refs[:-1]
    head, tail = pl.ds((n - 1) * rows, rows), pl.ds(0, (n - 1) * rows)
    loads = [pltpu.make_async_copy(cot.at[part, :], cot_v.at[part, :], load_sems.at[i]) for i, part in enumerate((head, tail))]
    for copy in loads:
        copy.start()
    backward_kernel(delta, n, rows, stages, groups, t, meta, cot_v, arr, *refs[4:11], None, None, *refs[12:22], *refs[23:30],
                    *refs[42:49], *refs[39:42], *refs[49:], loads=loads)


def backward_next(delta, n, rows, stages, groups, *refs):
    t, meta, arr, cot = refs[:4]
    act, act_v, sem, refs = refs[31], refs[47], refs[-1], refs[:-1]
    fill = (t[0] >= 1) & (t[0] <= TILES)
    tile = jnp.clip(t[0] - 1, 0, TILES - 1)
    copy = pltpu.make_async_copy(act.at[tile], act_v.at[tile], sem)

    @pl.when(fill)
    def _():
        copy.start()

    backward_kernel(delta, n, rows, stages, groups, t, meta, cot, arr, *refs[4:11], *refs[15:27], *refs[32:39],
                    *refs[51:58], *refs[48:51], *refs[58:])

    @pl.when(fill)
    def _():
        copy.wait()


def backward_call(rows, n, delta, stages, groups, opening, limit=17):
    V = pl.BlockSpec(memory_space=pltpu.VMEM)
    S = pl.BlockSpec(memory_space=pltpu.SMEM)
    A = pl.BlockSpec(memory_space=pl.ANY)
    sd = jax.ShapeDtypeStruct
    every = n * rows
    made = [((rows, D), bf), ((rows, 4 * D), bf), ((4, rows, 128), bf)]
    saved = [((rows, D), bf), ((rows, 128), f32), ((rows, 4 * D), bf), ((rows, D), bf), ((rows, D), bf), ((rows, D), bf),
             ((rows, 2 * D), bf), ((rows, 2 * D), bf), ((rows, 2 * D), bf), ((PAIRS, 256, 256), bf)]
    own = [((rows, 3 * D), bf), ((rows, D), bf), ((rows, D), bf), ((rows, D), bf)]
    early, saved = saved[:3], saved[3:]
    big = [pltpu.HBM((every, D), bf), pltpu.HBM((TILES, every, TILE), bf), pltpu.HBM((TILES, every, TILE), bf), pltpu.HBM((every, D), bf)]
    if opening:
        aliases = {3 + i: 7 + i for i in range(9)}
    else:
        aliases = {**{3 + i: 7 + i for i in range(12)}, 15: 1, 16: 2, **{27 + i: 3 + i for i in range(4)}}
    return pl.pallas_call(
        functools.partial(backward_opening if opening else backward_next, delta, n, rows, stages, groups),
        in_specs=[S, S] + [V] * 10 + [A] * 11 if opening else [S, S] + [V] * 15 + [A] * 15,
        out_specs=[V] * 3 + [A] * 4 + [V] * 12,
        out_shape=[sd((rows, D), bf), sd((PAIRS, 256, 256), f32), sd((8, D), f32)] + big
        + [pltpu.VMEM(*item) for item in kept_items(every) + early],
        scratch_shapes=[pltpu.VMEM(*item) for item in made + own + saved] + [pltpu.SemaphoreType.DMA((40,)), pltpu.SemaphoreType.DMA((13,))]
        + [pltpu.SemaphoreType.DMA((2,)) if opening else pltpu.SemaphoreType.DMA],
        input_output_aliases=aliases,
        cost_estimate=pl.CostEstimate(flops=rows * 2 * 10 * 10**6, bytes_accessed=4 * 2**20, transcendentals=0),
        compiler_params=pltpu.CompilerParams(vmem_limit_bytes=limit * 2**20),
        name="layer_backward",
    )


HALF = D // 2


def weight_kernel(groups, half, mixed, waits, fetch, ahead, meta_ref, left, *refs):
    raws, refs = refs[:1 + mixed], refs[1 + mixed + waits:]
    sources, refs = refs[:ahead], refs[ahead:]
    keep_o, send_o, refs = refs[0], refs[1], refs[2:]
    kept, refs = refs[:fetch], refs[fetch:]
    targets, refs = refs[:ahead], refs[ahead:]
    turned, out_buf, out_sem, raw_sem, ahead_sem = refs
    me = meta_ref[1]
    share = TILES // groups
    every = raws[0].shape[0]
    raw_copies, later = [], []
    if fetch:
        raw_copies = [pltpu.make_async_copy(raws[0].at[k:k + 256, :], kept[0].at[k:k + 256, :], raw_sem.at[k // 256]) for k in range(0, every, 256)]
        raws = kept
    for source, target in zip(sources, targets):
        step = 1 if len(source.shape) == 3 else every // 4
        for k in range(0, source.shape[0], step):
            later.append(pltpu.make_async_copy(source.at[k:k + step], target.at[k:k + step], ahead_sem.at[len(later)]))
    for copy in raw_copies + later:
        copy.start()
    for j, raw in enumerate(raws):
        for k in range(0, every, 256):
            if fetch:
                raw_copies[k // 256].wait()
            turned[j, :, k:k + 256] = raw[k:k + 256, half * HALF:(half + 1) * HALF].T
    for g in range(groups):
        for i in range(share):
            cols = slice(i * TILE, (i + 1) * TILE)
            value = nn_dot(turned[0], left[g * share + i])
            if mixed and i == share - 1:
                other = nn_dot(turned[1], left[g * share + i])
                lane = lax.broadcasted_iota(jnp.int32, other.shape, 1)
                value = jnp.where(lane < 3 * D // groups - i * TILE, value, other)
            out_buf[g, :, cols] = value.astype(bf)
        rel = g ^ me

        @pl.when((rel & 1) == 0)
        def _():
            pltpu.make_async_copy(out_buf.at[g], keep_o.at[rel >> 1], out_sem).start()

        @pl.when((rel & 1) == 1)
        def _():
            pltpu.make_async_copy(out_buf.at[g], send_o.at[rel >> 1], out_sem).start()
    pltpu.make_async_copy(out_buf, out_buf, out_sem).wait()
    for copy in later:
        copy.wait()


def weight_call(every, groups, half, mixed, waits, fetch, ahead, limit=12):
    V = pl.BlockSpec(memory_space=pltpu.VMEM)
    S = pl.BlockSpec(memory_space=pltpu.SMEM)
    A = pl.BlockSpec(memory_space=pl.ANY)
    raws = 1 + mixed
    return pl.pallas_call(
        functools.partial(weight_kernel, groups, half, mixed, waits, fetch, len(ahead)),
        in_specs=[S, V] + [A if fetch else V] * raws + [A] * (waits + len(ahead)),
        out_specs=[A] * 2 + [V] * (fetch + len(ahead)),
        out_shape=[pltpu.HBM((2, HALF, D), bf)] * 2 + [pltpu.VMEM((every, D), bf)] * fetch + [pltpu.VMEM(shape, bf) for shape in ahead],
        scratch_shapes=[pltpu.VMEM((raws, HALF, every), bf), pltpu.VMEM((groups, HALF, D), bf), pltpu.SemaphoreType.DMA,
                        pltpu.SemaphoreType.DMA((every // 256,)), pltpu.SemaphoreType.DMA((24,))],
        cost_estimate=pl.CostEstimate(flops=2 * every * HALF * 4 * D, bytes_accessed=every * 5 * D * 2, transcendentals=0),
        compiler_params=pltpu.CompilerParams(vmem_limit_bytes=limit * 2**20),
        name="weight_grad",
    )


READY = {2: 0, 3: 1, 4: 2, 5: 3}
MB_ROWS = 1024
MICRO = 2
ROWS = 256
DELTA = 2


def geometry(doc_ids):
    quarter = MB_ROWS // 4
    marks = doc_ids.reshape(-1, MB_ROWS)[:, ::quarter]
    pieces = 1 + jnp.sum((marks[:, 1:] != marks[:, :-1]).astype(jnp.int32), axis=1)
    length = MB_ROWS // pieces
    row = jnp.arange(MB_ROWS, dtype=jnp.int32)
    position = row[None, :] % length[:, None]
    angle = (0.5 * math.pi) * position.astype(f32) / length[:, None].astype(f32)
    angle = angle.reshape(-1, 1)
    starts = jnp.arange(0, MB_ROWS, ROWS, dtype=jnp.int32)
    first = (starts[None, :] % length[:, None]) == 0
    last = ((starts[None, :] + ROWS) % length[:, None]) == 0
    wide = (angle.shape[0], 128)
    return (jnp.broadcast_to(jnp.cos(angle), wide), jnp.broadcast_to(jnp.sin(angle), wide),
            first.reshape(-1).astype(jnp.int32), last.reshape(-1).astype(jnp.int32))


def exchange(block, axis, flip):
    route = [(i, i ^ flip) for i in range(lax.axis_size(axis))]
    return lax.ppermute(block, axis, route)


def add_kernel(*refs):
    total = sum(ref[...].reshape(refs[-1].shape).astype(f32) for ref in refs[:-1])
    refs[-1][...] = total.astype(refs[-1].dtype)


def add_call(slot, keep, got, *more, limit=12):
    rows, columns = keep.shape[1:]
    step = min(rows, 192)
    pick = pl.BlockSpec((1, step, columns), lambda i: (slot, i, 0))
    flat = pl.BlockSpec((step, columns), lambda i: (i, 0))
    return pl.pallas_call(
        add_kernel,
        grid=(rows // step,),
        in_specs=[pick, pick] + [flat] * len(more),
        out_specs=flat,
        out_shape=jax.ShapeDtypeStruct((rows, columns), keep.dtype),
        cost_estimate=pl.CostEstimate(flops=rows * columns * 2, bytes_accessed=rows * columns * 6, transcendentals=0),
        compiler_params=pltpu.CompilerParams(vmem_limit_bytes=limit * 2**20),
        name="add_parts",
    )(keep, got, *more)


def plain_add(*items, limit=12):
    V = pl.BlockSpec(memory_space=pltpu.VMEM)
    return pl.pallas_call(
        add_kernel, in_specs=[V] * len(items), out_specs=V, out_shape=jax.ShapeDtypeStruct(items[0].shape, items[0].dtype),
        cost_estimate=pl.CostEstimate(flops=items[0].size, bytes_accessed=items[0].size * 4, transcendentals=0),
        compiler_params=pltpu.CompilerParams(vmem_limit_bytes=limit * 2**20), name="add_vectors",
    )(*items)


def spread(own, before):
    if lax.axis_size("dp") != 2:
        return lax.psum(own, "dp")
    if before:
        before[-1], own = lax.optimization_barrier((before[-1], own))
    return exchange(own, "dp", 1)


def finished(own, other):
    if lax.axis_size("dp") == 2:
        return own.astype(f32) + other.astype(f32)
    return other.astype(f32)


def join_half(own, other, half, before, limit=12):
    step = HALF // 2
    flat = pl.BlockSpec((step, D), lambda i: (i, 0))
    return pl.pallas_call(
        lambda *refs: add_kernel(refs[0], refs[1], refs[-1]),
        grid=(2,),
        in_specs=[flat, flat] + [pl.BlockSpec(memory_space=pl.ANY)] * len(before),
        out_specs=pl.BlockSpec((step, D), lambda i: (2 * half + i, 0)),
        out_shape=jax.ShapeDtypeStruct((D, D), f32),
        input_output_aliases={2: 0} if before else {},
        cost_estimate=pl.CostEstimate(flops=HALF * D, bytes_accessed=HALF * D * 8, transcendentals=0),
        compiler_params=pltpu.CompilerParams(vmem_limit_bytes=limit * 2**20),
        name="join_half",
    )(own, other, *before)


def local(tokens, doc_ids, cotangent, w_qkv, w_out, w_up, w_down,
          first_gain, first_bias, second_gain, second_bias):
    stages = lax.axis_size("pipe")
    groups = lax.axis_size("group")
    stage = lax.axis_index("pipe").astype(jnp.int32)
    me = lax.axis_index("group").astype(jnp.int32)
    n = tokens.shape[0] // ROWS
    ticks = n + DELTA * (stages - 1)
    cos, sin, first, last = geometry(doc_ids)
    meta = jnp.concatenate([stage[None], me[None], first, last])
    resident = far((tokens,)) + [cos, sin] + far((w_qkv[0], w_out[0], w_up[0], w_down[0]))
    gb = jnp.concatenate([first_gain, first_bias, second_gain, second_bias], axis=0)
    blank = jnp.zeros((ROWS, D), bf)
    arriving = [blank] * DELTA
    resident = resident + [gb]
    state, big = (), ()
    for t in range(ticks):
        made = forward_call(ROWS, n, DELTA, t == 0, t == ticks - 1)(jnp.full((1,), t, jnp.int32), meta, arriving.pop(0), *resident, *state, *big)
        state, big, resident = [made[1], made[0], made[2], made[3]], made[4:18], made[18:]
        route = [(a, a + 1) for a in range(stages - 1) if 0 <= t - a * DELTA < n]
        arriving.append(lax.ppermute(made[0], "pipe", route) if route else made[0])
    block_out, x, att, hb, act, qn, kf, v, sg, n1, gp, n2, rs, sb = big
    arriving = [made[0]] * DELTA
    state, big = (), ()
    for t in range(ticks):
        made = backward_call(ROWS, n, DELTA, stages, groups, t == 0)(
            jnp.full((1,), t, jnp.int32), meta, arriving.pop(0), *resident, *state,
            *far((n2, rs, gp, n1, att, v, qn, kf, sg, sb)), *big, *far([act if t > 0 else cotangent]))
        state, big, resident = made[1:3], made[3:7], made[7:]
        route = [(a, a - 1) for a in range(1, stages) if 0 <= t - (stages - 1 - a) * DELTA < n]
        arriving.append(lax.ppermute(made[0], "pipe", route) if route else made[0])
    df, du, de, input_grad = big
    act = resident[8]
    pieces = [(act, df), (de, x, att), (du, hb)]
    vectors = state[1]
    for flip in (1, 2):
        vectors = plain_add(vectors, exchange(vectors, "group", flip))
    aways, keeps, gots, backs, owns, others = [], [], [], [], [], []

    def turn(k):
        if backs:
            backs[-1], aways[k] = lax.optimization_barrier((backs[-1], aways[k]))
        backs.append(exchange(aways[k], "group", 2))

    for piece in range(3):
        left, *rights = pieces[piece]
        for half in range(2):
            k = len(keeps)
            fetch = k == 0
            ready = READY.get(k)
            waits = [] if ready is None else [aways[ready]]
            call = weight_call(n * ROWS, groups, half, len(rights) == 2, len(waits), fetch, [])
            keep, send, *loads = call(meta, left, *(far(rights) if fetch else rights), *waits)
            rights = loads if fetch else rights
            keeps.append(keep)
            gots.append(exchange(send, "group", 1))
            away = add_call(1, keep, gots[-1])
            if k in (1, 5):
                vectors, away = lax.optimization_barrier((vectors, away))
            aways.append(away)
            turn(k)
    for keep, got, back in zip(keeps, gots, backs):
        own = add_call(0, keep, got, back)
        other = spread(own, others)
        owns.append(own)
        others.append(other)
    parts = [finished(*pair) for pair in zip(owns, others)]
    if lax.axis_size("dp") == 2:
        vectors = plain_add(vectors, exchange(vectors, "dp", 1))
    else:
        vectors = lax.psum(vectors, "dp")
    vectors, me, _ = lax.optimization_barrier((vectors, me, owns[3]))
    mine = lax.dynamic_slice_in_dim(vectors, me * (D // groups), D // groups, axis=1)
    g_down, g_mixed, g_up = (jnp.concatenate(parts[i:i + 2], axis=0) for i in (0, 2, 4))
    if lax.axis_size("dp") == 2:
        g_up = join_half(owns[5], others[5], 1, [join_half(owns[4], others[4], 0, [])])
    odd = (me & 1) == 1
    swap = lambda a, b: jnp.concatenate([g_mixed[:, a], g_mixed[:, b]], axis=1)
    low, one, two, high = slice(0, 512), slice(512, 576), slice(576, 640), slice(640, 768)
    g_qkv = jnp.where(odd, swap(one, low), swap(low, one))
    g_out = jnp.where(odd, swap(two, high), swap(high, two))
    return (block_out[None], input_grad[None], g_qkv[None], g_out[None], g_up[None], g_down.T[None],
            mine[0:1], mine[1:2], mine[2:3], mine[3:4])


def solution(mesh):
    rows = ("group", "dp")
    whole = P("pipe", None, None)
    vector = P("pipe", None)
    return jax.shard_map(
        local,
        mesh=mesh,
        in_specs=(P(rows, None), P(rows), P(rows, None)) + (whole,) * 4 + (vector,) * 4,
        out_specs=(P("pipe", rows, None), P("pipe", rows, None), P("pipe", None, "group"), P("pipe", None, "group"),
                   P("pipe", None, "group"), P("pipe", "group", None)) + (P("pipe", "group"),) * 4,
        check_vma=False,
    )
```
